32 devices in a mesh: chan: 4 (over z), tm: 8 (over y, x, core).
Axes of the slice: x: 2, y: 2, z: 4, core: 2. Of those that a mesh axis runs over, the one named last changes fastest.
Arguments:
- recording: bfloat16 [4096, 120000], P('chan', 'tm'), may hold values from -6 to 6
- offsets: int32 [16], replicated, may hold values from 0 to 3749, as said below
- band_bins: int32 [20], replicated, may hold values from 61 to 300
- dead_flags: int32 [4096], P('chan'), may hold values 0 or 1
Outputs:
- stacks: bfloat16 [2, 20, 4096, 4096], P(None, None, 'tm', 'chan')
The draws below stay inside these ranges and needn't reach their ends.
Inputs may be any that keep to these rules, and one draw needn't show every extreme that they name: `offsets`: every window's offset is drawn afresh; the last window of some block of 2 consecutive windows has the largest offset.
All inputs are finite; a program needn't handle non-finite values. No bound on the sum of `dead_flags` on one device may be relied on, other than what follows from the above.
Results may differ from the reference program's by a relative error of at most 0.0063.
Values may be sent and summed in bfloat16 or wider, within the bound.
No kernel may reach another device: no remote copies, remote signals or barrier semaphores. Data moves between devices by JAX's collectives and lax.ppermute only.
A program may use at most 192 MiB of HBM per device.

```python
import math
import jax
import jax.numpy as jnp
from jax import lax

CH = 4096
L = 15000
NB = 20
W_DEV = 2
WIN = 16
SAMPLES = 120000


def draw_offsets(key, part):
    off_limit = L // 4
    key_values, key_place = jax.random.split(key)
    values = jax.random.randint(key_values, (WIN,), 0, off_limit, dtype=jnp.int32)
    device = jax.random.randint(key_place, (), 0, WIN // W_DEV, dtype=jnp.int32)
    return values.at[device * W_DEV + W_DEV - 1].set(off_limit - 1)


def touch_ends(array, rng, least, high):
    place = [jax.random.randint(jax.random.fold_in(rng, axis), (), 0, length) for axis, length in enumerate(array.shape)]
    widest = array.shape.index(max(array.shape))
    beside = place[:widest] + [(place[widest] + 1) % array.shape[widest]] + place[widest + 1:]
    return array.at[tuple(place)].set(least).at[tuple(beside)].set(high)


def block_levels(stream_key, shape, pieces, low, largest):
    def one(position, blocks):
        steps = jax.random.uniform(jax.random.fold_in(jax.random.fold_in(stream_key, 6), position), (blocks,), jnp.float32, low / len(pieces), largest / len(pieces))
        return jnp.repeat(jnp.exp(steps), shape[position] // blocks).reshape((-1,) + (1,) * (len(shape) - position - 1))

    factor_of = one(*pieces[0])
    for cut in pieces[1:]:
        factor_of = factor_of * one(*cut)
    return factor_of


def scatter_about(stream_key, shape, scale, limit, pieces=(), kind=jnp.bfloat16):
    loudness = block_levels(stream_key, shape, pieces, -0.22, 0.18) if pieces else 1.0
    drawn = jax.random.normal(stream_key, shape, jnp.float32) * scale * loudness
    return jnp.minimum(jnp.maximum(drawn, -limit), limit).astype(kind)


def setup_inputs(seed: int = 0) -> dict:
    keys = jax.random.split(jax.random.key(seed), 5)
    recording = scatter_about(keys[0], (CH, SAMPLES), 1.0, 6.0, ((0, 4), (1, 8)))
    offsets = draw_offsets(jax.random.fold_in(keys[4], 71), 0)
    band_bins = touch_ends(jax.random.randint(keys[2], (NB,), L // 250 + 1, L // 50 + 1), jax.random.fold_in(keys[2], 1), L // 250 + 1, (L // 50 + 1) - 1).astype(jnp.int32)
    dead_flags = touch_ends((jax.random.randint(keys[3], (CH,), 0, 16) < 1).astype(jnp.int32), jax.random.fold_in(keys[3], 1), 0, 1)
    return dict(recording=recording, offsets=offsets, band_bins=band_bins, dead_flags=dead_flags)


TWO_PI = 2.0 * math.pi
FLOOR = 0.7

def dft_rows(band_bins):
    sample_index = jnp.arange(L, dtype=jnp.int32)
    turn_index = band_bins[:, None] * sample_index[None, :] % L
    angles = turn_index.astype(jnp.float32) * (TWO_PI / L)
    norm_scale = 1.0 / math.sqrt(L)
    return jnp.concatenate([jnp.cos(angles) * norm_scale, -jnp.sin(angles) * norm_scale], axis=0).astype(jnp.bfloat16)

def reference(recording, offsets, band_bins, dead_flags):
    hop_size = L // 2
    rim_width = hop_size + hop_size // 2
    dft_table = dft_rows(band_bins).astype(jnp.float32)
    alive = (1 - dead_flags).astype(jnp.float32)
    last_start = SAMPLES - L
    tail_region = jnp.concatenate([recording[:, last_start:], jnp.zeros((CH, rim_width), jnp.bfloat16)], axis=1)

    def one_window(index):
        start = (index * hop_size + offsets[index]).astype(jnp.int32)
        main_piece = lax.dynamic_slice_in_dim(recording, jnp.minimum(start, last_start).astype(jnp.int32), L, 1)
        tail_piece = lax.dynamic_slice_in_dim(tail_region, jnp.maximum(start - last_start, 0).astype(jnp.int32), L, 1)
        piece = jnp.where(start > last_start, tail_piece, main_piece).astype(jnp.float32)
        raw_spectra = lax.dot_general(dft_table, piece, (((1,), (1,)), ((), ())), precision=lax.Precision.HIGHEST)
        energy = lax.optimization_barrier(jnp.sum(piece * piece, axis=1))
        spectra = raw_spectra / jnp.sqrt(energy / L + 1e-06)[None, :]
        level = lax.optimization_barrier(jnp.mean(spectra * spectra, axis=0)) * 2.0
        factor = alive / jnp.sqrt(jnp.maximum(level, FLOOR))
        return (spectra * factor[None, :]).astype(jnp.bfloat16).reshape(2, NB, CH)
    white = lax.map(one_window, jnp.arange(WIN, dtype=jnp.int32))
    stack_scale = 1.0 / math.sqrt(WIN)

    def one_bin(index):
        part_now = lax.dynamic_index_in_dim(white, index, 2, keepdims=False).astype(jnp.float32)
        real_part = jnp.einsum('wpj,wpi->ji', part_now, part_now, precision=lax.Precision.HIGHEST)
        flipped = jnp.stack([-part_now[:, 1], part_now[:, 0]], axis=1)
        imag_part = jnp.einsum('wpj,wpi->ji', flipped, part_now, precision=lax.Precision.HIGHEST)
        return (jnp.stack([real_part, imag_part]) * stack_scale).astype(jnp.bfloat16)
    per_bin = lax.map(one_bin, jnp.arange(NB, dtype=jnp.int32))
    return jnp.swapaxes(per_bin, 0, 1)
```

```python
import functools
import math

import jax
import jax.numpy as jnp
from jax import lax
from jax.experimental import pallas as pl
from jax.experimental.pallas import tpu as pltpu
from jax.sharding import PartitionSpec as P

L = 15000
FLOOR = 0.7
F32 = jnp.float32
BF16 = jnp.bfloat16
LANE = 128
DEPTH = 256
STEP = 2048
ROW_TILE = 16


def shifted(block, axis, distance):
    devices = range(lax.axis_size(axis))
    route = [(i - distance, i) for i in devices if i - distance in devices]
    return lax.ppermute(block, axis, route)


def cos_sin(turns, length):
    quarter = jnp.floor(turns * (4.0 / length) + 0.5)
    angle = (turns * 4.0 - quarter * length) * (math.pi / (2.0 * length))
    square = angle * angle
    sine = angle * (
        1.0 + square * (-1.0 / 6 + square * (1.0 / 120 + square * (-1.0 / 5040 + square * (1.0 / 362880))))
    )
    cosine = 1.0 + square * (
        -0.5 + square * (1.0 / 24 + square * (-1.0 / 720 + square * (1.0 / 40320)))
    )
    quadrant = quarter - 4.0 * jnp.floor(quarter * 0.25)
    odd = (quadrant == 1.0) | (quadrant == 3.0)
    cos_sign = jnp.where((quadrant == 1.0) | (quadrant == 2.0), -1.0, 1.0)
    sin_sign = jnp.where(quadrant >= 2.0, -1.0, 1.0)
    return cos_sign * jnp.where(odd, sine, cosine), sin_sign * jnp.where(odd, cosine, sine)


def spectra_kernel(
    bins, windows, block_len, steps,
    offsets, band_bins, x_ref, own_ref, back_ref,
    acc, seg, cos_now, sin_now, cos_turn, sin_turn, place, even, odd,
):
    channels = x_ref.shape[1]
    length, hop = L, L // 2
    rows = bins * windows * 2
    half_tile = ROW_TILE // 2
    per_group = half_tile // windows
    groups = rows // ROW_TILE
    states = groups * half_tile
    step = pl.program_id(0)
    half = STEP // 2
    tiles = STEP // ROW_TILE
    tm = lax.axis_index("tm")
    ahead = [offsets[tm * windows + w] + w * hop for w in range(windows)]
    before = jnp.maximum(tm - 1, 0) * windows
    behind = [offsets[before + w] + w * hop + length - block_len for w in range(windows)]
    ends = []
    for w in range(windows):
        ends += [jnp.minimum(ahead[w], behind[w]), jnp.maximum(ahead[w], behind[w])]
    segments = len(ends) + 1
    trash = segments

    def make_table(table, first, count):
        for j in range(count):
            moved = ((first + j) * DEPTH).astype(F32)
            for side in range(2):
                limit = moved if side else -moved
                for g in range(groups):
                    at = slice(side * states + g * half_tile, side * states + (g + 1) * half_tile)
                    to = side * rows + g * ROW_TILE
                    c, s = cos_now[at, :], sin_now[at, :]
                    inside = place[at, :] >= limit
                    wave = jnp.concatenate([jnp.where(inside, c, 0.0), jnp.where(inside, s, 0.0)], axis=0)
                    table[to:to + ROW_TILE, j * DEPTH:(j + 1) * DEPTH] = wave.astype(BF16)
                    ct, st = cos_turn[at, :], sin_turn[at, :]
                    cos_now[at, :] = c * ct + s * st
                    sin_now[at, :] = s * ct - c * st

    @pl.when(step == 0)
    def _():
        shape = (half_tile, DEPTH)
        row = lax.broadcasted_iota(jnp.int32, shape, 0)
        lane = lax.broadcasted_iota(jnp.int32, shape, 1).astype(F32)
        norm = 1.0 / math.sqrt(length)
        for side in range(2):
            for g in range(groups):
                at = slice(side * states + g * half_tile, side * states + (g + 1) * half_tile)
                tone = jnp.zeros(shape, jnp.int32)
                start = jnp.zeros(shape, jnp.int32)
                for i in range(per_group):
                    tone = jnp.where(row // windows == i, band_bins[g * per_group + i], tone)
                for w in range(windows):
                    here = behind[w] - length if side else ahead[w]
                    start = jnp.where(row % windows == w, here, start)
                tone, start = tone.astype(F32), start.astype(F32)
                cosine, sine = cos_sin((lane - start) * tone, length)
                cos_now[at, :] = cosine * norm
                sin_now[at, :] = -sine * norm
                cos_turn[at, :], sin_turn[at, :] = cos_sin(tone * DEPTH, length)
                place[at, :] = start + (length - 1) - lane if side else lane - start
        make_table(even, jnp.int32(0), half // DEPTH)
        acc[...] = jnp.zeros_like(acc)
        seg[...] = jnp.zeros_like(seg)

    base = step * STEP

    def segment_of(position):
        index = jnp.int32(0)
        for end in ends:
            index += (end <= position).astype(jnp.int32)
        return index

    def body(kind):
        used = STEP if kind != "last" else block_len - (steps - 1) * STEP
        first = step * (STEP // DEPTH)

        def piece(low):
            full = max(0, min(half, used - low)) // LANE * LANE
            rest = max(0, min(half, used - low)) - full
            table = even if low == 0 else odd
            if full:
                acc[...] += jnp.dot(table[:, :full], x_ref[low:low + full, :], preferred_element_type=F32)
            if rest:
                cut = x_ref[low + full:low + full + LANE, :]
                inside = lax.broadcasted_iota(jnp.int32, cut.shape, 0) < rest
                cut = jnp.where(inside, cut.astype(F32), 0.0).astype(BF16)
                acc[...] += jnp.dot(table[:, full:full + LANE], cut, preferred_element_type=F32)

        def energy(low, high):
            total = None
            for t in range(low, high):
                if t * ROW_TILE >= used:
                    continue
                x = x_ref[t * ROW_TILE:(t + 1) * ROW_TILE, :].astype(F32)
                if (t + 1) * ROW_TILE > used:
                    inside = lax.broadcasted_iota(jnp.int32, x.shape, 0) < used - t * ROW_TILE
                    x = jnp.where(inside, x, 0.0)
                square = x * x
                square = square[:half_tile] + square[half_tile:]
                if kind == "edge":
                    seg[targets[t]] += square
                else:
                    total = square if total is None else total + square
            if total is not None:
                seg[target] += total

        if kind == "edge":
            targets = []
            for t in range(tiles):
                cut = functools.reduce(
                    jnp.logical_or, [end // ROW_TILE == step * tiles + t for end in ends]
                )
                targets.append(jnp.where(cut, trash, segment_of(base + t * ROW_TILE)))
        else:
            target = segment_of(base)
        piece(0)
        energy(0, tiles // 2)
        if used > half:
            make_table(odd, first + half // DEPTH, pl.cdiv(min(used - half, half), DEPTH))
        piece(half)
        energy(tiles // 2, tiles)
        if kind != "last":
            make_table(even, first + STEP // DEPTH, half // DEPTH)

    last = steps - 1
    cut_here = functools.reduce(jnp.logical_or, [end // STEP == step for end in ends])

    @pl.when(jnp.logical_and(step < last, jnp.logical_not(cut_here)))
    def _():
        body("plain")

    @pl.when(jnp.logical_and(step < last, cut_here))
    def _():
        body("edge")
        for i, end in enumerate(ends):
            low = ends[i - 1] if i else jnp.int32(0)
            high = ends[i + 1] if i + 1 < len(ends) else jnp.int32(block_len)

            @pl.when(end // STEP == step)
            def _():
                tile = end // ROW_TILE
                at = pl.ds(pl.multiple_of((tile - step * tiles) * ROW_TILE, ROW_TILE), ROW_TILE)
                x = x_ref[at, :].astype(F32)
                spot = lax.broadcasted_iota(jnp.int32, x.shape, 0) + tile * ROW_TILE
                under = jnp.logical_and(spot >= low, spot < end)
                over = jnp.logical_and(spot >= end, spot < high)
                over = jnp.logical_and(over, high // ROW_TILE != tile)
                square = x * x
                for where, index in ((under, i), (over, i + 1)):
                    kept = jnp.where(where, square, 0.0)
                    seg[index] += kept[:half_tile] + kept[half_tile:]

    @pl.when(step == last)
    def _():
        body("last")
        own_ref[:rows, :] = acc[:rows, :]
        back_ref[:rows, :] = acc[rows:, :]
        parts = [seg[i] for i in range(segments)]
        own_energy, back_energy = [], []
        for w in range(windows):
            turn = parts[2 * w + 1]
            early = ahead[w] <= behind[w]
            after = sum(parts[2 * w + 2:]) + jnp.where(early, turn, 0.0)
            until = sum(parts[:2 * w + 1]) + jnp.where(early, turn, 0.0)
            own_energy.append(jnp.sum(after, axis=0, keepdims=True))
            back_energy.append(jnp.sum(until, axis=0, keepdims=True))
        row = lax.broadcasted_iota(jnp.int32, (half_tile, channels), 0)
        for ref, found in ((own_ref, own_energy), (back_ref, back_energy)):
            block = jnp.zeros((half_tile, channels), F32)
            for w in range(windows):
                block = jnp.where(row == w, found[w], block)
            ref[rows:, :] = block


def spectra_of(recording, offsets, band_bins, windows):
    channels, block_len = recording.shape
    bins = band_bins.shape[0]
    rows = bins * windows * 2
    kept = rows + ROW_TILE // 2
    steps = pl.cdiv(block_len, STEP)
    out = jax.ShapeDtypeStruct((kept, channels), F32)
    state = pltpu.VMEM((rows, DEPTH), F32)
    table = pltpu.VMEM((2 * rows, STEP // 2), BF16)
    return pl.pallas_call(
        functools.partial(spectra_kernel, bins, windows, block_len, steps),
        out_shape=(out, out),
        grid=(steps,),
        in_specs=[
            pl.BlockSpec(memory_space=pltpu.SMEM),
            pl.BlockSpec(memory_space=pltpu.SMEM),
            pl.BlockSpec((STEP, channels), lambda i: (i, 0)),
        ],
        out_specs=(
            pl.BlockSpec((kept, channels), lambda i: (0, 0)),
            pl.BlockSpec((kept, channels), lambda i: (0, 0)),
        ),
        scratch_shapes=[
            pltpu.VMEM((2 * rows, channels), F32),
            pltpu.VMEM((2 * windows + 2, ROW_TILE // 2, channels), F32),
            state, state, state, state, state, table, table,
        ],
        compiler_params=pltpu.CompilerParams(
            dimension_semantics=("arbitrary",), vmem_limit_bytes=40 * 2**20
        ),
        cost_estimate=pl.CostEstimate(
            flops=2 * channels * block_len * 2 * rows,
            bytes_accessed=channels * block_len * 2,
            transcendentals=0,
        ),
        name="band_spectra",
    )(offsets, band_bins, recording.T)


def whiten_kernel(bins, windows, own_ref, more_ref, dead_ref, white_ref):
    rows = bins * windows * 2
    raw = own_ref[:rows, :] + more_ref[:rows, :]
    energy = own_ref[rows:rows + 8, :] + more_ref[rows:rows + 8, :]
    inverse = 1.0 / jnp.sqrt(energy / L + 1e-06)
    which = lax.broadcasted_iota(jnp.int32, (rows, 1), 0) % windows
    scale = inverse[windows - 1:windows, :]
    for w in range(windows - 1):
        scale = jnp.where(which == w, inverse[w:w + 1, :], scale)
    spectra = raw * scale
    power = spectra * spectra
    alive = (1 - dead_ref[...]).astype(F32)
    factor = None
    for w in reversed(range(windows)):
        level = jnp.sum(jnp.where(which == w, power, 0.0), axis=0, keepdims=True) * (1.0 / bins)
        one = alive / jnp.sqrt(jnp.maximum(level, FLOOR))
        factor = one if factor is None else jnp.where(which == w, one, factor)
    white = (spectra * factor).astype(BF16)
    width = white_ref.shape[2]
    for h in range(white_ref.shape[0]):
        white_ref[h] = white[:, h * width:(h + 1) * width]


def whiten(own, more, dead, bins, windows, halves):
    channels = own.shape[1]
    rows = bins * windows * 2
    return pl.pallas_call(
        functools.partial(whiten_kernel, bins, windows),
        out_shape=jax.ShapeDtypeStruct((halves, rows, channels // halves), BF16),
        name="whiten",
    )(own, more, dead.reshape(1, channels))


def stack_kernel(windows, scale, cols_ref, rows_ref, out_ref, lhs):
    bin_index = pl.program_id(0)
    per_group = ROW_TILE // (2 * windows)
    devices = cols_ref.shape[0]
    depth = devices * ROW_TILE
    width = cols_ref.shape[2]
    slot = bin_index % per_group
    exact = math.frexp(scale)[0] == 0.5

    @pl.when(slot == 0)
    def _():
        cols = cols_ref[...].astype(F32)
        if exact:
            cols = cols * scale
        head, tail = cols[:, :ROW_TILE // 2], cols[:, ROW_TILE // 2:]
        straight = cols.reshape(depth, width)
        turned = jnp.concatenate([-tail, head], axis=1).reshape(depth, width)
        lhs[:width, :] = straight.T.astype(BF16)
        lhs[width:, :] = turned.T.astype(BF16)

    which = lax.broadcasted_iota(jnp.int32, (depth, 1), 0) % (ROW_TILE // 2) // windows
    for h in range(rows_ref.shape[1]):
        span = rows_ref.shape[3]
        block = rows_ref[:, h].reshape(depth, span).astype(F32)
        rhs = jnp.where(which == slot, block, 0.0).astype(BF16)
        for part in range(2):
            product = jnp.dot(
                lhs[part * width:(part + 1) * width, :], rhs, preferred_element_type=F32
            )
            if not exact:
                product = product * scale
            out_ref[part, 0, :, h * span:(h + 1) * span] = product.astype(BF16)


def stacks_of(cols_all, rows_all, bins, windows):
    devices, halves, _, span = rows_all.shape
    width = cols_all.shape[2]
    per_group = ROW_TILE // (2 * windows)
    scale = 1.0 / math.sqrt(windows * devices)
    channels = halves * span
    return pl.pallas_call(
        functools.partial(stack_kernel, windows, scale),
        out_shape=jax.ShapeDtypeStruct((2, bins, width, channels), BF16),
        grid=(bins,),
        in_specs=[
            pl.BlockSpec((devices, ROW_TILE, width), lambda b: (0, b // per_group, 0)),
            pl.BlockSpec((devices, halves, ROW_TILE, span), lambda b: (0, 0, b // per_group, 0)),
        ],
        out_specs=pl.BlockSpec((2, 1, width, channels), lambda b: (0, b, 0, 0)),
        scratch_shapes=[pltpu.VMEM((2 * width, devices * ROW_TILE), BF16)],
        compiler_params=pltpu.CompilerParams(
            dimension_semantics=("arbitrary",), vmem_limit_bytes=40 * 2**20
        ),
        cost_estimate=pl.CostEstimate(
            flops=2 * 2 * bins * width * channels * devices * ROW_TILE,
            bytes_accessed=2 * bins * width * channels * 2,
            transcendentals=0,
        ),
        name="stack_products",
    )(cols_all, rows_all)


def shards(recording, offsets, band_bins, dead_flags):
    channels, block_len = recording.shape
    windows = block_len // (L // 2)
    bins = band_bins.shape[0]
    rows = bins * windows * 2
    chan_count, tm_count = lax.axis_size("chan"), lax.axis_size("tm")
    halves = tm_count // chan_count
    own, back = spectra_of(recording, offsets, band_bins, windows)
    more = shifted(back, "tm", -1)
    white = whiten(own, more, dead_flags, bins, windows, halves)
    rows_all = lax.all_gather(white, "tm", axis=0)
    every_chan = lax.all_gather(white, "chan", axis=0)
    every_chan = every_chan.reshape(tm_count, rows, channels // halves)
    cols_all = lax.all_to_all(every_chan, "tm", split_axis=0, concat_axis=0, tiled=True)
    return stacks_of(cols_all, rows_all, bins, windows)


def solution(mesh):
    placed = (P("chan", "tm"), P(), P(), P("chan"))
    return jax.shard_map(
        shards, mesh=mesh, in_specs=placed, out_specs=P(None, None, "tm", "chan"), check_vma=False
    )
```

```python
import functools
import math

import jax
import jax.numpy as jnp
from jax import lax
from jax.experimental import pallas as pl
from jax.experimental.pallas import tpu as pltpu
from jax.sharding import PartitionSpec as P

L = 15000
FLOOR = 0.7
F32 = jnp.float32
BF16 = jnp.bfloat16
LANE = 128
DEPTH = 256
PIECE = 512
STEP = 2 * PIECE
ROW_TILE = 16


def shifted(block, axis, distance):
    devices = range(lax.axis_size(axis))
    route = [(i - distance, i) for i in devices if i - distance in devices]
    return lax.ppermute(block, axis, route)


def cos_sin(turns, length):
    quarter = jnp.floor(turns * (4.0 / length) + 0.5)
    angle = (turns * 4.0 - quarter * length) * (math.pi / (2.0 * length))
    square = angle * angle
    sine = angle * (
        1.0 + square * (-1.0 / 6 + square * (1.0 / 120 + square * (-1.0 / 5040 + square * (1.0 / 362880))))
    )
    cosine = 1.0 + square * (
        -0.5 + square * (1.0 / 24 + square * (-1.0 / 720 + square * (1.0 / 40320)))
    )
    quadrant = quarter - 4.0 * jnp.floor(quarter * 0.25)
    odd = (quadrant == 1.0) | (quadrant == 3.0)
    cos_sign = jnp.where((quadrant == 1.0) | (quadrant == 2.0), -1.0, 1.0)
    sin_sign = jnp.where(quadrant >= 2.0, -1.0, 1.0)
    return cos_sign * jnp.where(odd, sine, cosine), sin_sign * jnp.where(odd, cosine, sine)


def spectra_kernel(
    bins, windows, block_len,
    offsets_hbm, bins_hbm, dead_hbm, x_hbm, tail_ref, own_ref, back_ref,
    offsets, band_bins, dead, x_ref, acc, seg, cos_now, sin_now, cos_turn, sin_turn, place, even, odd,
    small_sems, x_sems,
):
    channels = x_ref.shape[1]
    length, hop = L, L // 2
    rows = bins * windows * 2
    half_tile = ROW_TILE // 2
    per_group = half_tile // windows
    groups = rows // ROW_TILE
    states = groups * half_tile
    bulk = block_len // ROW_TILE * ROW_TILE
    padded = x_ref.shape[0]
    steps = padded // STEP
    columns = [slice(n, min(n + DEPTH, channels)) for n in range(0, channels, DEPTH)]

    def x_copy(i):
        size = min(STEP, bulk - i * STEP)
        at = pl.ds(i * STEP, size)
        return pltpu.make_async_copy(x_hbm.at[at], x_ref.at[at], x_sems.at[i])

    small = [
        pltpu.make_async_copy(offsets_hbm, offsets, small_sems.at[0]),
        pltpu.make_async_copy(bins_hbm, band_bins, small_sems.at[1]),
        pltpu.make_async_copy(dead_hbm, dead, small_sems.at[2]),
    ]
    for copy in small:
        copy.start()
    for i in range(pl.cdiv(bulk, STEP)):
        x_copy(i).start()
    for copy in small:
        copy.wait()

    tm = lax.axis_index("tm")
    ahead = [offsets[tm * windows + w] + w * hop for w in range(windows)]
    before = jnp.maximum(tm - 1, 0) * windows
    behind = [offsets[before + w] + w * hop + length - block_len for w in range(windows)]
    ends = []
    for w in range(windows):
        ends += [jnp.minimum(ahead[w], behind[w]), jnp.maximum(ahead[w], behind[w])]
    segments = len(ends) + 1
    trash = segments

    def make_table(table, first, count):
        for j in range(count):
            moved = jnp.asarray((first + j) * DEPTH, jnp.int32).astype(F32)
            for side in range(2):
                limit = moved if side else -moved
                for g in range(groups):
                    at = slice(side * states + g * half_tile, side * states + (g + 1) * half_tile)
                    to = side * rows + g * ROW_TILE
                    c, s = cos_now[at, :], sin_now[at, :]
                    inside = place[at, :] >= limit
                    wave = jnp.concatenate([jnp.where(inside, c, 0.0), jnp.where(inside, s, 0.0)], axis=0)
                    table[to:to + ROW_TILE, j * DEPTH:(j + 1) * DEPTH] = wave.astype(BF16)
                    ct, st = cos_turn[at, :], sin_turn[at, :]
                    cos_now[at, :] = c * ct + s * st
                    sin_now[at, :] = s * ct - c * st

    shape = (half_tile, DEPTH)
    row = lax.broadcasted_iota(jnp.int32, shape, 0)
    lane = lax.broadcasted_iota(jnp.int32, shape, 1).astype(F32)
    norm = 1.0 / math.sqrt(length)
    for side in range(2):
        for g in range(groups):
            at = slice(side * states + g * half_tile, side * states + (g + 1) * half_tile)
            tone = jnp.zeros(shape, jnp.int32)
            start = jnp.zeros(shape, jnp.int32)
            for i in range(per_group):
                tone = jnp.where(row // windows == i, band_bins[g * per_group + i], tone)
            for w in range(windows):
                here = behind[w] - length if side else ahead[w]
                start = jnp.where(row % windows == w, here, start)
            tone, start = tone.astype(F32), start.astype(F32)
            cosine, sine = cos_sin((lane - start) * tone, length)
            cos_now[at, :] = cosine * norm
            sin_now[at, :] = -sine * norm
            cos_turn[at, :], sin_turn[at, :] = cos_sin(tone * DEPTH, length)
            place[at, :] = start + (length - 1) - lane if side else lane - start
    make_table(even, 0, PIECE // DEPTH)
    acc[...] = jnp.zeros_like(acc)
    seg[...] = jnp.zeros_like(seg)
    x_ref[bulk:, :] = jnp.zeros((padded - bulk, channels), BF16)
    if block_len > bulk:
        inside = lax.broadcasted_iota(jnp.int32, (ROW_TILE, channels), 0) < block_len - bulk
        x_ref[bulk:bulk + ROW_TILE, :] = jnp.where(inside, tail_ref[...].astype(F32), 0.0).astype(BF16)

    def segment_of(position):
        index = jnp.int32(0)
        for end in ends:
            index += (end <= position).astype(jnp.int32)
        return index

    def has_end(first, size):
        return functools.reduce(
            jnp.logical_or, [jnp.logical_and(end >= first, end < first + size) for end in ends]
        )

    def piece(base, size, table, edge):
        tiles = size // ROW_TILE
        if edge:
            targets = [
                jnp.where(has_end(base + t * ROW_TILE, ROW_TILE), trash, segment_of(base + t * ROW_TILE))
                for t in range(tiles)
            ]
        else:
            target = segment_of(base)
        for at in columns:
            block = x_ref[pl.ds(base, size), at]
            acc[:, at] += jnp.dot(table[:, :size], block, preferred_element_type=F32)
            total = None
            for t in range(tiles):
                x = x_ref[pl.ds(base + t * ROW_TILE, ROW_TILE), at].astype(F32)
                square = x * x
                square = square[:half_tile] + square[half_tile:]
                if edge:
                    seg[targets[t], :, at] += square
                else:
                    total = square if total is None else total + square
            if not edge:
                seg[target, :, at] += total

    def body(i, edge):
        base = pl.multiple_of(i * STEP, STEP)
        make_table(odd, i * (STEP // DEPTH) + PIECE // DEPTH, PIECE // DEPTH)
        piece(base, PIECE, even, edge)
        make_table(even, (i + 1) * (STEP // DEPTH), PIECE // DEPTH)
        piece(base + PIECE, PIECE, odd, edge)

    @pl.loop(0, steps)
    def _(i):
        at = pl.ds(pl.multiple_of(i * STEP, STEP), STEP)
        pltpu.make_async_copy(x_hbm.at[at], x_ref.at[at], x_sems.at[i]).wait()
        cut = has_end(i * STEP, STEP)

        @pl.when(jnp.logical_not(cut))
        def _():
            body(i, False)

        @pl.when(cut)
        def _():
            body(i, True)

    done = steps * STEP
    if done < padded:
        if done < bulk:
            x_copy(steps).wait()
        first = min(PIECE, padded - done)
        if padded - done > first:
            make_table(odd, (done + first) // DEPTH, (padded - done - first) // DEPTH)
        piece(done, first, even, False)
        if padded - done > first:
            piece(done + first, padded - done - first, odd, False)

    for i, end in enumerate(ends):
        low = ends[i - 1] if i else jnp.int32(0)
        high = ends[i + 1] if i + 1 < len(ends) else jnp.int32(block_len)
        tile = end // ROW_TILE
        x = x_ref[pl.ds(pl.multiple_of(tile * ROW_TILE, ROW_TILE), ROW_TILE), :].astype(F32)
        spot = lax.broadcasted_iota(jnp.int32, x.shape, 0) + tile * ROW_TILE
        under = jnp.logical_and(spot >= low, spot < end)
        over = jnp.logical_and(spot >= end, spot < high)
        over = jnp.logical_and(over, high // ROW_TILE != tile)
        square = x * x
        for where, index in ((under, i), (over, i + 1)):
            kept = jnp.where(where, square, 0.0)
            seg[index] += kept[:half_tile] + kept[half_tile:]

    own_ref[:rows, :] = acc[:rows, :]
    back_ref[:rows, :] = acc[rows:, :].astype(BF16)
    parts = [seg[i] for i in range(segments)]
    row = lax.broadcasted_iota(jnp.int32, (half_tile, channels), 0)
    own_block = jnp.where(row == windows, (1 - dead[...]).astype(F32), 0.0)
    back_block = jnp.zeros((ROW_TILE, channels), F32)
    back_row = lax.broadcasted_iota(jnp.int32, (ROW_TILE, channels), 0)
    for w in range(windows):
        turn = parts[2 * w + 1]
        early = ahead[w] <= behind[w]
        after = sum(parts[2 * w + 2:]) + jnp.where(early, turn, 0.0)
        until = sum(parts[:2 * w + 1]) + jnp.where(early, turn, 0.0)
        own_block = jnp.where(row == w, jnp.sum(after, axis=0, keepdims=True), own_block)
        rest = jnp.sum(until, axis=0, keepdims=True)
        for term in range(3):
            piece_of = rest.astype(BF16).astype(F32)
            rest = rest - piece_of
            back_block = jnp.where(back_row == term * windows + w, piece_of, back_block)
    own_ref[rows:, :] = own_block
    back_ref[rows:, :] = back_block.astype(BF16)


def spectra_of(recording, offsets, band_bins, dead, windows):
    channels, block_len = recording.shape
    bins = band_bins.shape[0]
    rows = bins * windows * 2
    padded = pl.cdiv(block_len, DEPTH) * DEPTH
    bulk = block_len // ROW_TILE * ROW_TILE
    samples = recording.T
    hbm = pl.BlockSpec(memory_space=pltpu.HBM)
    whole = pl.BlockSpec(memory_space=pltpu.VMEM)
    state = pltpu.VMEM((rows, DEPTH), F32)
    table = pltpu.VMEM((2 * rows, PIECE), BF16)
    return pl.pallas_call(
        functools.partial(spectra_kernel, bins, windows, block_len),
        out_shape=(
            jax.ShapeDtypeStruct((rows + ROW_TILE // 2, channels), F32),
            jax.ShapeDtypeStruct((rows + ROW_TILE, channels), BF16),
        ),
        grid=(1,),
        in_specs=[
            hbm, hbm, hbm, hbm,
            pl.BlockSpec((ROW_TILE, channels), lambda i: (min(bulk, block_len - 1) // ROW_TILE, 0)),
        ],
        out_specs=(whole, whole),
        scratch_shapes=[
            pltpu.SMEM(offsets.shape, jnp.int32),
            pltpu.SMEM(band_bins.shape, jnp.int32),
            pltpu.VMEM((1, channels), jnp.int32),
            pltpu.VMEM((padded, channels), BF16),
            pltpu.VMEM((2 * rows, channels), F32),
            pltpu.VMEM((2 * windows + 2, ROW_TILE // 2, channels), F32),
            state, state, state, state, state, table, table,
            pltpu.SemaphoreType.DMA((3,)),
            pltpu.SemaphoreType.DMA((pl.cdiv(padded, STEP),)),
        ],
        compiler_params=pltpu.CompilerParams(vmem_limit_bytes=48 * 2**20),
        cost_estimate=pl.CostEstimate(
            flops=2 * channels * block_len * 2 * rows,
            bytes_accessed=channels * block_len * 2,
            transcendentals=0,
        ),
        name="band_spectra",
    )(offsets, band_bins, dead.reshape(1, channels), samples, samples)


def whiten_kernel(bins, windows, own_ref, more_ref, white_ref):
    rows = bins * windows * 2
    raw = own_ref[:rows, :] + more_ref[:rows, :].astype(F32)
    extra = more_ref[rows:, :].astype(F32)
    which = lax.broadcasted_iota(jnp.int32, (rows, 1), 0) % windows
    alive = own_ref[rows + windows:rows + windows + 1, :]
    scale = factor = None
    for w in range(windows):
        energy = own_ref[rows + w:rows + w + 1, :]
        for term in range(3):
            energy = energy + extra[term * windows + w:term * windows + w + 1, :]
        inverse = 1.0 / jnp.sqrt(energy / L + 1e-06)
        scale = inverse if w == 0 else jnp.where(which == w, inverse, scale)
    spectra = raw * scale
    power = spectra * spectra
    for w in range(windows):
        level = jnp.sum(jnp.where(which == w, power, 0.0), axis=0, keepdims=True) * (1.0 / bins)
        one = alive / jnp.sqrt(jnp.maximum(level, FLOOR))
        factor = one if w == 0 else jnp.where(which == w, one, factor)
    white = (spectra * factor).astype(BF16)
    width = white_ref.shape[2]
    for h in range(white_ref.shape[0]):
        white_ref[h] = white[:, h * width:(h + 1) * width]


def whiten(own, more, bins, windows, halves):
    channels = own.shape[1]
    rows = bins * windows * 2
    return pl.pallas_call(
        functools.partial(whiten_kernel, bins, windows),
        out_shape=jax.ShapeDtypeStruct((halves, rows, channels // halves), BF16),
        name="whiten",
    )(own, more)


def order_kernel(*refs):
    blocks, out_ref = refs[:-1], refs[-1]
    mine = lax.axis_index("chan")
    halves = blocks[0].shape[0]
    for away, block in enumerate(blocks):
        out_ref[pl.ds(jnp.bitwise_xor(mine, away) * halves, halves)] = block[...]


def in_order(blocks):
    halves, rows, width = blocks[0].shape
    return pl.pallas_call(
        order_kernel,
        out_shape=jax.ShapeDtypeStruct((len(blocks) * halves, rows, width), BF16),
        name="order_blocks",
    )(*blocks)


BINS_A_STEP = 2


def stack_kernel(windows, scale, devices, cols_ref, *refs):
    row_refs, out_ref, lhs, held = refs[:devices], refs[devices], refs[devices + 1], refs[devices + 2]
    per_group = ROW_TILE // (2 * windows)
    per_step = out_ref.shape[1]
    step = pl.program_id(0)
    width = cols_ref.shape[2]
    depth = devices * ROW_TILE
    halves, _, span = row_refs[0].shape
    first = step * per_step % per_group
    exact = math.frexp(scale)[0] == 0.5
    tm = lax.axis_index("tm")

    @pl.when(first == 0)
    def _():
        cols = cols_ref[...].astype(F32)
        if exact:
            cols = cols * scale
        head, tail = cols[:, :ROW_TILE // 2], cols[:, ROW_TILE // 2:]
        straight = cols.reshape(depth, width)
        turned = jnp.concatenate([-tail, head], axis=1).reshape(depth, width)
        lhs[:width, :] = straight.T.astype(BF16)
        lhs[width:, :] = turned.T.astype(BF16)
        for away in range(devices):
            to = pl.multiple_of(jnp.bitwise_xor(tm, away) * ROW_TILE, ROW_TILE)
            for h in range(halves):
                held[pl.ds(to, ROW_TILE), h * span:(h + 1) * span] = row_refs[away][h].astype(F32)

    channels = halves * span
    which = lax.broadcasted_iota(jnp.int32, (depth, 1), 0) % (ROW_TILE // 2) // windows
    for b in range(per_step):
        for n in range(0, channels, DEPTH):
            at = slice(n, min(n + DEPTH, channels))
            rhs = jnp.where(which == first + b, held[:, at], 0.0).astype(BF16)
            for part in range(2):
                product = jnp.dot(
                    lhs[part * width:(part + 1) * width, :], rhs, preferred_element_type=F32
                )
                if not exact:
                    product = product * scale
                out_ref[part, b, :, at] = product.astype(BF16)


def stacks_of(cols_all, row_blocks, bins, windows):
    devices = len(row_blocks)
    halves, _, span = row_blocks[0].shape
    width = cols_all.shape[2]
    per_group = ROW_TILE // (2 * windows)
    scale = 1.0 / math.sqrt(windows * devices)
    channels = halves * span
    group = lambda i: i * BINS_A_STEP // per_group
    return pl.pallas_call(
        functools.partial(stack_kernel, windows, scale, devices),
        out_shape=jax.ShapeDtypeStruct((2, bins, width, channels), BF16),
        grid=(bins // BINS_A_STEP,),
        in_specs=[pl.BlockSpec((devices, ROW_TILE, width), lambda i: (0, group(i), 0))]
        + [pl.BlockSpec((halves, ROW_TILE, span), lambda i: (0, group(i), 0))] * devices,
        out_specs=pl.BlockSpec((2, BINS_A_STEP, width, channels), lambda i: (0, i, 0, 0)),
        scratch_shapes=[
            pltpu.VMEM((2 * width, devices * ROW_TILE), BF16),
            pltpu.VMEM((devices * ROW_TILE, channels), F32),
        ],
        compiler_params=pltpu.CompilerParams(
            dimension_semantics=("arbitrary",), vmem_limit_bytes=40 * 2**20
        ),
        cost_estimate=pl.CostEstimate(
            flops=2 * 2 * bins * width * channels * devices * ROW_TILE,
            bytes_accessed=2 * bins * width * channels * 2,
            transcendentals=0,
        ),
        name="stack_products",
    )(cols_all, *row_blocks)


def from_partners(block, axis):
    count = lax.axis_size(axis)
    blocks = [block]
    for away in range(1, count):
        blocks.append(lax.ppermute(block, axis, [(i, i ^ away) for i in range(count)]))
    return blocks


def shards(recording, offsets, band_bins, dead_flags):
    channels, block_len = recording.shape
    windows = block_len // (L // 2)
    bins = band_bins.shape[0]
    halves = lax.axis_size("tm") // lax.axis_size("chan")
    own, back = spectra_of(recording, offsets, band_bins, dead_flags, windows)
    more = shifted(back, "tm", -1)
    white = whiten(own, more, bins, windows, halves)
    every_chan = in_order(from_partners(white, "chan"))
    row_blocks = from_partners(white, "tm")
    cols_all = lax.all_to_all(every_chan, "tm", split_axis=0, concat_axis=0, tiled=True)
    return stacks_of(cols_all, row_blocks, bins, windows)


def solution(mesh):
    placed = (P("chan", "tm"), P(), P(), P("chan"))
    return jax.shard_map(
        shards, mesh=mesh, in_specs=placed, out_specs=P(None, None, "tm", "chan"), check_vma=False
    )
```

```python
import functools
import math

import jax
import jax.numpy as jnp
from jax import lax
from jax.experimental import pallas as pl
from jax.experimental.pallas import tpu as pltpu
from jax.sharding import PartitionSpec as P

L = 15000
FLOOR = 0.7
F32 = jnp.float32
BF16 = jnp.bfloat16
LANE = 128
DEPTH = 256
PIECE = 512
STEP = 2 * PIECE
ROW_TILE = 16


def shifted(block, axis, distance):
    devices = range(lax.axis_size(axis))
    route = [(i - distance, i) for i in devices if i - distance in devices]
    return lax.ppermute(block, axis, route)


def cos_sin(turns, length):
    quarter = jnp.floor(turns * (4.0 / length) + 0.5)
    angle = (turns * 4.0 - quarter * length) * (math.pi / (2.0 * length))
    square = angle * angle
    sine = angle * (
        1.0 + square * (-1.0 / 6 + square * (1.0 / 120 + square * (-1.0 / 5040 + square * (1.0 / 362880))))
    )
    cosine = 1.0 + square * (
        -0.5 + square * (1.0 / 24 + square * (-1.0 / 720 + square * (1.0 / 40320)))
    )
    quadrant = quarter - 4.0 * jnp.floor(quarter * 0.25)
    odd = (quadrant == 1.0) | (quadrant == 3.0)
    cos_sign = jnp.where((quadrant == 1.0) | (quadrant == 2.0), -1.0, 1.0)
    sin_sign = jnp.where(quadrant >= 2.0, -1.0, 1.0)
    return cos_sign * jnp.where(odd, sine, cosine), sin_sign * jnp.where(odd, cosine, sine)


def spectra_kernel(
    bins, windows, block_len,
    offsets_hbm, bins_hbm, dead_hbm, x_hbm, tail_ref, own_ref, back_ref,
    offsets, band_bins, dead, x_ref, acc, seg, cos_now, sin_now, cos_turn, sin_turn, place, even, odd,
    small_sems, x_sems,
):
    channels = x_ref.shape[1]
    length, hop = L, L // 2
    rows = bins * windows * 2
    half_tile = ROW_TILE // 2
    per_group = half_tile // windows
    groups = rows // ROW_TILE
    states = groups * half_tile
    bulk = block_len // ROW_TILE * ROW_TILE
    padded = x_ref.shape[0]
    steps = padded // STEP
    columns = [slice(n, min(n + DEPTH, channels)) for n in range(0, channels, DEPTH)]

    def x_copy(i):
        size = min(STEP, bulk - i * STEP)
        at = pl.ds(i * STEP, size)
        return pltpu.make_async_copy(x_hbm.at[at], x_ref.at[at], x_sems.at[i])

    small = [
        pltpu.make_async_copy(offsets_hbm, offsets, small_sems.at[0]),
        pltpu.make_async_copy(bins_hbm, band_bins, small_sems.at[1]),
        pltpu.make_async_copy(dead_hbm, dead, small_sems.at[2]),
    ]
    for copy in small:
        copy.start()
    for i in range(pl.cdiv(bulk, STEP)):
        x_copy(i).start()
    for copy in small:
        copy.wait()

    tm = lax.axis_index("tm")
    ahead = [offsets[tm * windows + w] + w * hop for w in range(windows)]
    before = jnp.maximum(tm - 1, 0) * windows
    behind = [offsets[before + w] + w * hop + length - block_len for w in range(windows)]
    ends = []
    for w in range(windows):
        ends += [jnp.minimum(ahead[w], behind[w]), jnp.maximum(ahead[w], behind[w])]
    segments = len(ends) + 1

    def make_table(table, j, index):
        moved = jnp.asarray(index * DEPTH, jnp.int32).astype(F32)
        for side in range(2):
            limit = moved if side else -moved
            for g in range(groups):
                at = slice(side * states + g * half_tile, side * states + (g + 1) * half_tile)
                to = side * rows + g * ROW_TILE
                c, s = cos_now[at, :], sin_now[at, :]
                inside = place[at, :] >= limit
                wave = jnp.concatenate([jnp.where(inside, c, 0.0), jnp.where(inside, s, 0.0)], axis=0)
                table[to:to + ROW_TILE, j * DEPTH:(j + 1) * DEPTH] = wave.astype(BF16)
                ct, st = cos_turn[at, :], sin_turn[at, :]
                cos_now[at, :] = c * ct + s * st
                sin_now[at, :] = s * ct - c * st

    shape = (half_tile, DEPTH)
    row = lax.broadcasted_iota(jnp.int32, shape, 0)
    lane = lax.broadcasted_iota(jnp.int32, shape, 1).astype(F32)
    norm = 1.0 / math.sqrt(length)
    for side in range(2):
        for g in range(groups):
            at = slice(side * states + g * half_tile, side * states + (g + 1) * half_tile)
            tone = jnp.zeros(shape, jnp.int32)
            start = jnp.zeros(shape, jnp.int32)
            for i in range(per_group):
                tone = jnp.where(row // windows == i, band_bins[g * per_group + i], tone)
            for w in range(windows):
                here = behind[w] - length if side else ahead[w]
                start = jnp.where(row % windows == w, here, start)
            tone, start = tone.astype(F32), start.astype(F32)
            cosine, sine = cos_sin((lane - start) * tone, length)
            cos_now[at, :] = cosine * norm
            sin_now[at, :] = -sine * norm
            cos_turn[at, :], sin_turn[at, :] = cos_sin(tone * DEPTH, length)
            place[at, :] = start + (length - 1) - lane if side else lane - start
    for j in range(PIECE // DEPTH):
        make_table(even, j, j)
    acc[...] = jnp.zeros_like(acc)
    seg[...] = jnp.zeros_like(seg)
    x_ref[bulk:, :] = jnp.zeros((padded - bulk, channels), BF16)
    if block_len > bulk:
        inside = lax.broadcasted_iota(jnp.int32, (ROW_TILE, channels), 0) < block_len - bulk
        x_ref[bulk:bulk + ROW_TILE, :] = jnp.where(inside, tail_ref[...].astype(F32), 0.0).astype(BF16)

    def segment_of(position):
        index = jnp.int32(0)
        for end in ends:
            index += (end <= position).astype(jnp.int32)
        return index

    def has_end(first, size):
        return functools.reduce(
            jnp.logical_or, [jnp.logical_and(end >= first, end < first + size) for end in ends]
        )

    def weights_of(base, tiles, first):
        kept = []
        for t in range(tiles):
            at = base + t * ROW_TILE
            whole = jnp.logical_not(has_end(at, ROW_TILE))
            index = segment_of(at) - first
            kept.append([
                jnp.where(jnp.logical_and(whole, index == k), 1.0, 0.0).astype(F32) for k in range(3)
            ])
        return kept

    def energy(base, size, at, weights):
        totals = [None] * (3 if weights else 1)
        for t in range(size // ROW_TILE):
            x = x_ref[pl.ds(base + t * ROW_TILE, ROW_TILE), at].astype(F32)
            square = x * x
            square = square[:half_tile] + square[half_tile:]
            for k in range(len(totals)):
                term = square * weights[t][k] if weights else square
                totals[k] = term if t == 0 else totals[k] + term
        return totals

    def store(found):
        if found is None:
            return
        at, product, totals, target = found
        acc[:, at] += product
        for k, total in enumerate(totals):
            seg[target + k, :, at] += total

    def pieces(parts, edge):
        held = None
        for base, size, table, later, tile, count in parts:
            target = segment_of(base)
            weights = weights_of(base, size // ROW_TILE, target) if edge else None
            for n, at in enumerate(columns):
                product = jnp.dot(table[:, :size], x_ref[pl.ds(base, size), at], preferred_element_type=F32)
                totals = energy(base, size, at, weights)
                store(held)
                held = at, product, totals, target
                if later is not None and n < count:
                    make_table(later, n, tile + n)
            if later is not None:
                for n in range(len(columns), count):
                    make_table(later, n, tile + n)
        store(held)

    def body(i, edge):
        base = pl.multiple_of(i * STEP, STEP)
        tile = i * (STEP // DEPTH)
        per_piece = PIECE // DEPTH
        pieces([
            (base, PIECE, even, odd, tile + per_piece, per_piece),
            (base + PIECE, PIECE, odd, even, tile + 2 * per_piece, per_piece),
        ], edge)

    @pl.loop(0, steps)
    def _(i):
        at = pl.ds(pl.multiple_of(i * STEP, STEP), STEP)
        pltpu.make_async_copy(x_hbm.at[at], x_ref.at[at], x_sems.at[i]).wait()
        cut = has_end(i * STEP, STEP)

        @pl.when(jnp.logical_not(cut))
        def _():
            body(i, False)

        @pl.when(cut)
        def _():
            body(i, True)

    done = steps * STEP
    if done < padded:
        if done < bulk:
            x_copy(steps).wait()
        first = min(PIECE, padded - done)
        rest = padded - done - first
        tile = (done + first) // DEPTH
        parts = [(done, first, even, odd if rest else None, tile, rest // DEPTH)]
        if rest:
            parts.append((done + first, rest, odd, None, 0, 0))
        pieces(parts, False)

    for i, end in enumerate(ends):
        low = ends[i - 1] if i else jnp.int32(0)
        high = ends[i + 1] if i + 1 < len(ends) else jnp.int32(block_len)
        tile = end // ROW_TILE
        x = x_ref[pl.ds(pl.multiple_of(tile * ROW_TILE, ROW_TILE), ROW_TILE), :].astype(F32)
        spot = lax.broadcasted_iota(jnp.int32, x.shape, 0) + tile * ROW_TILE
        under = jnp.logical_and(spot >= low, spot < end)
        over = jnp.logical_and(spot >= end, spot < high)
        over = jnp.logical_and(over, high // ROW_TILE != tile)
        square = x * x
        for where, index in ((under, i), (over, i + 1)):
            kept = jnp.where(where, square, 0.0)
            seg[index] += kept[:half_tile] + kept[half_tile:]

    own_ref[:rows, :] = acc[:rows, :]
    back_ref[:rows, :] = acc[rows:, :].astype(BF16)
    parts = [seg[i] for i in range(segments)]
    row = lax.broadcasted_iota(jnp.int32, (half_tile, channels), 0)
    own_block = jnp.where(row == windows, (1 - dead[...]).astype(F32), 0.0)
    back_block = jnp.zeros((ROW_TILE, channels), F32)
    back_row = lax.broadcasted_iota(jnp.int32, (ROW_TILE, channels), 0)
    for w in range(windows):
        turn = parts[2 * w + 1]
        early = ahead[w] <= behind[w]
        after = sum(parts[2 * w + 2:]) + jnp.where(early, turn, 0.0)
        until = sum(parts[:2 * w + 1]) + jnp.where(early, turn, 0.0)
        own_block = jnp.where(row == w, jnp.sum(after, axis=0, keepdims=True), own_block)
        rest = jnp.sum(until, axis=0, keepdims=True)
        for term in range(3):
            piece_of = rest.astype(BF16).astype(F32)
            rest = rest - piece_of
            back_block = jnp.where(back_row == term * windows + w, piece_of, back_block)
    own_ref[rows:, :] = own_block
    back_ref[rows:, :] = back_block.astype(BF16)


def spectra_of(recording, offsets, band_bins, dead, windows):
    channels, block_len = recording.shape
    bins = band_bins.shape[0]
    rows = bins * windows * 2
    padded = pl.cdiv(block_len, DEPTH) * DEPTH
    bulk = block_len // ROW_TILE * ROW_TILE
    samples = recording.T
    hbm = pl.BlockSpec(memory_space=pltpu.HBM)
    whole = pl.BlockSpec(memory_space=pltpu.VMEM)
    state = pltpu.VMEM((rows, DEPTH), F32)
    table = pltpu.VMEM((2 * rows, PIECE), BF16)
    return pl.pallas_call(
        functools.partial(spectra_kernel, bins, windows, block_len),
        out_shape=(
            jax.ShapeDtypeStruct((rows + ROW_TILE // 2, channels), F32),
            jax.ShapeDtypeStruct((rows + ROW_TILE, channels), BF16),
        ),
        grid=(1,),
        in_specs=[
            hbm, hbm, hbm, hbm,
            pl.BlockSpec((ROW_TILE, channels), lambda i: (min(bulk, block_len - 1) // ROW_TILE, 0)),
        ],
        out_specs=(whole, whole),
        scratch_shapes=[
            pltpu.SMEM(offsets.shape, jnp.int32),
            pltpu.SMEM(band_bins.shape, jnp.int32),
            pltpu.VMEM((1, channels), jnp.int32),
            pltpu.VMEM((padded, channels), BF16),
            pltpu.VMEM((2 * rows, channels), F32),
            pltpu.VMEM((2 * windows + 3, ROW_TILE // 2, channels), F32),
            state, state, state, state, state, table, table,
            pltpu.SemaphoreType.DMA((3,)),
            pltpu.SemaphoreType.DMA((pl.cdiv(padded, STEP),)),
        ],
        compiler_params=pltpu.CompilerParams(vmem_limit_bytes=60 * 2**20),
        cost_estimate=pl.CostEstimate(
            flops=2 * channels * block_len * 2 * rows,
            bytes_accessed=channels * block_len * 2,
            transcendentals=0,
        ),
        name="band_spectra",
    )(offsets, band_bins, dead.reshape(1, channels), samples, samples)


def whiten_kernel(bins, windows, own_ref, more_ref, *white_refs):
    rows = bins * windows * 2
    raw = own_ref[:rows, :] + more_ref[:rows, :].astype(F32)
    extra = more_ref[rows:, :].astype(F32)
    which = lax.broadcasted_iota(jnp.int32, (rows, 1), 0) % windows
    alive = own_ref[rows + windows:rows + windows + 1, :]
    scale = factor = None
    for w in range(windows):
        energy = own_ref[rows + w:rows + w + 1, :]
        for term in range(3):
            energy = energy + extra[term * windows + w:term * windows + w + 1, :]
        inverse = 1.0 / jnp.sqrt(energy / L + 1e-06)
        scale = inverse if w == 0 else jnp.where(which == w, inverse, scale)
    spectra = raw * scale
    power = spectra * spectra
    for w in range(windows):
        level = jnp.sum(jnp.where(which == w, power, 0.0), axis=0, keepdims=True) * (1.0 / bins)
        one = alive / jnp.sqrt(jnp.maximum(level, FLOOR))
        factor = one if w == 0 else jnp.where(which == w, one, factor)
    white = (spectra * factor).astype(BF16)
    for white_ref in white_refs:
        copies, halves, _, width = white_ref.shape
        for h in range(halves):
            for copy in range(copies):
                white_ref[copy, h] = white[:, h * width:(h + 1) * width]


def whiten(own, more, bins, windows, halves, copies):
    channels = own.shape[1]
    rows = bins * windows * 2
    return pl.pallas_call(
        functools.partial(whiten_kernel, bins, windows),
        out_shape=[
            jax.ShapeDtypeStruct((count, halves, rows, channels // halves), BF16) for count in copies
        ],
        compiler_params=pltpu.CompilerParams(vmem_limit_bytes=12 * 2**20),
        name="whiten",
    )(own, more)


BINS_A_STEP = 2


def stack_kernel(windows, scale, devices, cols_ref, *refs):
    row_refs, (out_ref, lhs, held) = refs[:devices], refs[devices:]
    per_group = ROW_TILE // (2 * windows)
    per_step = out_ref.shape[1]
    step = pl.program_id(0)
    width = cols_ref.shape[2]
    depth = devices * ROW_TILE
    halves, _, span = row_refs[0].shape
    tm = lax.axis_index("tm")
    first = step * per_step % per_group
    exact = math.frexp(scale)[0] == 0.5

    @pl.when(first == 0)
    def _():
        cols = cols_ref[...].astype(F32)
        if exact:
            cols = cols * scale
        head, tail = cols[:, :ROW_TILE // 2], cols[:, ROW_TILE // 2:]
        straight = cols.reshape(depth, width)
        turned = jnp.concatenate([-tail, head], axis=1).reshape(depth, width)
        lhs[:width, :] = straight.T.astype(BF16)
        lhs[width:, :] = turned.T.astype(BF16)
        for away in range(devices):
            to = pl.multiple_of(jnp.bitwise_xor(tm, away) * ROW_TILE, ROW_TILE)
            for h in range(halves):
                held[pl.ds(to, ROW_TILE), h * span:(h + 1) * span] = row_refs[away][h].astype(F32)

    channels = halves * span
    which = lax.broadcasted_iota(jnp.int32, (depth, 1), 0) % (ROW_TILE // 2) // windows
    tall = min(DEPTH, width)
    late = None
    for b in range(per_step):
        for n in range(0, channels, DEPTH):
            at = slice(n, min(n + DEPTH, channels))
            rhs = jnp.where(which == first + b, held[:, at], 0.0).astype(BF16)
            for part in range(2):
                for m in range(0, width, tall):
                    low = part * width + m
                    product = jnp.dot(lhs[low:low + tall, :], rhs, preferred_element_type=F32)
                    if not exact:
                        product = product * scale
                    product = product.astype(BF16)
                    if late is not None:
                        out_ref[late[0]] = late[1]
                    late = (part, b, slice(m, m + tall), at), product
    out_ref[late[0]] = late[1]


def stacks_of(cols_all, row_blocks, bins, windows):
    devices = len(row_blocks)
    halves, _, span = row_blocks[0].shape
    width = cols_all.shape[2]
    per_group = ROW_TILE // (2 * windows)
    scale = 1.0 / math.sqrt(windows * devices)
    channels = halves * span
    group = lambda i: i * BINS_A_STEP // per_group
    return pl.pallas_call(
        functools.partial(stack_kernel, windows, scale, devices),
        out_shape=jax.ShapeDtypeStruct((2, bins, width, channels), BF16),
        grid=(bins // BINS_A_STEP,),
        in_specs=[pl.BlockSpec((devices, ROW_TILE, width), lambda i: (0, group(i), 0))]
        + [pl.BlockSpec((halves, ROW_TILE, span), lambda i: (0, group(i), 0))] * devices,
        out_specs=pl.BlockSpec((2, BINS_A_STEP, width, channels), lambda i: (0, i, 0, 0)),
        scratch_shapes=[
            pltpu.VMEM((2 * width, devices * ROW_TILE), BF16),
            pltpu.VMEM((devices * ROW_TILE, channels), F32),
        ],
        compiler_params=pltpu.CompilerParams(
            dimension_semantics=("arbitrary",), vmem_limit_bytes=40 * 2**20
        ),
        cost_estimate=pl.CostEstimate(
            flops=2 * 2 * bins * width * channels * devices * ROW_TILE,
            bytes_accessed=2 * bins * width * channels * 2,
            transcendentals=0,
        ),
        name="stack_products",
    )(cols_all, *row_blocks)


def exchanged(blocks, axis):
    return lax.all_to_all(blocks, axis, split_axis=0, concat_axis=0, tiled=True)


def from_partner(block, axis, away):
    return lax.ppermute(block, axis, [(i, i ^ away) for i in range(lax.axis_size(axis))])


def shards(recording, offsets, band_bins, dead_flags):
    channels, block_len = recording.shape
    windows = block_len // (L // 2)
    bins = band_bins.shape[0]
    chan_count, tm_count = lax.axis_size("chan"), lax.axis_size("tm")
    halves = tm_count // chan_count
    own, back = spectra_of(recording, offsets, band_bins, dead_flags, windows)
    more = shifted(back, "tm", -1)
    white, for_chan = whiten(own, more, bins, windows, halves, (1, chan_count))
    white = white[0]
    row_blocks = {0: white}
    for away in [*range(2, tm_count, 2), 1]:
        row_blocks[away] = from_partner(white, "tm", away)
    every_chan = exchanged(for_chan, "chan").reshape(tm_count, *for_chan.shape[2:])
    for away in range(2, tm_count, 2):
        row_blocks[away + 1] = from_partner(row_blocks[away], "tm", 1)
    cols_all = exchanged(every_chan, "tm")
    return stacks_of(cols_all, [row_blocks[i] for i in range(tm_count)], bins, windows)


def solution(mesh):
    placed = (P("chan", "tm"), P(), P(), P("chan"))
    return jax.shard_map(
        shards, mesh=mesh, in_specs=placed, out_specs=P(None, None, "tm", "chan"), check_vma=False
    )
```

```python
import functools
import math

import jax
import jax.numpy as jnp
from jax import lax
from jax.experimental import pallas as pl
from jax.experimental.pallas import tpu as pltpu
from jax.sharding import PartitionSpec as P

L = 15000
FLOOR = 0.7
F32 = jnp.float32
BF16 = jnp.bfloat16
LANE = 128
DEPTH = 256
PIECE = 1024
STEP = 2 * PIECE
ROW_TILE = 16


def shifted(block, axis, distance):
    devices = range(lax.axis_size(axis))
    route = [(i - distance, i) for i in devices if i - distance in devices]
    return lax.ppermute(block, axis, route)


def cos_sin(turns, length):
    quarter = jnp.floor(turns * (4.0 / length) + 0.5)
    angle = (turns * 4.0 - quarter * length) * (math.pi / (2.0 * length))
    square = angle * angle
    sine = angle * (
        1.0 + square * (-1.0 / 6 + square * (1.0 / 120 + square * (-1.0 / 5040 + square * (1.0 / 362880))))
    )
    cosine = 1.0 + square * (
        -0.5 + square * (1.0 / 24 + square * (-1.0 / 720 + square * (1.0 / 40320)))
    )
    quadrant = quarter - 4.0 * jnp.floor(quarter * 0.25)
    odd = (quadrant == 1.0) | (quadrant == 3.0)
    cos_sign = jnp.where((quadrant == 1.0) | (quadrant == 2.0), -1.0, 1.0)
    sin_sign = jnp.where(quadrant >= 2.0, -1.0, 1.0)
    return cos_sign * jnp.where(odd, sine, cosine), sin_sign * jnp.where(odd, cosine, sine)


def spectra_kernel(
    bins, windows, block_len,
    offsets_hbm, bins_hbm, dead_hbm, x_hbm, tail_ref, own_ref, back_ref,
    offsets, band_bins, dead, x_ref, acc, seg, cos_now, sin_now, cos_turn, sin_turn, place, even, odd,
    small_sems, x_sems,
):
    channels = x_ref.shape[1]
    length, hop = L, L // 2
    rows = bins * windows * 2
    half_tile = ROW_TILE // 2
    per_group = half_tile // windows
    groups = rows // ROW_TILE
    states = groups * half_tile
    bulk = block_len // ROW_TILE * ROW_TILE
    padded = x_ref.shape[0]
    steps = padded // STEP

    def x_copy(i):
        size = min(STEP, bulk - i * STEP)
        at = pl.ds(i * STEP, size)
        return pltpu.make_async_copy(x_hbm.at[at], x_ref.at[at], x_sems.at[i])

    small = [
        pltpu.make_async_copy(offsets_hbm, offsets, small_sems.at[0]),
        pltpu.make_async_copy(bins_hbm, band_bins, small_sems.at[1]),
        pltpu.make_async_copy(dead_hbm, dead, small_sems.at[2]),
    ]
    for copy in small:
        copy.start()
    for i in range(pl.cdiv(bulk, STEP)):
        x_copy(i).start()
    for copy in small:
        copy.wait()

    tm = lax.axis_index("tm")
    ahead = [offsets[tm * windows + w] + w * hop for w in range(windows)]
    before = jnp.maximum(tm - 1, 0) * windows
    behind = [offsets[before + w] + w * hop + length - block_len for w in range(windows)]
    ends = []
    for w in range(windows):
        ends += [jnp.minimum(ahead[w], behind[w]), jnp.maximum(ahead[w], behind[w])]
    segments = len(ends) + 1
    trash = segments

    def make_table(table, first, count):
        for j in range(count):
            moved = jnp.asarray((first + j) * DEPTH, jnp.int32).astype(F32)
            for side in range(2):
                limit = moved if side else -moved
                for g in range(groups):
                    at = slice(side * states + g * half_tile, side * states + (g + 1) * half_tile)
                    to = side * rows + g * ROW_TILE
                    c, s = cos_now[at, :], sin_now[at, :]
                    inside = place[at, :] >= limit
                    wave = jnp.concatenate([jnp.where(inside, c, 0.0), jnp.where(inside, s, 0.0)], axis=0)
                    table[to:to + ROW_TILE, j * DEPTH:(j + 1) * DEPTH] = wave.astype(BF16)
                    ct, st = cos_turn[at, :], sin_turn[at, :]
                    cos_now[at, :] = c * ct + s * st
                    sin_now[at, :] = s * ct - c * st

    shape = (half_tile, DEPTH)
    row = lax.broadcasted_iota(jnp.int32, shape, 0)
    lane = lax.broadcasted_iota(jnp.int32, shape, 1).astype(F32)
    norm = 1.0 / math.sqrt(length)
    for side in range(2):
        for g in range(groups):
            at = slice(side * states + g * half_tile, side * states + (g + 1) * half_tile)
            tone = jnp.zeros(shape, jnp.int32)
            start = jnp.zeros(shape, jnp.int32)
            for i in range(per_group):
                tone = jnp.where(row // windows == i, band_bins[g * per_group + i], tone)
            for w in range(windows):
                here = behind[w] - length if side else ahead[w]
                start = jnp.where(row % windows == w, here, start)
            tone, start = tone.astype(F32), start.astype(F32)
            cosine, sine = cos_sin((lane - start) * tone, length)
            cos_now[at, :] = cosine * norm
            sin_now[at, :] = -sine * norm
            cos_turn[at, :], sin_turn[at, :] = cos_sin(tone * DEPTH, length)
            place[at, :] = start + (length - 1) - lane if side else lane - start
    make_table(even, 0, PIECE // DEPTH)
    acc[...] = jnp.zeros_like(acc)
    seg[...] = jnp.zeros_like(seg)
    x_ref[bulk:, :] = jnp.zeros((padded - bulk, channels), BF16)
    if block_len > bulk:
        inside = lax.broadcasted_iota(jnp.int32, (ROW_TILE, channels), 0) < block_len - bulk
        x_ref[bulk:bulk + ROW_TILE, :] = jnp.where(inside, tail_ref[...].astype(F32), 0.0).astype(BF16)

    def segment_of(position):
        index = jnp.int32(0)
        for end in ends:
            index += (end <= position).astype(jnp.int32)
        return index

    def has_end(first, size):
        return functools.reduce(
            jnp.logical_or, [jnp.logical_and(end >= first, end < first + size) for end in ends]
        )

    def piece(base, size, table, edge):
        tiles = size // ROW_TILE
        if edge:
            targets = [
                jnp.where(has_end(base + t * ROW_TILE, ROW_TILE), trash, segment_of(base + t * ROW_TILE))
                for t in range(tiles)
            ]
        else:
            target = segment_of(base)
        acc[...] += jnp.dot(table[:, :size], x_ref[pl.ds(base, size), :], preferred_element_type=F32)
        total = None
        for t in range(tiles):
            x = x_ref[pl.ds(base + t * ROW_TILE, ROW_TILE), :].astype(F32)
            square = x * x
            square = square[:half_tile] + square[half_tile:]
            if edge:
                seg[targets[t]] += square
            else:
                total = square if total is None else total + square
        if not edge:
            seg[target] += total

    def body(i, edge):
        base = pl.multiple_of(i * STEP, STEP)
        piece(base, PIECE, even, edge)
        make_table(odd, i * (STEP // DEPTH) + PIECE // DEPTH, PIECE // DEPTH)
        piece(base + PIECE, PIECE, odd, edge)
        make_table(even, (i + 1) * (STEP // DEPTH), PIECE // DEPTH)

    @pl.loop(0, steps)
    def _(i):
        at = pl.ds(pl.multiple_of(i * STEP, STEP), STEP)
        pltpu.make_async_copy(x_hbm.at[at], x_ref.at[at], x_sems.at[i]).wait()
        cut = has_end(i * STEP, STEP)

        @pl.when(jnp.logical_not(cut))
        def _():
            body(i, False)

        @pl.when(cut)
        def _():
            body(i, True)

    done = steps * STEP
    if done < padded:
        if done < bulk:
            x_copy(steps).wait()
        first = min(PIECE, padded - done)
        if padded - done > first:
            make_table(odd, (done + first) // DEPTH, (padded - done - first) // DEPTH)
        piece(done, first, even, False)
        if padded - done > first:
            piece(done + first, padded - done - first, odd, False)

    for i, end in enumerate(ends):
        low = ends[i - 1] if i else jnp.int32(0)
        high = ends[i + 1] if i + 1 < len(ends) else jnp.int32(block_len)
        tile = end // ROW_TILE
        x = x_ref[pl.ds(pl.multiple_of(tile * ROW_TILE, ROW_TILE), ROW_TILE), :].astype(F32)
        spot = lax.broadcasted_iota(jnp.int32, x.shape, 0) + tile * ROW_TILE
        under = jnp.logical_and(spot >= low, spot < end)
        over = jnp.logical_and(spot >= end, spot < high)
        over = jnp.logical_and(over, high // ROW_TILE != tile)
        square = x * x
        for where, index in ((under, i), (over, i + 1)):
            kept = jnp.where(where, square, 0.0)
            seg[index] += kept[:half_tile] + kept[half_tile:]

    own_ref[:rows, :] = acc[:rows, :]
    back_ref[:rows, :] = acc[rows:, :].astype(BF16)
    parts = [seg[i] for i in range(segments)]
    row = lax.broadcasted_iota(jnp.int32, (half_tile, channels), 0)
    own_block = jnp.where(row == windows, (1 - dead[...]).astype(F32), 0.0)
    back_block = jnp.zeros((ROW_TILE, channels), F32)
    back_row = lax.broadcasted_iota(jnp.int32, (ROW_TILE, channels), 0)
    for w in range(windows):
        turn = parts[2 * w + 1]
        early = ahead[w] <= behind[w]
        after = sum(parts[2 * w + 2:]) + jnp.where(early, turn, 0.0)
        until = sum(parts[:2 * w + 1]) + jnp.where(early, turn, 0.0)
        own_block = jnp.where(row == w, jnp.sum(after, axis=0, keepdims=True), own_block)
        rest = jnp.sum(until, axis=0, keepdims=True)
        for term in range(3):
            piece_of = rest.astype(BF16).astype(F32)
            rest = rest - piece_of
            back_block = jnp.where(back_row == term * windows + w, piece_of, back_block)
    own_ref[rows:, :] = own_block
    back_ref[rows:, :] = back_block.astype(BF16)


def spectra_of(recording, offsets, band_bins, dead, windows):
    channels, block_len = recording.shape
    bins = band_bins.shape[0]
    rows = bins * windows * 2
    padded = pl.cdiv(block_len, DEPTH) * DEPTH
    bulk = block_len // ROW_TILE * ROW_TILE
    samples = recording.T
    hbm = pl.BlockSpec(memory_space=pltpu.HBM)
    whole = pl.BlockSpec(memory_space=pltpu.VMEM)
    state = pltpu.VMEM((rows, DEPTH), F32)
    table = pltpu.VMEM((2 * rows, PIECE), BF16)
    return pl.pallas_call(
        functools.partial(spectra_kernel, bins, windows, block_len),
        out_shape=(
            jax.ShapeDtypeStruct((rows + ROW_TILE // 2, channels), F32),
            jax.ShapeDtypeStruct((rows + ROW_TILE, channels), BF16),
        ),
        grid=(1,),
        in_specs=[
            hbm, hbm, hbm, hbm,
            pl.BlockSpec((ROW_TILE, channels), lambda i: (min(bulk, block_len - 1) // ROW_TILE, 0)),
        ],
        out_specs=(whole, whole),
        scratch_shapes=[
            pltpu.SMEM(offsets.shape, jnp.int32),
            pltpu.SMEM(band_bins.shape, jnp.int32),
            pltpu.VMEM((1, channels), jnp.int32),
            pltpu.VMEM((padded, channels), BF16),
            pltpu.VMEM((2 * rows, channels), F32),
            pltpu.VMEM((2 * windows + 2, ROW_TILE // 2, channels), F32),
            state, state, state, state, state, table, table,
            pltpu.SemaphoreType.DMA((3,)),
            pltpu.SemaphoreType.DMA((pl.cdiv(padded, STEP),)),
        ],
        compiler_params=pltpu.CompilerParams(vmem_limit_bytes=60 * 2**20),
        cost_estimate=pl.CostEstimate(
            flops=2 * channels * block_len * 2 * rows,
            bytes_accessed=channels * block_len * 2,
            transcendentals=0,
        ),
        name="band_spectra",
    )(offsets, band_bins, dead.reshape(1, channels), samples, samples)


def whiten_kernel(bins, windows, own_ref, more_ref, *white_refs):
    rows = bins * windows * 2
    raw = own_ref[:rows, :] + more_ref[:rows, :].astype(F32)
    extra = more_ref[rows:, :].astype(F32)
    which = lax.broadcasted_iota(jnp.int32, (rows, 1), 0) % windows
    alive = own_ref[rows + windows:rows + windows + 1, :]
    scale = factor = None
    for w in range(windows):
        energy = own_ref[rows + w:rows + w + 1, :]
        for term in range(3):
            energy = energy + extra[term * windows + w:term * windows + w + 1, :]
        inverse = 1.0 / jnp.sqrt(energy / L + 1e-06)
        scale = inverse if w == 0 else jnp.where(which == w, inverse, scale)
    spectra = raw * scale
    power = spectra * spectra
    for w in range(windows):
        level = jnp.sum(jnp.where(which == w, power, 0.0), axis=0, keepdims=True) * (1.0 / bins)
        one = alive / jnp.sqrt(jnp.maximum(level, FLOOR))
        factor = one if w == 0 else jnp.where(which == w, one, factor)
    white = (spectra * factor).astype(BF16)
    for white_ref in white_refs:
        copies, halves, _, width = white_ref.shape
        for h in range(halves):
            for copy in range(copies):
                white_ref[copy, h] = white[:, h * width:(h + 1) * width]


def whiten(own, more, bins, windows, halves, copies):
    channels = own.shape[1]
    rows = bins * windows * 2
    return pl.pallas_call(
        functools.partial(whiten_kernel, bins, windows),
        out_shape=[
            jax.ShapeDtypeStruct((count, halves, rows, channels // halves), BF16) for count in copies
        ],
        compiler_params=pltpu.CompilerParams(vmem_limit_bytes=12 * 2**20),
        name="whiten",
    )(own, more)


def stack_kernel(windows, scale, devices, cols_ref, *refs):
    row_refs, (out_hbm, lhs, held, made, sems) = refs[:devices], refs[devices:]
    per_group = ROW_TILE // (2 * windows)
    step = pl.program_id(0)
    width = cols_ref.shape[2]
    depth = devices * ROW_TILE
    halves, _, span = row_refs[0].shape
    channels = halves * span
    exact = math.frexp(scale)[0] == 0.5
    tm = lax.axis_index("tm")

    cols = cols_ref[...].astype(F32)
    if exact:
        cols = cols * scale
    head, tail = cols[:, :ROW_TILE // 2], cols[:, ROW_TILE // 2:]
    straight = cols.reshape(depth, width)
    turned = jnp.concatenate([-tail, head], axis=1).reshape(depth, width)
    lhs[:width, :] = straight.T.astype(BF16)
    lhs[width:, :] = turned.T.astype(BF16)
    for away in range(devices):
        to = pl.multiple_of(jnp.bitwise_xor(tm, away) * ROW_TILE, ROW_TILE)
        for h in range(halves):
            held[pl.ds(to, ROW_TILE), h * span:(h + 1) * span] = row_refs[away][h].astype(F32)

    def out_copy(slot, part, bin_index):
        return pltpu.make_async_copy(made.at[slot], out_hbm.at[part, bin_index], sems.at[slot])

    which = lax.broadcasted_iota(jnp.int32, (depth, 1), 0) % (ROW_TILE // 2) // windows
    for b in range(per_group):
        for part in range(2):
            slot = 2 * b + part

            @pl.when(step > 0)
            def _():
                out_copy(slot, part, (step - 1) * per_group + b).wait()

        for n in range(0, channels, DEPTH):
            at = slice(n, min(n + DEPTH, channels))
            rhs = jnp.where(which == b, held[:, at], 0.0).astype(BF16)
            for part in range(2):
                product = jnp.dot(
                    lhs[part * width:(part + 1) * width, :], rhs, preferred_element_type=F32
                )
                if not exact:
                    product = product * scale
                made[2 * b + part, :, at] = product.astype(BF16)
        for part in range(2):
            out_copy(2 * b + part, part, step * per_group + b).start()

    @pl.when(step == pl.num_programs(0) - 1)
    def _():
        for b in range(per_group):
            for part in range(2):
                out_copy(2 * b + part, part, step * per_group + b).wait()


def stacks_of(cols_all, row_blocks, bins, windows):
    devices = len(row_blocks)
    halves, _, span = row_blocks[0].shape
    width = cols_all.shape[2]
    per_group = ROW_TILE // (2 * windows)
    scale = 1.0 / math.sqrt(windows * devices)
    channels = halves * span
    return pl.pallas_call(
        functools.partial(stack_kernel, windows, scale, devices),
        out_shape=jax.ShapeDtypeStruct((2, bins, width, channels), BF16),
        grid=(bins // per_group,),
        in_specs=[pl.BlockSpec((devices, ROW_TILE, width), lambda i: (0, i, 0))]
        + [pl.BlockSpec((halves, ROW_TILE, span), lambda i: (0, i, 0))] * devices,
        out_specs=pl.BlockSpec(memory_space=pltpu.HBM),
        scratch_shapes=[
            pltpu.VMEM((2 * width, devices * ROW_TILE), BF16),
            pltpu.VMEM((devices * ROW_TILE, channels), F32),
            pltpu.VMEM((2 * per_group, width, channels), BF16),
            pltpu.SemaphoreType.DMA((2 * per_group,)),
        ],
        compiler_params=pltpu.CompilerParams(
            dimension_semantics=("arbitrary",), vmem_limit_bytes=40 * 2**20
        ),
        cost_estimate=pl.CostEstimate(
            flops=2 * 2 * bins * width * channels * devices * ROW_TILE,
            bytes_accessed=2 * bins * width * channels * 2,
            transcendentals=0,
        ),
        name="stack_products",
    )(cols_all, *row_blocks)


def after(block, *others):
    return pl.pallas_call(
        lambda *refs: None,
        out_shape=jax.ShapeDtypeStruct(block.shape, block.dtype),
        in_specs=[pl.BlockSpec(memory_space=pl.ANY)] * (1 + len(others)),
        out_specs=pl.BlockSpec(memory_space=pl.ANY),
        input_output_aliases={0: 0},
        name="after",
    )(block, *others)


def exchanged(blocks, axis):
    return lax.all_to_all(blocks, axis, split_axis=0, concat_axis=0, tiled=True)


def from_partner(block, axis, away):
    return lax.ppermute(block, axis, [(i, i ^ away) for i in range(lax.axis_size(axis))])


def shards(recording, offsets, band_bins, dead_flags):
    channels, block_len = recording.shape
    windows = block_len // (L // 2)
    bins = band_bins.shape[0]
    chan_count, tm_count = lax.axis_size("chan"), lax.axis_size("tm")
    halves = tm_count // chan_count
    own, back = spectra_of(recording, offsets, band_bins, dead_flags, windows)
    more = shifted(back, "tm", -1)
    white, for_chan = whiten(own, more, bins, windows, halves, (1, chan_count))
    white = white[0]
    row_blocks = {0: white}
    for away in [*range(2, tm_count, 2), 1]:
        row_blocks[away] = from_partner(white, "tm", away)
    every_chan = exchanged(for_chan, "chan").reshape(tm_count, *for_chan.shape[2:])
    every_chan = after(every_chan, *[row_blocks[away] for away in range(2, tm_count, 2)])
    for away in range(2, tm_count, 2):
        row_blocks[away + 1] = from_partner(row_blocks[away], "tm", 1)
    cols_all = exchanged(every_chan, "tm")
    return stacks_of(cols_all, [row_blocks[i] for i in range(tm_count)], bins, windows)


def solution(mesh):
    placed = (P("chan", "tm"), P(), P(), P("chan"))
    return jax.shard_map(
        shards, mesh=mesh, in_specs=placed, out_specs=P(None, None, "tm", "chan"), check_vma=False
    )
```

```python
import functools
import math

import jax
import jax.numpy as jnp
from jax import lax
from jax.experimental import pallas as pl
from jax.experimental.pallas import tpu as pltpu
from jax.sharding import PartitionSpec as P

L = 15000
FLOOR = 0.7
F32 = jnp.float32
BF16 = jnp.bfloat16
LANE = 128
DEPTH = 256
PIECE = 512
STEP = 2 * PIECE
ROW_TILE = 16


def shifted(block, axis, distance):
    devices = range(lax.axis_size(axis))
    route = [(i - distance, i) for i in devices if i - distance in devices]
    return lax.ppermute(block, axis, route)


def cos_sin(turns, length):
    quarter = jnp.floor(turns * (4.0 / length) + 0.5)
    angle = (turns * 4.0 - quarter * length) * (math.pi / (2.0 * length))
    square = angle * angle
    sine = angle * (
        1.0 + square * (-1.0 / 6 + square * (1.0 / 120 + square * (-1.0 / 5040 + square * (1.0 / 362880))))
    )
    cosine = 1.0 + square * (
        -0.5 + square * (1.0 / 24 + square * (-1.0 / 720 + square * (1.0 / 40320)))
    )
    quadrant = quarter - 4.0 * jnp.floor(quarter * 0.25)
    odd = (quadrant == 1.0) | (quadrant == 3.0)
    cos_sign = jnp.where((quadrant == 1.0) | (quadrant == 2.0), -1.0, 1.0)
    sin_sign = jnp.where(quadrant >= 2.0, -1.0, 1.0)
    return cos_sign * jnp.where(odd, sine, cosine), sin_sign * jnp.where(odd, cosine, sine)


def spectra_kernel(
    bins, windows, block_len,
    offsets_hbm, bins_hbm, dead_hbm, x_hbm, tail_ref, own_ref, back_ref,
    offsets, band_bins, dead, x_ref, acc, seg, cos_now, sin_now, cos_turn, sin_turn, place, even, odd,
    small_sems, x_sems,
):
    channels = x_ref.shape[1]
    length, hop = L, L // 2
    rows = bins * windows * 2
    half_tile = ROW_TILE // 2
    per_group = half_tile // windows
    groups = rows // ROW_TILE
    states = groups * half_tile
    bulk = block_len // ROW_TILE * ROW_TILE
    padded = x_ref.shape[0]
    steps = padded // STEP
    columns = [slice(n, min(n + DEPTH, channels)) for n in range(0, channels, DEPTH)]

    def x_copy(i):
        size = min(STEP, bulk - i * STEP)
        at = pl.ds(i * STEP, size)
        return pltpu.make_async_copy(x_hbm.at[at], x_ref.at[at], x_sems.at[i])

    small = [
        pltpu.make_async_copy(offsets_hbm, offsets, small_sems.at[0]),
        pltpu.make_async_copy(bins_hbm, band_bins, small_sems.at[1]),
        pltpu.make_async_copy(dead_hbm, dead, small_sems.at[2]),
    ]
    for copy in small:
        copy.start()
    for i in range(pl.cdiv(bulk, STEP)):
        x_copy(i).start()
    for copy in small:
        copy.wait()

    tm = lax.axis_index("tm")
    ahead = [offsets[tm * windows + w] + w * hop for w in range(windows)]
    before = jnp.maximum(tm - 1, 0) * windows
    behind = [offsets[before + w] + w * hop + length - block_len for w in range(windows)]
    ends = []
    for w in range(windows):
        ends += [jnp.minimum(ahead[w], behind[w]), jnp.maximum(ahead[w], behind[w])]
    segments = len(ends) + 1
    trash = segments

    def make_table(table, first, count):
        for j in range(count):
            moved = jnp.asarray((first + j) * DEPTH, jnp.int32).astype(F32)
            for side in range(2):
                limit = moved if side else -moved
                for g in range(groups):
                    at = slice(side * states + g * half_tile, side * states + (g + 1) * half_tile)
                    to = side * rows + g * ROW_TILE
                    c, s = cos_now[at, :], sin_now[at, :]
                    inside = place[at, :] >= limit
                    wave = jnp.concatenate([jnp.where(inside, c, 0.0), jnp.where(inside, s, 0.0)], axis=0)
                    table[to:to + ROW_TILE, j * DEPTH:(j + 1) * DEPTH] = wave.astype(BF16)
                    ct, st = cos_turn[at, :], sin_turn[at, :]
                    cos_now[at, :] = c * ct + s * st
                    sin_now[at, :] = s * ct - c * st

    shape = (half_tile, DEPTH)
    row = lax.broadcasted_iota(jnp.int32, shape, 0)
    lane = lax.broadcasted_iota(jnp.int32, shape, 1).astype(F32)
    norm = 1.0 / math.sqrt(length)
    for side in range(2):
        for g in range(groups):
            at = slice(side * states + g * half_tile, side * states + (g + 1) * half_tile)
            tone = jnp.zeros(shape, jnp.int32)
            start = jnp.zeros(shape, jnp.int32)
            for i in range(per_group):
                tone = jnp.where(row // windows == i, band_bins[g * per_group + i], tone)
            for w in range(windows):
                here = behind[w] - length if side else ahead[w]
                start = jnp.where(row % windows == w, here, start)
            tone, start = tone.astype(F32), start.astype(F32)
            cosine, sine = cos_sin((lane - start) * tone, length)
            cos_now[at, :] = cosine * norm
            sin_now[at, :] = -sine * norm
            cos_turn[at, :], sin_turn[at, :] = cos_sin(tone * DEPTH, length)
            place[at, :] = start + (length - 1) - lane if side else lane - start
    make_table(even, 0, PIECE // DEPTH)
    acc[...] = jnp.zeros_like(acc)
    seg[...] = jnp.zeros_like(seg)
    x_ref[bulk:, :] = jnp.zeros((padded - bulk, channels), BF16)
    if block_len > bulk:
        inside = lax.broadcasted_iota(jnp.int32, (ROW_TILE, channels), 0) < block_len - bulk
        x_ref[bulk:bulk + ROW_TILE, :] = jnp.where(inside, tail_ref[...].astype(F32), 0.0).astype(BF16)

    def segment_of(position):
        index = jnp.int32(0)
        for end in ends:
            index += (end <= position).astype(jnp.int32)
        return index

    def has_end(first, size):
        return functools.reduce(
            jnp.logical_or, [jnp.logical_and(end >= first, end < first + size) for end in ends]
        )

    def piece(view, low, base, size, table, edge):
        tiles = size // ROW_TILE
        if edge:
            targets = [
                jnp.where(has_end(base + t * ROW_TILE, ROW_TILE), trash, segment_of(base + t * ROW_TILE))
                for t in range(tiles)
            ]
        else:
            target = segment_of(base)
        for at in columns:
            block = view[low:low + size, at]
            acc[:, at] += jnp.dot(table[:, :size], block, preferred_element_type=F32)
            total = None
            for t in range(tiles):
                x = view[low + t * ROW_TILE:low + (t + 1) * ROW_TILE, at].astype(F32)
                square = x * x
                square = square[:half_tile] + square[half_tile:]
                if edge:
                    seg[targets[t], :, at] += square
                else:
                    total = square if total is None else total + square
            if not edge:
                seg[target, :, at] += total

    def body(i, edge):
        base = pl.multiple_of(i * STEP, STEP)
        view = x_ref.at[pl.ds(base, STEP)]
        make_table(odd, i * (STEP // DEPTH) + PIECE // DEPTH, PIECE // DEPTH)
        piece(view, 0, base, PIECE, even, edge)
        make_table(even, (i + 1) * (STEP // DEPTH), PIECE // DEPTH)
        piece(view, PIECE, base + PIECE, PIECE, odd, edge)

    @pl.loop(0, steps)
    def _(i):
        at = pl.ds(pl.multiple_of(i * STEP, STEP), STEP)
        pltpu.make_async_copy(x_hbm.at[at], x_ref.at[at], x_sems.at[i]).wait()
        cut = has_end(i * STEP, STEP)

        @pl.when(jnp.logical_not(cut))
        def _():
            body(i, False)

        @pl.when(cut)
        def _():
            body(i, True)

    done = steps * STEP
    if done < padded:
        if done < bulk:
            x_copy(steps).wait()
        first = min(PIECE, padded - done)
        if padded - done > first:
            make_table(odd, (done + first) // DEPTH, (padded - done - first) // DEPTH)
        piece(x_ref, done, done, first, even, False)
        if padded - done > first:
            piece(x_ref, done + first, done + first, padded - done - first, odd, False)

    for i, end in enumerate(ends):
        low = ends[i - 1] if i else jnp.int32(0)
        high = ends[i + 1] if i + 1 < len(ends) else jnp.int32(block_len)
        tile = end // ROW_TILE
        x = x_ref[pl.ds(pl.multiple_of(tile * ROW_TILE, ROW_TILE), ROW_TILE), :].astype(F32)
        spot = lax.broadcasted_iota(jnp.int32, x.shape, 0) + tile * ROW_TILE
        under = jnp.logical_and(spot >= low, spot < end)
        over = jnp.logical_and(spot >= end, spot < high)
        over = jnp.logical_and(over, high // ROW_TILE != tile)
        square = x * x
        for where, index in ((under, i), (over, i + 1)):
            kept = jnp.where(where, square, 0.0)
            seg[index] += kept[:half_tile] + kept[half_tile:]

    own_ref[:rows, :] = acc[:rows, :]
    back_ref[:rows, :] = acc[rows:, :].astype(BF16)
    parts = [seg[i] for i in range(segments)]
    row = lax.broadcasted_iota(jnp.int32, (half_tile, channels), 0)
    own_block = jnp.where(row == windows, (1 - dead[...]).astype(F32), 0.0)
    back_block = jnp.zeros((ROW_TILE, channels), F32)
    back_row = lax.broadcasted_iota(jnp.int32, (ROW_TILE, channels), 0)
    for w in range(windows):
        turn = parts[2 * w + 1]
        early = ahead[w] <= behind[w]
        after = sum(parts[2 * w + 2:]) + jnp.where(early, turn, 0.0)
        until = sum(parts[:2 * w + 1]) + jnp.where(early, turn, 0.0)
        own_block = jnp.where(row == w, jnp.sum(after, axis=0, keepdims=True), own_block)
        rest = jnp.sum(until, axis=0, keepdims=True)
        for term in range(3):
            piece_of = rest.astype(BF16).astype(F32)
            rest = rest - piece_of
            back_block = jnp.where(back_row == term * windows + w, piece_of, back_block)
    own_ref[rows:, :] = own_block
    back_ref[rows:, :] = back_block.astype(BF16)


def spectra_of(recording, offsets, band_bins, dead, windows):
    channels, block_len = recording.shape
    bins = band_bins.shape[0]
    rows = bins * windows * 2
    padded = pl.cdiv(block_len, DEPTH) * DEPTH
    bulk = block_len // ROW_TILE * ROW_TILE
    samples = recording.T
    hbm = pl.BlockSpec(memory_space=pltpu.HBM)
    whole = pl.BlockSpec(memory_space=pltpu.VMEM)
    state = pltpu.VMEM((rows, DEPTH), F32)
    table = pltpu.VMEM((2 * rows, PIECE), BF16)
    return pl.pallas_call(
        functools.partial(spectra_kernel, bins, windows, block_len),
        out_shape=(
            jax.ShapeDtypeStruct((rows + ROW_TILE // 2, channels), F32),
            jax.ShapeDtypeStruct((rows + ROW_TILE, channels), BF16),
        ),
        grid=(1,),
        in_specs=[
            hbm, hbm, hbm, hbm,
            pl.BlockSpec((ROW_TILE, channels), lambda i: (min(bulk, block_len - 1) // ROW_TILE, 0)),
        ],
        out_specs=(whole, whole),
        scratch_shapes=[
            pltpu.SMEM(offsets.shape, jnp.int32),
            pltpu.SMEM(band_bins.shape, jnp.int32),
            pltpu.VMEM((1, channels), jnp.int32),
            pltpu.VMEM((padded, channels), BF16),
            pltpu.VMEM((2 * rows, channels), F32),
            pltpu.VMEM((2 * windows + 2, ROW_TILE // 2, channels), F32),
            state, state, state, state, state, table, table,
            pltpu.SemaphoreType.DMA((3,)),
            pltpu.SemaphoreType.DMA((pl.cdiv(padded, STEP),)),
        ],
        compiler_params=pltpu.CompilerParams(vmem_limit_bytes=60 * 2**20),
        cost_estimate=pl.CostEstimate(
            flops=2 * channels * block_len * 2 * rows,
            bytes_accessed=channels * block_len * 2,
            transcendentals=0,
        ),
        name="band_spectra",
    )(offsets, band_bins, dead.reshape(1, channels), samples, samples)


def whiten_kernel(bins, windows, firsts, own_ref, more_ref, *white_refs):
    rows = bins * windows * 2
    raw = own_ref[:rows, :] + more_ref[:rows, :].astype(F32)
    extra = more_ref[rows:, :].astype(F32)
    which = lax.broadcasted_iota(jnp.int32, (rows, 1), 0) % windows
    alive = own_ref[rows + windows:rows + windows + 1, :]
    scale = factor = None
    for w in range(windows):
        energy = own_ref[rows + w:rows + w + 1, :]
        for term in range(3):
            energy = energy + extra[term * windows + w:term * windows + w + 1, :]
        inverse = 1.0 / jnp.sqrt(energy / L + 1e-06)
        scale = inverse if w == 0 else jnp.where(which == w, inverse, scale)
    spectra = raw * scale
    power = spectra * spectra
    for w in range(windows):
        level = jnp.sum(jnp.where(which == w, power, 0.0), axis=0, keepdims=True) * (1.0 / bins)
        one = alive / jnp.sqrt(jnp.maximum(level, FLOOR))
        factor = one if w == 0 else jnp.where(which == w, one, factor)
    white = (spectra * factor).astype(BF16)
    for first, white_ref in zip(firsts, white_refs):
        copies, halves, count, width = white_ref.shape
        for h in range(halves):
            for copy in range(copies):
                white_ref[copy, h] = white[first:first + count, h * width:(h + 1) * width]


def whiten(own, more, bins, windows, halves, wanted):
    channels = own.shape[1]
    return pl.pallas_call(
        functools.partial(whiten_kernel, bins, windows, [first for _, first, _ in wanted]),
        out_shape=[
            jax.ShapeDtypeStruct((copies, halves, count, channels // halves), BF16)
            for copies, _, count in wanted
        ],
        compiler_params=pltpu.CompilerParams(vmem_limit_bytes=12 * 2**20),
        name="whiten",
    )(own, more)


def stack_kernel(windows, scale, devices, first_group, cols_ref, *refs):
    row_refs, (out_hbm, lhs, held, made, sems) = refs[:devices], refs[-5:]
    per_group = ROW_TILE // (2 * windows)
    step = pl.program_id(0)
    width = cols_ref.shape[2]
    depth = devices * ROW_TILE
    halves, _, span = row_refs[0].shape
    channels = halves * span
    exact = math.frexp(scale)[0] == 0.5
    tm = lax.axis_index("tm")

    cols = cols_ref[...].astype(F32)
    if exact:
        cols = cols * scale
    head, tail = cols[:, :ROW_TILE // 2], cols[:, ROW_TILE // 2:]
    straight = cols.reshape(depth, width)
    turned = jnp.concatenate([-tail, head], axis=1).reshape(depth, width)
    lhs[:width, :] = straight.T.astype(BF16)
    lhs[width:, :] = turned.T.astype(BF16)
    for away in range(devices):
        to = pl.multiple_of(jnp.bitwise_xor(tm, away) * ROW_TILE, ROW_TILE)
        for h in range(halves):
            held[pl.ds(to, ROW_TILE), h * span:(h + 1) * span] = row_refs[away][h].astype(F32)

    def out_copy(slot, part, bin_index):
        to = out_hbm.at[part, first_group * per_group + bin_index]
        return pltpu.make_async_copy(made.at[slot], to, sems.at[slot])

    which = lax.broadcasted_iota(jnp.int32, (depth, 1), 0) % (ROW_TILE // 2) // windows
    for b in range(per_group):
        for part in range(2):
            slot = 2 * b + part

            @pl.when(step > 0)
            def _():
                out_copy(slot, part, (step - 1) * per_group + b).wait()

        for n in range(0, channels, DEPTH):
            at = slice(n, min(n + DEPTH, channels))
            rhs = jnp.where(which == b, held[:, at], 0.0).astype(BF16)
            for part in range(2):
                product = jnp.dot(
                    lhs[part * width:(part + 1) * width, :], rhs, preferred_element_type=F32
                )
                if not exact:
                    product = product * scale
                made[2 * b + part, :, at] = product.astype(BF16)
        for part in range(2):
            out_copy(2 * b + part, part, step * per_group + b).start()

    @pl.when(step == pl.num_programs(0) - 1)
    def _():
        for b in range(per_group):
            for part in range(2):
                out_copy(2 * b + part, part, step * per_group + b).wait()


def stacks_of(cols_all, row_blocks, first_group, bins, windows, before=None):
    devices = len(row_blocks)
    halves, _, span = row_blocks[0].shape
    _, rows, width = cols_all.shape
    per_group = ROW_TILE // (2 * windows)
    groups = rows // ROW_TILE
    scale = 1.0 / math.sqrt(windows * devices)
    channels = halves * span
    hbm = pl.BlockSpec(memory_space=pltpu.HBM)
    return pl.pallas_call(
        functools.partial(stack_kernel, windows, scale, devices, first_group),
        out_shape=jax.ShapeDtypeStruct((2, bins, width, channels), BF16),
        grid=(groups,),
        in_specs=[pl.BlockSpec((devices, ROW_TILE, width), lambda i: (0, i, 0))]
        + [pl.BlockSpec((halves, ROW_TILE, span), lambda i: (0, first_group + i, 0))] * devices
        + ([] if before is None else [hbm]),
        out_specs=hbm,
        input_output_aliases={} if before is None else {1 + devices: 0},
        scratch_shapes=[
            pltpu.VMEM((2 * width, devices * ROW_TILE), BF16),
            pltpu.VMEM((devices * ROW_TILE, channels), F32),
            pltpu.VMEM((2 * per_group, width, channels), BF16),
            pltpu.SemaphoreType.DMA((2 * per_group,)),
        ],
        compiler_params=pltpu.CompilerParams(
            dimension_semantics=("arbitrary",), vmem_limit_bytes=24 * 2**20
        ),
        cost_estimate=pl.CostEstimate(
            flops=2 * 2 * groups * per_group * width * channels * devices * ROW_TILE,
            bytes_accessed=2 * groups * per_group * width * channels * 2,
            transcendentals=0,
        ),
        name="stack_products",
    )(cols_all, *row_blocks, *([] if before is None else [before]))


def after(block, *others):
    return pl.pallas_call(
        lambda *refs: None,
        out_shape=jax.ShapeDtypeStruct(block.shape, block.dtype),
        in_specs=[pl.BlockSpec(memory_space=pl.ANY)] * (1 + len(others)),
        out_specs=pl.BlockSpec(memory_space=pl.ANY),
        input_output_aliases={0: 0},
        compiler_params=pltpu.CompilerParams(vmem_limit_bytes=2**20),
        name="after",
    )(block, *others)


def exchanged(blocks, axis):
    return lax.all_to_all(blocks, axis, split_axis=0, concat_axis=0, tiled=True)


def from_partner(block, axis, away):
    return lax.ppermute(block, axis, [(i, i ^ away) for i in range(lax.axis_size(axis))])


def shards(recording, offsets, band_bins, dead_flags):
    channels, block_len = recording.shape
    windows = block_len // (L // 2)
    bins = band_bins.shape[0]
    chan_count, tm_count = lax.axis_size("chan"), lax.axis_size("tm")
    halves = tm_count // chan_count
    own, back = spectra_of(recording, offsets, band_bins, dead_flags, windows)
    more = shifted(back, "tm", -1)
    rows = bins * windows * 2
    groups = rows // ROW_TILE
    cut = (groups + 1) // 2
    spans = [(0, cut), (cut, groups - cut)]
    white, *for_chan = whiten(
        own, more, bins, windows, halves,
        [(1, 0, rows)] + [(chan_count, first * ROW_TILE, count * ROW_TILE) for first, count in spans],
    )
    white = white[0]
    row_blocks = {0: white}
    for away in [*range(2, tm_count, 2), 1]:
        row_blocks[away] = from_partner(white, "tm", away)
    every_chan = [
        exchanged(block, "chan").reshape(tm_count, *block.shape[2:]) for block in for_chan
    ]
    every_chan[0] = after(every_chan[0], *[row_blocks[away] for away in range(2, tm_count, 2)])
    for away in range(2, tm_count, 2):
        row_blocks[away + 1] = from_partner(row_blocks[away], "tm", 1)
    cols = [exchanged(every_chan[0], "tm")]
    cols.append(exchanged(after(every_chan[1], cols[0]), "tm"))
    in_order = [row_blocks[i] for i in range(tm_count)]
    stacks = None
    for (first, _), part in zip(spans, cols):
        stacks = stacks_of(part, in_order, first, bins, windows, stacks)
    return stacks


def solution(mesh):
    placed = (P("chan", "tm"), P(), P(), P("chan"))
    return jax.shard_map(
        shards, mesh=mesh, in_specs=placed, out_specs=P(None, None, "tm", "chan"), check_vma=False
    )
```

```python
import functools
import math

import jax
import jax.numpy as jnp
from jax import lax
from jax.experimental import pallas as pl
from jax.experimental.pallas import tpu as pltpu
from jax.sharding import PartitionSpec as P

L = 15000
FLOOR = 0.7
F32 = jnp.float32
BF16 = jnp.bfloat16
LANE = 128
DEPTH = 256
STEP = 1024
ROW_TILE = 16


def shifted(block, axis, distance):
    devices = range(lax.axis_size(axis))
    route = [(i - distance, i) for i in devices if i - distance in devices]
    return lax.ppermute(block, axis, route)


def cos_sin(turns, length):
    quarter = jnp.floor(turns * (4.0 / length) + 0.5)
    angle = (turns * 4.0 - quarter * length) * (math.pi / (2.0 * length))
    square = angle * angle
    sine = angle * (
        1.0 + square * (-1.0 / 6 + square * (1.0 / 120 + square * (-1.0 / 5040 + square * (1.0 / 362880))))
    )
    cosine = 1.0 + square * (
        -0.5 + square * (1.0 / 24 + square * (-1.0 / 720 + square * (1.0 / 40320)))
    )
    quadrant = quarter - 4.0 * jnp.floor(quarter * 0.25)
    odd = (quadrant == 1.0) | (quadrant == 3.0)
    cos_sign = jnp.where((quadrant == 1.0) | (quadrant == 2.0), -1.0, 1.0)
    sin_sign = jnp.where(quadrant >= 2.0, -1.0, 1.0)
    return cos_sign * jnp.where(odd, sine, cosine), sin_sign * jnp.where(odd, cosine, sine)


def spectra_kernel(
    bins, windows, block_len,
    offsets_hbm, bins_hbm, dead_hbm, x_hbm, tail_ref, own_ref, back_ref,
    offsets, band_bins, dead, x_ref, acc, seg, part_seg, cos_now, sin_now, cos_turn, sin_turn, place, table,
    small_sems, x_sems,
):
    channels = x_ref.shape[1]
    length, hop = L, L // 2
    rows = bins * windows * 2
    half_tile = ROW_TILE // 2
    per_group = half_tile // windows
    groups = rows // ROW_TILE
    states = groups * half_tile
    bulk = block_len // ROW_TILE * ROW_TILE
    padded = x_ref.shape[0]
    steps = padded // STEP
    columns = [slice(n, min(n + DEPTH, channels)) for n in range(0, channels, DEPTH)]

    def x_copy(i):
        size = min(STEP, bulk - i * STEP)
        at = pl.ds(i * STEP, size)
        return pltpu.make_async_copy(x_hbm.at[at], x_ref.at[at], x_sems.at[i])

    small = [
        pltpu.make_async_copy(offsets_hbm, offsets, small_sems.at[0]),
        pltpu.make_async_copy(bins_hbm, band_bins, small_sems.at[1]),
        pltpu.make_async_copy(dead_hbm, dead, small_sems.at[2]),
    ]
    for copy in small:
        copy.start()
    for copy in small:
        copy.wait()
    for i in range(pl.cdiv(bulk, STEP)):
        x_copy(i).start()

    tm = lax.axis_index("tm")
    ahead = [offsets[tm * windows + w] + w * hop for w in range(windows)]
    before = jnp.maximum(tm - 1, 0) * windows
    behind = [offsets[before + w] + w * hop + length - block_len for w in range(windows)]
    ends = []
    for w in range(windows):
        ends += [jnp.minimum(ahead[w], behind[w]), jnp.maximum(ahead[w], behind[w])]
    segments = len(ends) + 1
    trash = segments

    def make_table(index):
        moved = (index * DEPTH).astype(F32)
        to_lanes = pl.ds(pl.multiple_of(index * DEPTH, DEPTH), DEPTH)
        for side in range(2):
            limit = moved if side else -moved
            for g in range(groups):
                at = slice(side * states + g * half_tile, side * states + (g + 1) * half_tile)
                to = side * rows + g * ROW_TILE
                c, s = cos_now[at, :], sin_now[at, :]
                inside = place[at, :] >= limit
                wave = jnp.concatenate([jnp.where(inside, c, 0.0), jnp.where(inside, s, 0.0)], axis=0)
                table[to:to + ROW_TILE, to_lanes] = wave.astype(BF16)
                ct, st = cos_turn[at, :], sin_turn[at, :]
                cos_now[at, :] = c * ct + s * st
                sin_now[at, :] = s * ct - c * st

    shape = (half_tile, DEPTH)
    row = lax.broadcasted_iota(jnp.int32, shape, 0)
    lane = lax.broadcasted_iota(jnp.int32, shape, 1).astype(F32)
    norm = 1.0 / math.sqrt(length)
    for side in range(2):
        for g in range(groups):
            at = slice(side * states + g * half_tile, side * states + (g + 1) * half_tile)
            tone = jnp.zeros(shape, jnp.int32)
            start = jnp.zeros(shape, jnp.int32)
            for i in range(per_group):
                tone = jnp.where(row // windows == i, band_bins[g * per_group + i], tone)
            for w in range(windows):
                here = behind[w] - length if side else ahead[w]
                start = jnp.where(row % windows == w, here, start)
            tone, start = tone.astype(F32), start.astype(F32)
            cosine, sine = cos_sin((lane - start) * tone, length)
            cos_now[at, :] = cosine * norm
            sin_now[at, :] = -sine * norm
            cos_turn[at, :], sin_turn[at, :] = cos_sin(tone * DEPTH, length)
            place[at, :] = start + (length - 1) - lane if side else lane - start

    @pl.loop(0, padded // DEPTH)
    def _(index):
        make_table(index)

    acc[...] = jnp.zeros_like(acc)
    seg[...] = jnp.zeros_like(seg)
    x_ref[bulk:, :] = jnp.zeros((padded - bulk, channels), BF16)
    if block_len > bulk:
        inside = lax.broadcasted_iota(jnp.int32, (ROW_TILE, channels), 0) < block_len - bulk
        x_ref[bulk:bulk + ROW_TILE, :] = jnp.where(inside, tail_ref[...].astype(F32), 0.0).astype(BF16)

    def segment_of(position):
        index = jnp.int32(0)
        for end in ends:
            index += (end <= position).astype(jnp.int32)
        return index

    def has_end(first, size):
        return functools.reduce(
            jnp.logical_or, [jnp.logical_and(end >= first, end < first + size) for end in ends]
        )

    def body(base, size, edge):
        view = x_ref.at[pl.ds(base, size)]
        waves = table.at[:, pl.ds(base, size)]
        tiles = size // ROW_TILE

        def squares(t, at):
            x = view[t * ROW_TILE:(t + 1) * ROW_TILE, at].astype(F32)
            square = x * x
            return square[:half_tile] + square[half_tile:]

        for at in columns:
            if not edge:
                total = squares(0, at)
                for t in range(1, tiles):
                    total = total + squares(t, at)
            product = jnp.dot(waves[...], view[:, at], preferred_element_type=F32)
            acc[:, at] += product
            if not edge:
                part_seg[:, at] = total
        if edge:
            for t in range(tiles):
                first = base + t * ROW_TILE
                target = jnp.where(has_end(first, ROW_TILE), trash, segment_of(first))
                for at in columns:
                    seg[target, :, at] += squares(t, at)
        else:
            seg[segment_of(base)] += part_seg[...]

    @pl.loop(0, steps)
    def _(i):
        at = pl.ds(pl.multiple_of(i * STEP, STEP), STEP)
        pltpu.make_async_copy(x_hbm.at[at], x_ref.at[at], x_sems.at[i]).wait()
        cut = has_end(i * STEP, STEP)

        @pl.when(jnp.logical_not(cut))
        def _():
            body(pl.multiple_of(i * STEP, STEP), STEP, False)

        @pl.when(cut)
        def _():
            body(pl.multiple_of(i * STEP, STEP), STEP, True)

    done = steps * STEP
    if done < padded:
        if done < bulk:
            x_copy(steps).wait()
        body(done, padded - done, False)

    for i, end in enumerate(ends):
        low = ends[i - 1] if i else jnp.int32(0)
        high = ends[i + 1] if i + 1 < len(ends) else jnp.int32(block_len)
        tile = end // ROW_TILE
        x = x_ref[pl.ds(pl.multiple_of(tile * ROW_TILE, ROW_TILE), ROW_TILE), :].astype(F32)
        spot = lax.broadcasted_iota(jnp.int32, x.shape, 0) + tile * ROW_TILE
        under = jnp.logical_and(spot >= low, spot < end)
        over = jnp.logical_and(spot >= end, spot < high)
        over = jnp.logical_and(over, high // ROW_TILE != tile)
        square = x * x
        for where, index in ((under, i), (over, i + 1)):
            kept = jnp.where(where, square, 0.0)
            seg[index] += kept[:half_tile] + kept[half_tile:]

    own_ref[:rows, :] = acc[:rows, :]
    back_ref[:rows, :] = acc[rows:, :].astype(BF16)
    parts = [seg[i] for i in range(segments)]
    row = lax.broadcasted_iota(jnp.int32, (half_tile, channels), 0)
    own_block = jnp.where(row == windows, (1 - dead[...]).astype(F32), 0.0)
    back_block = jnp.zeros((ROW_TILE, channels), F32)
    back_row = lax.broadcasted_iota(jnp.int32, (ROW_TILE, channels), 0)
    for w in range(windows):
        turn = parts[2 * w + 1]
        early = ahead[w] <= behind[w]
        after = sum(parts[2 * w + 2:]) + jnp.where(early, turn, 0.0)
        until = sum(parts[:2 * w + 1]) + jnp.where(early, turn, 0.0)
        own_block = jnp.where(row == w, jnp.sum(after, axis=0, keepdims=True), own_block)
        rest = jnp.sum(until, axis=0, keepdims=True)
        for term in range(3):
            piece_of = rest.astype(BF16).astype(F32)
            rest = rest - piece_of
            back_block = jnp.where(back_row == term * windows + w, piece_of, back_block)
    own_ref[rows:, :] = own_block
    back_ref[rows:, :] = back_block.astype(BF16)


def spectra_of(recording, offsets, band_bins, dead, windows):
    channels, block_len = recording.shape
    bins = band_bins.shape[0]
    rows = bins * windows * 2
    padded = pl.cdiv(block_len, DEPTH) * DEPTH
    bulk = block_len // ROW_TILE * ROW_TILE
    samples = recording.T
    hbm = pl.BlockSpec(memory_space=pltpu.HBM)
    whole = pl.BlockSpec(memory_space=pltpu.VMEM)
    state = pltpu.VMEM((rows, DEPTH), F32)
    return pl.pallas_call(
        functools.partial(spectra_kernel, bins, windows, block_len),
        out_shape=(
            jax.ShapeDtypeStruct((rows + ROW_TILE // 2, channels), F32),
            jax.ShapeDtypeStruct((rows + ROW_TILE, channels), BF16),
        ),
        grid=(1,),
        in_specs=[
            hbm, hbm, hbm, hbm,
            pl.BlockSpec((ROW_TILE, channels), lambda i: (min(bulk, block_len - 1) // ROW_TILE, 0)),
        ],
        out_specs=(whole, whole),
        scratch_shapes=[
            pltpu.SMEM(offsets.shape, jnp.int32),
            pltpu.SMEM(band_bins.shape, jnp.int32),
            pltpu.VMEM((1, channels), jnp.int32),
            pltpu.VMEM((padded, channels), BF16),
            pltpu.VMEM((2 * rows, channels), F32),
            pltpu.VMEM((2 * windows + 2, ROW_TILE // 2, channels), F32),
            pltpu.VMEM((ROW_TILE // 2, channels), F32),
            state, state, state, state, state,
            pltpu.VMEM((2 * rows, padded), BF16),
            pltpu.SemaphoreType.DMA((3,)),
            pltpu.SemaphoreType.DMA((pl.cdiv(padded, STEP),)),
        ],
        compiler_params=pltpu.CompilerParams(vmem_limit_bytes=60 * 2**20),
        cost_estimate=pl.CostEstimate(
            flops=2 * channels * block_len * 2 * rows,
            bytes_accessed=channels * block_len * 2,
            transcendentals=0,
        ),
        name="band_spectra",
    )(offsets, band_bins, dead.reshape(1, channels), samples, samples)


def whiten_kernel(bins, windows, firsts, own_ref, more_ref, *white_refs):
    rows = bins * windows * 2
    raw = own_ref[:rows, :] + more_ref[:rows, :].astype(F32)
    extra = more_ref[rows:, :].astype(F32)
    which = lax.broadcasted_iota(jnp.int32, (rows, 1), 0) % windows
    alive = own_ref[rows + windows:rows + windows + 1, :]
    scale = factor = None
    for w in range(windows):
        energy = own_ref[rows + w:rows + w + 1, :]
        for term in range(3):
            energy = energy + extra[term * windows + w:term * windows + w + 1, :]
        inverse = 1.0 / jnp.sqrt(energy / L + 1e-06)
        scale = inverse if w == 0 else jnp.where(which == w, inverse, scale)
    spectra = raw * scale
    power = spectra * spectra
    for w in range(windows):
        level = jnp.sum(jnp.where(which == w, power, 0.0), axis=0, keepdims=True) * (1.0 / bins)
        one = alive / jnp.sqrt(jnp.maximum(level, FLOOR))
        factor = one if w == 0 else jnp.where(which == w, one, factor)
    white = (spectra * factor).astype(BF16)
    for first, white_ref in zip(firsts, white_refs):
        copies, halves, count, width = white_ref.shape
        for h in range(halves):
            for copy in range(copies):
                white_ref[copy, h] = white[first:first + count, h * width:(h + 1) * width]


def whiten(own, more, bins, windows, halves, wanted):
    channels = own.shape[1]
    return pl.pallas_call(
        functools.partial(whiten_kernel, bins, windows, [first for _, first, _ in wanted]),
        out_shape=[
            jax.ShapeDtypeStruct((copies, halves, count, channels // halves), BF16)
            for copies, _, count in wanted
        ],
        compiler_params=pltpu.CompilerParams(vmem_limit_bytes=12 * 2**20),
        name="whiten",
    )(own, more)


def stack_kernel(windows, scale, devices, *refs):
    col_refs, row_refs = refs[:devices], refs[devices:2 * devices]
    out_hbm, lhs, held, made, sems = refs[2 * devices:]
    per_group = ROW_TILE // (2 * windows)
    step = pl.program_id(0)
    width = col_refs[0].shape[1]
    depth = devices * ROW_TILE
    halves, _, span = row_refs[0].shape
    channels = halves * span
    exact = math.frexp(scale)[0] == 0.5

    cols = jnp.stack([ref[...].astype(F32) for ref in col_refs])
    if exact:
        cols = cols * scale
    head, tail = cols[:, :ROW_TILE // 2], cols[:, ROW_TILE // 2:]
    straight = cols.reshape(depth, width)
    turned = jnp.concatenate([-tail, head], axis=1).reshape(depth, width)
    lhs[:width, :] = straight.T.astype(BF16)
    lhs[width:, :] = turned.T.astype(BF16)
    for away in range(devices):
        to = slice(away * ROW_TILE, (away + 1) * ROW_TILE)
        for h in range(halves):
            held[to, h * span:(h + 1) * span] = row_refs[away][h].astype(F32)

    def out_copy(slot, part, bin_index):
        to = out_hbm.at[part, bin_index]
        return pltpu.make_async_copy(made.at[slot], to, sems.at[slot])

    which = lax.broadcasted_iota(jnp.int32, (depth, 1), 0) % (ROW_TILE // 2) // windows
    for b in range(per_group):
        for part in range(2):
            slot = 2 * b + part

            @pl.when(step > 0)
            def _():
                out_copy(slot, part, (step - 1) * per_group + b).wait()

        for n in range(0, channels, DEPTH):
            at = slice(n, min(n + DEPTH, channels))
            rhs = jnp.where(which == b, held[:, at], 0.0).astype(BF16)
            for part in range(2):
                product = jnp.dot(
                    lhs[part * width:(part + 1) * width, :], rhs, preferred_element_type=F32
                )
                if not exact:
                    product = product * scale
                made[2 * b + part, :, at] = product.astype(BF16)
        for part in range(2):
            out_copy(2 * b + part, part, step * per_group + b).start()

    @pl.when(step == pl.num_programs(0) - 1)
    def _():
        for b in range(per_group):
            for part in range(2):
                out_copy(2 * b + part, part, step * per_group + b).wait()


def stacks_of(col_blocks, row_blocks, bins, windows):
    devices = len(row_blocks)
    halves, _, span = row_blocks[0].shape
    width = col_blocks[0].shape[1]
    per_group = ROW_TILE // (2 * windows)
    scale = 1.0 / math.sqrt(windows * devices)
    channels = halves * span
    return pl.pallas_call(
        functools.partial(stack_kernel, windows, scale, devices),
        out_shape=jax.ShapeDtypeStruct((2, bins, width, channels), BF16),
        grid=(bins // per_group,),
        in_specs=[pl.BlockSpec((ROW_TILE, width), lambda i: (i, 0))] * devices
        + [pl.BlockSpec((halves, ROW_TILE, span), lambda i: (0, i, 0))] * devices,
        out_specs=pl.BlockSpec(memory_space=pltpu.HBM),
        scratch_shapes=[
            pltpu.VMEM((2 * width, devices * ROW_TILE), BF16),
            pltpu.VMEM((devices * ROW_TILE, channels), F32),
            pltpu.VMEM((2 * per_group, width, channels), BF16),
            pltpu.SemaphoreType.DMA((2 * per_group,)),
        ],
        compiler_params=pltpu.CompilerParams(
            dimension_semantics=("arbitrary",), vmem_limit_bytes=24 * 2**20
        ),
        cost_estimate=pl.CostEstimate(
            flops=2 * 2 * bins * width * channels * devices * ROW_TILE,
            bytes_accessed=2 * bins * width * channels * 2,
            transcendentals=0,
        ),
        name="stack_products",
    )(*col_blocks, *row_blocks)


def pick_kernel(count, blocks_ref, *refs):
    tm = lax.axis_index("tm")
    for away, out_ref in enumerate(refs[-count:]):
        out_ref[...] = blocks_ref[jnp.bitwise_xor(tm, away)]


def picked(blocks, *others):
    count, rows, width = blocks.shape
    return pl.pallas_call(
        functools.partial(pick_kernel, count),
        out_shape=[jax.ShapeDtypeStruct((rows, width), blocks.dtype)] * count,
        in_specs=[pl.BlockSpec(memory_space=pltpu.VMEM)]
        + [pl.BlockSpec(memory_space=pl.ANY)] * len(others),
        out_specs=[pl.BlockSpec(memory_space=pltpu.VMEM)] * count,
        compiler_params=pltpu.CompilerParams(vmem_limit_bytes=8 * 2**20),
        name="pick_blocks",
    )(blocks, *others)


def exchanged(blocks, axis):
    return lax.all_to_all(blocks, axis, split_axis=0, concat_axis=0, tiled=True)


def from_partner(block, axis, away):
    return lax.ppermute(block, axis, [(i, i ^ away) for i in range(lax.axis_size(axis))])


def shards(recording, offsets, band_bins, dead_flags):
    channels, block_len = recording.shape
    windows = block_len // (L // 2)
    bins = band_bins.shape[0]
    chan_count, tm_count = lax.axis_size("chan"), lax.axis_size("tm")
    halves = tm_count // chan_count
    own, back = spectra_of(recording, offsets, band_bins, dead_flags, windows)
    more = shifted(back, "tm", -1)
    rows = bins * windows * 2
    white, for_chan = whiten(own, more, bins, windows, halves, [(1, 0, rows), (chan_count, 0, rows)])
    white = white[0]
    row_blocks = {0: white}
    for away in [*range(2, tm_count, 2), 1]:
        row_blocks[away] = from_partner(white, "tm", away)
    every_chan = exchanged(for_chan, "chan").reshape(tm_count, rows, channels // halves)
    col_blocks = list(picked(every_chan, *[row_blocks[away] for away in range(2, tm_count, 2)]))
    for away in range(1, tm_count):
        col_blocks[away] = from_partner(col_blocks[away], "tm", away)
    for away in range(2, tm_count, 2):
        row_blocks[away + 1] = from_partner(row_blocks[away], "tm", 1)
    return stacks_of(col_blocks, [row_blocks[i] for i in range(tm_count)], bins, windows)


def solution(mesh):
    placed = (P("chan", "tm"), P(), P(), P("chan"))
    return jax.shard_map(
        shards, mesh=mesh, in_specs=placed, out_specs=P(None, None, "tm", "chan"), check_vma=False
    )
```

```python
import functools
import math

import jax
import jax.numpy as jnp
from jax import lax
from jax.experimental import pallas as pl
from jax.experimental.pallas import tpu as pltpu
from jax.sharding import PartitionSpec as P

L = 15000
FLOOR = 0.7
F32 = jnp.float32
BF16 = jnp.bfloat16
LANE = 128
DEPTH = 256
STEP = 1024
ROW_TILE = 16


def cos_sin(turns, length):
    quarter = jnp.floor(turns * (4.0 / length) + 0.5)
    angle = (turns * 4.0 - quarter * length) * (math.pi / (2.0 * length))
    square = angle * angle
    sine = angle * (
        1.0 + square * (-1.0 / 6 + square * (1.0 / 120 + square * (-1.0 / 5040 + square * (1.0 / 362880))))
    )
    cosine = 1.0 + square * (
        -0.5 + square * (1.0 / 24 + square * (-1.0 / 720 + square * (1.0 / 40320)))
    )
    quadrant = quarter - 4.0 * jnp.floor(quarter * 0.25)
    odd = (quadrant == 1.0) | (quadrant == 3.0)
    cos_sign = jnp.where((quadrant == 1.0) | (quadrant == 2.0), -1.0, 1.0)
    sin_sign = jnp.where(quadrant >= 2.0, -1.0, 1.0)
    return cos_sign * jnp.where(odd, sine, cosine), sin_sign * jnp.where(odd, cosine, sine)


def spectra_kernel(
    bins, windows, block_len, low_end, high_end, sides,
    offsets_hbm, bins_hbm, dead_hbm, x_hbm, tail_ref, own_ref, *refs,
):
    back_ref = refs[0] if sides == 2 else None
    offsets, band_bins, dead, x_ref, acc, seg, part_seg, cos_now, sin_now, cos_turn, sin_turn, place, table = refs[-15:-2]
    small_sems, x_sems = refs[-2:]
    channels = x_ref.shape[1]
    length, hop = L, L // 2
    rows = bins * windows * 2
    half_tile = ROW_TILE // 2
    per_group = half_tile // windows
    groups = rows // ROW_TILE
    states = groups * half_tile
    bulk = (high_end - low_end) // ROW_TILE * ROW_TILE
    padded = x_ref.shape[0]
    steps = padded // STEP
    columns = [slice(n, min(n + DEPTH, channels)) for n in range(0, channels, DEPTH)]

    def x_copy(i):
        size = min(STEP, bulk - i * STEP)
        return pltpu.make_async_copy(
            x_hbm.at[pl.ds(low_end + i * STEP, size)], x_ref.at[pl.ds(i * STEP, size)], x_sems.at[i]
        )

    small = [
        pltpu.make_async_copy(offsets_hbm, offsets, small_sems.at[0]),
        pltpu.make_async_copy(bins_hbm, band_bins, small_sems.at[1]),
        pltpu.make_async_copy(dead_hbm, dead, small_sems.at[2]),
    ]
    for copy in small:
        copy.start()
    for copy in small:
        copy.wait()
    for i in range(pl.cdiv(bulk, STEP)):
        x_copy(i).start()

    tm = lax.axis_index("tm")
    ahead = [offsets[tm * windows + w] + w * hop for w in range(windows)]
    before = jnp.maximum(tm - 1, 0) * windows
    behind = [offsets[before + w] + w * hop + length - block_len for w in range(windows)]
    ends = []
    for w in range(windows if sides == 2 else 0):
        ends += [jnp.minimum(ahead[w], behind[w]), jnp.maximum(ahead[w], behind[w])]
    segments = len(ends) + 1
    trash = segments

    def make_table(index):
        moved = (index * DEPTH).astype(F32)
        to_lanes = pl.ds(pl.multiple_of(index * DEPTH, DEPTH), DEPTH)
        for side in range(sides):
            limit = moved if side else -moved
            for g in range(groups):
                at = slice(side * states + g * half_tile, side * states + (g + 1) * half_tile)
                to = side * rows + g * ROW_TILE
                c, s = cos_now[at, :], sin_now[at, :]
                inside = place[at, :] >= limit
                wave = jnp.concatenate([jnp.where(inside, c, 0.0), jnp.where(inside, s, 0.0)], axis=0)
                table[to:to + ROW_TILE, to_lanes] = wave.astype(BF16)
                ct, st = cos_turn[at, :], sin_turn[at, :]
                cos_now[at, :] = c * ct + s * st
                sin_now[at, :] = s * ct - c * st

    shape = (half_tile, DEPTH)
    row = lax.broadcasted_iota(jnp.int32, shape, 0)
    lane = (lax.broadcasted_iota(jnp.int32, shape, 1) + low_end).astype(F32)
    norm = 1.0 / math.sqrt(length)
    for side in range(sides):
        for g in range(groups):
            at = slice(side * states + g * half_tile, side * states + (g + 1) * half_tile)
            tone = jnp.zeros(shape, jnp.int32)
            start = jnp.zeros(shape, jnp.int32)
            for i in range(per_group):
                tone = jnp.where(row // windows == i, band_bins[g * per_group + i], tone)
            for w in range(windows):
                here = behind[w] - length if side else ahead[w]
                start = jnp.where(row % windows == w, here, start)
            tone, start = tone.astype(F32), start.astype(F32)
            cosine, sine = cos_sin((lane - start) * tone, length)
            cos_now[at, :] = cosine * norm
            sin_now[at, :] = -sine * norm
            cos_turn[at, :], sin_turn[at, :] = cos_sin(tone * DEPTH, length)
            place[at, :] = start + (length - 1) - lane if side else lane - start

    @pl.loop(0, padded // DEPTH)
    def _(index):
        make_table(index)

    acc[...] = jnp.zeros_like(acc)
    seg[...] = jnp.zeros_like(seg)
    if padded > bulk:
        x_ref[bulk:, :] = jnp.zeros((padded - bulk, channels), BF16)
    if high_end - low_end > bulk:
        inside = lax.broadcasted_iota(jnp.int32, (ROW_TILE, channels), 0) < high_end - low_end - bulk
        x_ref[bulk:bulk + ROW_TILE, :] = jnp.where(inside, tail_ref[...].astype(F32), 0.0).astype(BF16)

    def segment_of(position):
        index = jnp.int32(0)
        for end in ends:
            index += (end <= position).astype(jnp.int32)
        return index

    def has_end(first, size):
        found = jnp.bool_(False)
        for end in ends:
            found = jnp.logical_or(found, jnp.logical_and(end >= first, end < first + size))
        return found

    def body(base, size, edge):
        view = x_ref.at[pl.ds(base, size)]
        waves = table.at[:, pl.ds(base, size)]
        tiles = size // ROW_TILE

        def squares(t, at):
            x = view[t * ROW_TILE:(t + 1) * ROW_TILE, at].astype(F32)
            square = x * x
            return square[:half_tile] + square[half_tile:]

        for at in columns:
            if not edge:
                total = squares(0, at)
                for t in range(1, tiles):
                    total = total + squares(t, at)
            product = jnp.dot(waves[...], view[:, at], preferred_element_type=F32)
            acc[:, at] += product
            if not edge:
                part_seg[:, at] = total
        if edge:
            for t in range(tiles):
                first = base + t * ROW_TILE
                target = jnp.where(has_end(first, ROW_TILE), trash, segment_of(first))
                for at in columns:
                    seg[target, :, at] += squares(t, at)
        else:
            seg[segment_of(base)] += part_seg[...]

    @pl.loop(0, steps)
    def _(i):
        base = pl.multiple_of(i * STEP, STEP)
        pltpu.make_async_copy(
            x_hbm.at[pl.ds(low_end + base, STEP)], x_ref.at[pl.ds(base, STEP)], x_sems.at[i]
        ).wait()
        if not ends:
            body(base, STEP, False)
            return
        cut = has_end(base, STEP)

        @pl.when(jnp.logical_not(cut))
        def _():
            body(base, STEP, False)

        @pl.when(cut)
        def _():
            body(base, STEP, True)

    done = steps * STEP
    if done < padded:
        if done < bulk:
            x_copy(steps).wait()
        body(done, padded - done, False)

    for i, end in enumerate(ends):
        low = ends[i - 1] if i else jnp.int32(0)
        high = ends[i + 1] if i + 1 < len(ends) else jnp.int32(high_end)
        tile = end // ROW_TILE
        x = x_ref[pl.ds(pl.multiple_of(tile * ROW_TILE, ROW_TILE), ROW_TILE), :].astype(F32)
        spot = lax.broadcasted_iota(jnp.int32, x.shape, 0) + tile * ROW_TILE
        under = jnp.logical_and(spot >= low, spot < end)
        over = jnp.logical_and(spot >= end, spot < high)
        over = jnp.logical_and(over, high // ROW_TILE != tile)
        square = x * x
        for where, index in ((under, i), (over, i + 1)):
            kept = jnp.where(where, square, 0.0)
            seg[index] += kept[:half_tile] + kept[half_tile:]

    own_ref[:rows, :] = acc[:rows, :]
    parts = [seg[i] for i in range(segments)]
    row = lax.broadcasted_iota(jnp.int32, (half_tile, channels), 0)
    own_block = jnp.where(row == windows, (1 - dead[...]).astype(F32), 0.0)
    for w in range(windows):
        after = sum(parts[2 * w + 2:]) if ends else parts[0]
        if ends:
            after = after + jnp.where(ahead[w] <= behind[w], parts[2 * w + 1], 0.0)
        own_block = jnp.where(row == w, jnp.sum(after, axis=0, keepdims=True), own_block)
    own_ref[rows:, :] = own_block
    if sides == 1:
        return
    back_ref[:rows, :] = acc[rows:, :].astype(BF16)
    back_block = jnp.zeros((ROW_TILE, channels), F32)
    back_row = lax.broadcasted_iota(jnp.int32, (ROW_TILE, channels), 0)
    for w in range(windows):
        until = sum(parts[:2 * w + 1]) + jnp.where(ahead[w] <= behind[w], parts[2 * w + 1], 0.0)
        rest = jnp.sum(until, axis=0, keepdims=True)
        for term in range(3):
            piece_of = rest.astype(BF16).astype(F32)
            rest = rest - piece_of
            back_block = jnp.where(back_row == term * windows + w, piece_of, back_block)
    back_ref[rows:, :] = back_block.astype(BF16)


def spectra_of(recording, offsets, band_bins, dead, windows, low_end, high_end, sides):
    channels, block_len = recording.shape
    bins = band_bins.shape[0]
    rows = bins * windows * 2
    padded = pl.cdiv(high_end - low_end, DEPTH) * DEPTH
    bulk = (high_end - low_end) // ROW_TILE * ROW_TILE
    tail = min(low_end + bulk, block_len - 1) // ROW_TILE
    samples = recording.T
    hbm = pl.BlockSpec(memory_space=pltpu.HBM)
    whole = pl.BlockSpec(memory_space=pltpu.VMEM)
    state = pltpu.VMEM((rows // 2 * sides, DEPTH), F32)
    out_shape = [
        jax.ShapeDtypeStruct((rows + ROW_TILE // 2, channels), F32),
        jax.ShapeDtypeStruct((rows + ROW_TILE, channels), BF16),
    ][:sides]
    return pl.pallas_call(
        functools.partial(spectra_kernel, bins, windows, block_len, low_end, high_end, sides),
        out_shape=out_shape,
        grid=(1,),
        in_specs=[
            hbm, hbm, hbm, hbm,
            pl.BlockSpec((ROW_TILE, channels), lambda i: (tail, 0)),
        ],
        out_specs=[whole] * sides,
        scratch_shapes=[
            pltpu.SMEM(offsets.shape, jnp.int32),
            pltpu.SMEM(band_bins.shape, jnp.int32),
            pltpu.VMEM((1, channels), jnp.int32),
            pltpu.VMEM((padded, channels), BF16),
            pltpu.VMEM((sides * rows, channels), F32),
            pltpu.VMEM((2 * windows + 2, ROW_TILE // 2, channels), F32),
            pltpu.VMEM((ROW_TILE // 2, channels), F32),
            state, state, state, state, state,
            pltpu.VMEM((sides * rows, padded), BF16),
            pltpu.SemaphoreType.DMA((3,)),
            pltpu.SemaphoreType.DMA((pl.cdiv(padded, STEP),)),
        ],
        compiler_params=pltpu.CompilerParams(vmem_limit_bytes=60 * 2**20),
        cost_estimate=pl.CostEstimate(
            flops=2 * channels * (high_end - low_end) * sides * rows,
            bytes_accessed=channels * (high_end - low_end) * 2,
            transcendentals=0,
        ),
        name="band_spectra" if sides == 2 else "band_spectra_rest",
    )(offsets, band_bins, dead.reshape(1, channels), samples, samples)


def whiten_kernel(bins, windows, own_ref, rest_ref, more_ref, white_ref):
    rows = bins * windows * 2
    raw = own_ref[:rows, :] + rest_ref[:rows, :] + more_ref[:rows, :].astype(F32)
    extra = more_ref[rows:, :].astype(F32)
    which = lax.broadcasted_iota(jnp.int32, (rows, 1), 0) % windows
    alive = own_ref[rows + windows:rows + windows + 1, :]
    scale = factor = None
    for w in range(windows):
        energy = own_ref[rows + w:rows + w + 1, :] + rest_ref[rows + w:rows + w + 1, :]
        for term in range(3):
            energy = energy + extra[term * windows + w:term * windows + w + 1, :]
        inverse = 1.0 / jnp.sqrt(energy / L + 1e-06)
        scale = inverse if w == 0 else jnp.where(which == w, inverse, scale)
    spectra = raw * scale
    power = spectra * spectra
    for w in range(windows):
        level = jnp.sum(jnp.where(which == w, power, 0.0), axis=0, keepdims=True) * (1.0 / bins)
        one = alive / jnp.sqrt(jnp.maximum(level, FLOOR))
        factor = one if w == 0 else jnp.where(which == w, one, factor)
    white = (spectra * factor).astype(BF16)
    width = white_ref.shape[2]
    for h in range(white_ref.shape[0]):
        white_ref[h] = white[:, h * width:(h + 1) * width]


def whiten(own, rest, more, bins, windows, halves):
    channels = own.shape[1]
    return pl.pallas_call(
        functools.partial(whiten_kernel, bins, windows),
        out_shape=jax.ShapeDtypeStruct((halves, bins * windows * 2, channels // halves), BF16),
        compiler_params=pltpu.CompilerParams(vmem_limit_bytes=12 * 2**20),
        name="whiten",
    )(own, rest, more)


def stack_kernel(windows, scale, devices, *refs):
    col_refs, row_refs = refs[:devices], refs[devices:devices + 2]
    out_hbm, lhs, held, made, sems = refs[devices + 2:]
    per_group = ROW_TILE // (2 * windows)
    step = pl.program_id(0)
    width = col_refs[0].shape[1]
    depth = devices * ROW_TILE
    _, halves, _, span = row_refs[0].shape
    channels = halves * span
    exact = math.frexp(scale)[0] == 0.5

    cols = jnp.stack([ref[...].astype(F32) for ref in col_refs])
    if exact:
        cols = cols * scale
    head, tail = cols[:, :ROW_TILE // 2], cols[:, ROW_TILE // 2:]
    straight = cols.reshape(depth, width)
    turned = jnp.concatenate([-tail, head], axis=1).reshape(depth, width)
    lhs[:width, :] = straight.T.astype(BF16)
    lhs[width:, :] = turned.T.astype(BF16)
    for away in range(devices):
        to = slice(away * ROW_TILE, (away + 1) * ROW_TILE)
        for h in range(halves):
            held[to, h * span:(h + 1) * span] = row_refs[away % 2][away // 2, h].astype(F32)

    def out_copy(slot, part, bin_index):
        to = out_hbm.at[part, bin_index]
        return pltpu.make_async_copy(made.at[slot], to, sems.at[slot])

    which = lax.broadcasted_iota(jnp.int32, (depth, 1), 0) % (ROW_TILE // 2) // windows
    for b in range(per_group):
        for part in range(2):
            slot = 2 * b + part

            @pl.when(step > 0)
            def _():
                out_copy(slot, part, (step - 1) * per_group + b).wait()

        for n in range(0, channels, DEPTH):
            at = slice(n, min(n + DEPTH, channels))
            rhs = jnp.where(which == b, held[:, at], 0.0).astype(BF16)
            for part in range(2):
                product = jnp.dot(
                    lhs[part * width:(part + 1) * width, :], rhs, preferred_element_type=F32
                )
                if not exact:
                    product = product * scale
                made[2 * b + part, :, at] = product.astype(BF16)
        for part in range(2):
            out_copy(2 * b + part, part, step * per_group + b).start()

    @pl.when(step == pl.num_programs(0) - 1)
    def _():
        for b in range(per_group):
            for part in range(2):
                out_copy(2 * b + part, part, step * per_group + b).wait()


def stacks_of(col_blocks, row_blocks, bins, windows):
    devices = len(col_blocks)
    chips, halves, _, span = row_blocks[0].shape
    width = col_blocks[0].shape[1]
    per_group = ROW_TILE // (2 * windows)
    scale = 1.0 / math.sqrt(windows * devices)
    channels = halves * span
    return pl.pallas_call(
        functools.partial(stack_kernel, windows, scale, devices),
        out_shape=jax.ShapeDtypeStruct((2, bins, width, channels), BF16),
        grid=(bins // per_group,),
        in_specs=[pl.BlockSpec((ROW_TILE, width), lambda i: (i, 0))] * devices
        + [pl.BlockSpec((chips, halves, ROW_TILE, span), lambda i: (0, 0, i, 0))] * 2,
        out_specs=pl.BlockSpec(memory_space=pltpu.HBM),
        scratch_shapes=[
            pltpu.VMEM((2 * width, devices * ROW_TILE), BF16),
            pltpu.VMEM((devices * ROW_TILE, channels), F32),
            pltpu.VMEM((2 * per_group, width, channels), BF16),
            pltpu.SemaphoreType.DMA((2 * per_group,)),
        ],
        compiler_params=pltpu.CompilerParams(
            dimension_semantics=("arbitrary",), vmem_limit_bytes=24 * 2**20
        ),
        cost_estimate=pl.CostEstimate(
            flops=2 * 2 * bins * width * channels * devices * ROW_TILE,
            bytes_accessed=2 * bins * width * channels * 2,
            transcendentals=0,
        ),
        name="stack_products",
    )(*col_blocks, *row_blocks)


def pick_kernel(count, reach, row_count, *refs):
    chan_refs, row_refs = refs[:len(reach)], refs[len(reach):len(reach) + row_count]
    joined_ref, out_refs, held = refs[len(reach) + row_count], refs[-1 - count:-1], refs[-1]
    tm, mine = lax.axis_index("tm"), lax.axis_index("chan")
    size = held.shape[0]
    halves = chan_refs[0].shape[0]
    for far, ref in zip(reach, chan_refs):
        @pl.when(jnp.logical_and(mine + far >= 0, mine + far < size))
        def _():
            held[mine + far] = ref[...]
    for i, ref in enumerate(row_refs):
        joined_ref[i] = ref[...]
    for away, out_ref in enumerate(out_refs):
        wanted = jnp.bitwise_xor(tm, away)
        out_ref[...] = held[wanted // halves, wanted % halves]


def picked(blocks, row_blocks, count, chan_count):
    reach = list(blocks)
    block = blocks[0]
    _, rows, width = block.shape
    whole = pl.BlockSpec(memory_space=pltpu.VMEM)
    joined, *picks = pl.pallas_call(
        functools.partial(pick_kernel, count, reach, len(row_blocks)),
        out_shape=[jax.ShapeDtypeStruct((len(row_blocks), *block.shape), block.dtype)]
        + [jax.ShapeDtypeStruct((rows, width), block.dtype)] * count,
        in_specs=[whole] * (len(blocks) + len(row_blocks)),
        out_specs=[whole] * (1 + count),
        scratch_shapes=[pltpu.VMEM((chan_count, *block.shape), block.dtype)],
        compiler_params=pltpu.CompilerParams(vmem_limit_bytes=16 * 2**20),
        name="pick_blocks",
    )(*blocks.values(), *row_blocks)
    return joined, picks


def moved(block, axis, far):
    count = lax.axis_size(axis)
    return lax.ppermute(block, axis, [(i + far, i) for i in range(count) if 0 <= i + far < count])


def chan_blocks(block):
    blocks = {0: block}
    for far in range(1, lax.axis_size("chan")):
        for sign in (-1, 1):
            if far < 3:
                blocks[sign * far] = moved(block, "chan", sign * far)
            else:
                blocks[sign * far] = moved(blocks[sign * (far - 1)], "chan", sign)
    return blocks


def from_partner(block, axis, away):
    return lax.ppermute(block, axis, [(i, i ^ away) for i in range(lax.axis_size(axis))])


def shards(recording, offsets, band_bins, dead_flags):
    channels, block_len = recording.shape
    windows = block_len // (L // 2)
    bins = band_bins.shape[0]
    chan_count, tm_count = lax.axis_size("chan"), lax.axis_size("tm")
    halves = tm_count // chan_count
    rim = L // 2 + L // 4
    cut = min(pl.cdiv(rim, STEP) * STEP, block_len)
    own, back = spectra_of(recording, offsets, band_bins, dead_flags, windows, 0, cut, 2)
    more = moved(back, "tm", 1)
    rest, = spectra_of(recording, offsets, band_bins, dead_flags, windows, cut, block_len, 1)
    white = whiten(own, rest, more, bins, windows, halves)
    blocks = chan_blocks(white)
    row_blocks = [white] + [from_partner(white, "tm", away) for away in range(2, tm_count, 2)]
    joined, col_blocks = picked(blocks, row_blocks, tm_count, chan_count)
    for away in range(1, tm_count):
        col_blocks[away] = from_partner(col_blocks[away], "tm", away)
    return stacks_of(col_blocks, [joined, from_partner(joined, "tm", 1)], bins, windows)


def solution(mesh):
    placed = (P("chan", "tm"), P(), P(), P("chan"))
    return jax.shard_map(
        shards, mesh=mesh, in_specs=placed, out_specs=P(None, None, "tm", "chan"), check_vma=False
    )
```

```python
import functools
import math

import jax
import jax.numpy as jnp
from jax import lax
from jax.experimental import pallas as pl
from jax.experimental.pallas import tpu as pltpu
from jax.sharding import PartitionSpec as P

L = 15000
FLOOR = 0.7
F32 = jnp.float32
BF16 = jnp.bfloat16
LANE = 128
DEPTH = 256
STEP = 1024
ROW_TILE = 16


def cos_sin(turns, length):
    quarter = jnp.floor(turns * (4.0 / length) + 0.5)
    angle = (turns * 4.0 - quarter * length) * (math.pi / (2.0 * length))
    square = angle * angle
    sine = angle * (
        1.0 + square * (-1.0 / 6 + square * (1.0 / 120 + square * (-1.0 / 5040 + square * (1.0 / 362880))))
    )
    cosine = 1.0 + square * (
        -0.5 + square * (1.0 / 24 + square * (-1.0 / 720 + square * (1.0 / 40320)))
    )
    quadrant = quarter - 4.0 * jnp.floor(quarter * 0.25)
    odd = (quadrant == 1.0) | (quadrant == 3.0)
    cos_sign = jnp.where((quadrant == 1.0) | (quadrant == 2.0), -1.0, 1.0)
    sin_sign = jnp.where(quadrant >= 2.0, -1.0, 1.0)
    return cos_sign * jnp.where(odd, sine, cosine), sin_sign * jnp.where(odd, cosine, sine)


def spectra_kernel(
    bins, windows, block_len, low_end, high_end, sides,
    offsets_hbm, bins_hbm, dead_hbm, x_hbm, tail_ref, own_ref, *refs,
):
    back_ref = refs[0] if sides == 2 else None
    offsets, band_bins, dead, x_ref, acc, seg, part_seg, cos_now, sin_now, cos_turn, sin_turn, place, table = refs[-15:-2]
    small_sems, x_sems = refs[-2:]
    channels = x_ref.shape[1]
    length, hop = L, L // 2
    rows = bins * windows * 2
    half_tile = ROW_TILE // 2
    per_group = half_tile // windows
    groups = rows // ROW_TILE
    states = groups * half_tile
    bulk = (high_end - low_end) // ROW_TILE * ROW_TILE
    padded = x_ref.shape[0]
    steps = padded // STEP
    columns = [slice(n, min(n + DEPTH, channels)) for n in range(0, channels, DEPTH)]

    def x_copy(i):
        size = min(STEP, bulk - i * STEP)
        return pltpu.make_async_copy(
            x_hbm.at[pl.ds(low_end + i * STEP, size)], x_ref.at[pl.ds(i * STEP, size)], x_sems.at[i]
        )

    small = [
        pltpu.make_async_copy(offsets_hbm, offsets, small_sems.at[0]),
        pltpu.make_async_copy(bins_hbm, band_bins, small_sems.at[1]),
        pltpu.make_async_copy(dead_hbm, dead, small_sems.at[2]),
    ]
    for copy in small:
        copy.start()
    x_copy(0).start()
    for copy in small:
        copy.wait()
    for i in range(1, pl.cdiv(bulk, STEP)):
        x_copy(i).start()

    tm = lax.axis_index("tm")
    ahead = [offsets[tm * windows + w] + w * hop for w in range(windows)]
    before = jnp.maximum(tm - 1, 0) * windows
    behind = [offsets[before + w] + w * hop + length - block_len for w in range(windows)]
    ends = []
    for w in range(windows if sides == 2 else 0):
        ends += [jnp.minimum(ahead[w], behind[w]), jnp.maximum(ahead[w], behind[w])]
    segments = len(ends) + 1
    trash = segments

    def make_table(index):
        moved = (index * DEPTH).astype(F32)
        to_lanes = pl.ds(pl.multiple_of(index * DEPTH, DEPTH), DEPTH)
        for side in range(sides):
            limit = moved if side else -moved
            for g in range(groups):
                at = slice(side * states + g * half_tile, side * states + (g + 1) * half_tile)
                to = side * rows + g * ROW_TILE
                c, s = cos_now[at, :], sin_now[at, :]
                inside = place[at, :] >= limit
                wave = jnp.concatenate([jnp.where(inside, c, 0.0), jnp.where(inside, s, 0.0)], axis=0)
                table[to:to + ROW_TILE, to_lanes] = wave.astype(BF16)
                ct, st = cos_turn[at, :], sin_turn[at, :]
                cos_now[at, :] = c * ct + s * st
                sin_now[at, :] = s * ct - c * st

    shape = (half_tile, DEPTH)
    row = lax.broadcasted_iota(jnp.int32, shape, 0)
    lane = (lax.broadcasted_iota(jnp.int32, shape, 1) + low_end).astype(F32)
    norm = 1.0 / math.sqrt(length)
    for side in range(sides):
        for g in range(groups):
            at = slice(side * states + g * half_tile, side * states + (g + 1) * half_tile)
            tone = jnp.zeros(shape, jnp.int32)
            start = jnp.zeros(shape, jnp.int32)
            for i in range(per_group):
                tone = jnp.where(row // windows == i, band_bins[g * per_group + i], tone)
            for w in range(windows):
                here = behind[w] - length if side else ahead[w]
                start = jnp.where(row % windows == w, here, start)
            tone, start = tone.astype(F32), start.astype(F32)
            cosine, sine = cos_sin((lane - start) * tone, length)
            cos_now[at, :] = cosine * norm
            sin_now[at, :] = -sine * norm
            cos_turn[at, :], sin_turn[at, :] = cos_sin(tone * DEPTH, length)
            place[at, :] = start + (length - 1) - lane if side else lane - start

    @pl.loop(0, padded // DEPTH)
    def _(index):
        make_table(index)

    acc[...] = jnp.zeros_like(acc)
    seg[...] = jnp.zeros_like(seg)
    if padded > bulk:
        x_ref[bulk:, :] = jnp.zeros((padded - bulk, channels), BF16)
    if high_end - low_end > bulk:
        inside = lax.broadcasted_iota(jnp.int32, (ROW_TILE, channels), 0) < high_end - low_end - bulk
        x_ref[bulk:bulk + ROW_TILE, :] = jnp.where(inside, tail_ref[...].astype(F32), 0.0).astype(BF16)

    def segment_of(position):
        index = jnp.int32(0)
        for end in ends:
            index += (end <= position).astype(jnp.int32)
        return index

    def has_end(first, size):
        found = jnp.bool_(False)
        for end in ends:
            found = jnp.logical_or(found, jnp.logical_and(end >= first, end < first + size))
        return found

    def body(base, size, edge):
        view = x_ref.at[pl.ds(base, size)]
        waves = table.at[:, pl.ds(base, size)]
        tiles = size // ROW_TILE

        def squares(t, at):
            x = view[t * ROW_TILE:(t + 1) * ROW_TILE, at].astype(F32)
            square = x * x
            return square[:half_tile] + square[half_tile:]

        for at in columns:
            if not edge:
                total = squares(0, at)
                for t in range(1, tiles):
                    total = total + squares(t, at)
            product = jnp.dot(waves[...], view[:, at], preferred_element_type=F32)
            acc[:, at] += product
            if not edge:
                part_seg[:, at] = total
        if edge:
            for t in range(tiles):
                first = base + t * ROW_TILE
                target = jnp.where(has_end(first, ROW_TILE), trash, segment_of(first))
                for at in columns:
                    seg[target, :, at] += squares(t, at)
        else:
            seg[segment_of(base)] += part_seg[...]

    @pl.loop(0, steps)
    def _(i):
        base = pl.multiple_of(i * STEP, STEP)
        pltpu.make_async_copy(
            x_hbm.at[pl.ds(low_end + base, STEP)], x_ref.at[pl.ds(base, STEP)], x_sems.at[i]
        ).wait()
        if not ends:
            body(base, STEP, False)
            return
        cut = has_end(base, STEP)

        @pl.when(jnp.logical_not(cut))
        def _():
            body(base, STEP, False)

        @pl.when(cut)
        def _():
            body(base, STEP, True)

    done = steps * STEP
    if done < padded:
        if done < bulk:
            x_copy(steps).wait()
        body(done, padded - done, False)

    for i, end in enumerate(ends):
        low = ends[i - 1] if i else jnp.int32(0)
        high = ends[i + 1] if i + 1 < len(ends) else jnp.int32(high_end)
        tile = end // ROW_TILE
        x = x_ref[pl.ds(pl.multiple_of(tile * ROW_TILE, ROW_TILE), ROW_TILE), :].astype(F32)
        spot = lax.broadcasted_iota(jnp.int32, x.shape, 0) + tile * ROW_TILE
        under = jnp.logical_and(spot >= low, spot < end)
        over = jnp.logical_and(spot >= end, spot < high)
        over = jnp.logical_and(over, high // ROW_TILE != tile)
        square = x * x
        for where, index in ((under, i), (over, i + 1)):
            kept = jnp.where(where, square, 0.0)
            seg[index] += kept[:half_tile] + kept[half_tile:]

    own_ref[:rows, :] = acc[:rows, :]
    parts = [seg[i] for i in range(segments)]
    row = lax.broadcasted_iota(jnp.int32, (half_tile, channels), 0)
    own_block = jnp.where(row == windows, (1 - dead[...]).astype(F32), 0.0)
    for w in range(windows):
        after = sum(parts[2 * w + 2:]) if ends else parts[0]
        if ends:
            after = after + jnp.where(ahead[w] <= behind[w], parts[2 * w + 1], 0.0)
        own_block = jnp.where(row == w, jnp.sum(after, axis=0, keepdims=True), own_block)
    own_ref[rows:, :] = own_block
    if sides == 1:
        return
    back_ref[:rows, :] = acc[rows:, :].astype(BF16)
    back_block = jnp.zeros((ROW_TILE, channels), F32)
    back_row = lax.broadcasted_iota(jnp.int32, (ROW_TILE, channels), 0)
    for w in range(windows):
        until = sum(parts[:2 * w + 1]) + jnp.where(ahead[w] <= behind[w], parts[2 * w + 1], 0.0)
        rest = jnp.sum(until, axis=0, keepdims=True)
        for term in range(3):
            piece_of = rest.astype(BF16).astype(F32)
            rest = rest - piece_of
            back_block = jnp.where(back_row == term * windows + w, piece_of, back_block)
    back_ref[rows:, :] = back_block.astype(BF16)


def spectra_of(recording, offsets, band_bins, dead, windows, low_end, high_end, sides):
    channels, block_len = recording.shape
    bins = band_bins.shape[0]
    rows = bins * windows * 2
    padded = pl.cdiv(high_end - low_end, DEPTH) * DEPTH
    bulk = (high_end - low_end) // ROW_TILE * ROW_TILE
    tail = min(low_end + bulk, block_len - 1) // ROW_TILE
    samples = recording.T
    hbm = pl.BlockSpec(memory_space=pltpu.HBM)
    whole = pl.BlockSpec(memory_space=pltpu.VMEM)
    state = pltpu.VMEM((rows // 2 * sides, DEPTH), F32)
    out_shape = [
        jax.ShapeDtypeStruct((rows + ROW_TILE // 2, channels), F32),
        jax.ShapeDtypeStruct((rows + ROW_TILE, channels), BF16),
    ][:sides]
    return pl.pallas_call(
        functools.partial(spectra_kernel, bins, windows, block_len, low_end, high_end, sides),
        out_shape=out_shape,
        grid=(1,),
        in_specs=[
            hbm, hbm, hbm, hbm,
            pl.BlockSpec((ROW_TILE, channels), lambda i: (tail, 0)),
        ],
        out_specs=[whole] * sides,
        scratch_shapes=[
            pltpu.SMEM(offsets.shape, jnp.int32),
            pltpu.SMEM(band_bins.shape, jnp.int32),
            pltpu.VMEM((1, channels), jnp.int32),
            pltpu.VMEM((padded, channels), BF16),
            pltpu.VMEM((sides * rows, channels), F32),
            pltpu.VMEM((2 * windows + 2, ROW_TILE // 2, channels), F32),
            pltpu.VMEM((ROW_TILE // 2, channels), F32),
            state, state, state, state, state,
            pltpu.VMEM((sides * rows, padded), BF16),
            pltpu.SemaphoreType.DMA((3,)),
            pltpu.SemaphoreType.DMA((pl.cdiv(padded, STEP),)),
        ],
        compiler_params=pltpu.CompilerParams(vmem_limit_bytes=60 * 2**20),
        cost_estimate=pl.CostEstimate(
            flops=2 * channels * (high_end - low_end) * sides * rows,
            bytes_accessed=channels * (high_end - low_end) * 2,
            transcendentals=0,
        ),
        name="band_spectra" if sides == 2 else "band_spectra_rest",
    )(offsets, band_bins, dead.reshape(1, channels), samples, samples)


def whiten_kernel(bins, windows, own_ref, rest_ref, more_ref, white_ref):
    rows = bins * windows * 2
    raw = own_ref[:rows, :] + rest_ref[:rows, :] + more_ref[:rows, :].astype(F32)
    extra = more_ref[rows:, :].astype(F32)
    which = lax.broadcasted_iota(jnp.int32, (rows, 1), 0) % windows
    alive = own_ref[rows + windows:rows + windows + 1, :]
    scale = factor = None
    for w in range(windows):
        energy = own_ref[rows + w:rows + w + 1, :] + rest_ref[rows + w:rows + w + 1, :]
        for term in range(3):
            energy = energy + extra[term * windows + w:term * windows + w + 1, :]
        inverse = 1.0 / jnp.sqrt(energy / L + 1e-06)
        scale = inverse if w == 0 else jnp.where(which == w, inverse, scale)
    spectra = raw * scale
    power = spectra * spectra
    for w in range(windows):
        level = jnp.sum(jnp.where(which == w, power, 0.0), axis=0, keepdims=True) * (1.0 / bins)
        one = alive / jnp.sqrt(jnp.maximum(level, FLOOR))
        factor = one if w == 0 else jnp.where(which == w, one, factor)
    white = (spectra * factor).astype(BF16)
    width = white_ref.shape[2]
    for h in range(white_ref.shape[0]):
        white_ref[h] = white[:, h * width:(h + 1) * width]


def whiten(own, rest, more, bins, windows, halves):
    channels = own.shape[1]
    return pl.pallas_call(
        functools.partial(whiten_kernel, bins, windows),
        out_shape=jax.ShapeDtypeStruct((halves, bins * windows * 2, channels // halves), BF16),
        compiler_params=pltpu.CompilerParams(vmem_limit_bytes=12 * 2**20),
        name="whiten",
    )(own, rest, more)


def stack_kernel(windows, scale, devices, *refs):
    col_refs, row_refs = refs[:devices], refs[devices:devices + 2]
    out_hbm, lhs, held, made, sems = refs[devices + 2:]
    per_group = ROW_TILE // (2 * windows)
    step = pl.program_id(0)
    width = col_refs[0].shape[1]
    depth = devices * ROW_TILE
    _, halves, _, span = row_refs[0].shape
    channels = halves * span
    exact = math.frexp(scale)[0] == 0.5

    by_partner = dict(zip([0, *partners(devices)], col_refs))
    cols = jnp.stack([by_partner[away][...].astype(F32) for away in range(devices)])
    if exact:
        cols = cols * scale
    head, tail = cols[:, :ROW_TILE // 2], cols[:, ROW_TILE // 2:]
    straight = cols.reshape(depth, width)
    turned = jnp.concatenate([-tail, head], axis=1).reshape(depth, width)
    lhs[:width, :] = straight.T.astype(BF16)
    lhs[width:, :] = turned.T.astype(BF16)
    for away in range(devices):
        to = slice(away * ROW_TILE, (away + 1) * ROW_TILE)
        for h in range(halves):
            held[to, h * span:(h + 1) * span] = row_refs[away % 2][away // 2, h].astype(F32)

    def out_copy(slot, part, bin_index):
        to = out_hbm.at[part, bin_index]
        return pltpu.make_async_copy(made.at[slot], to, sems.at[slot])

    which = lax.broadcasted_iota(jnp.int32, (depth, 1), 0) % (ROW_TILE // 2) // windows
    for b in range(per_group):
        for part in range(2):
            slot = 2 * b + part

            @pl.when(step > 0)
            def _():
                out_copy(slot, part, (step - 1) * per_group + b).wait()

        for n in range(0, channels, DEPTH):
            at = slice(n, min(n + DEPTH, channels))
            rhs = jnp.where(which == b, held[:, at], 0.0).astype(BF16)
            for part in range(2):
                product = jnp.dot(
                    lhs[part * width:(part + 1) * width, :], rhs, preferred_element_type=F32
                )
                if not exact:
                    product = product * scale
                made[2 * b + part, :, at] = product.astype(BF16)
        for part in range(2):
            out_copy(2 * b + part, part, step * per_group + b).start()

    @pl.when(step == pl.num_programs(0) - 1)
    def _():
        for b in range(per_group):
            for part in range(2):
                out_copy(2 * b + part, part, step * per_group + b).wait()


def stacks_of(col_blocks, row_blocks, bins, windows):
    devices = len(col_blocks)
    chips, halves, _, span = row_blocks[0].shape
    width = col_blocks[0].shape[1]
    per_group = ROW_TILE // (2 * windows)
    scale = 1.0 / math.sqrt(windows * devices)
    channels = halves * span
    return pl.pallas_call(
        functools.partial(stack_kernel, windows, scale, devices),
        out_shape=jax.ShapeDtypeStruct((2, bins, width, channels), BF16),
        grid=(bins // per_group,),
        in_specs=[pl.BlockSpec((ROW_TILE, width), lambda i: (i, 0))] * devices
        + [pl.BlockSpec((chips, halves, ROW_TILE, span), lambda i: (0, 0, i, 0))] * 2,
        out_specs=pl.BlockSpec(memory_space=pltpu.HBM),
        scratch_shapes=[
            pltpu.VMEM((2 * width, devices * ROW_TILE), BF16),
            pltpu.VMEM((devices * ROW_TILE, channels), F32),
            pltpu.VMEM((2 * per_group, width, channels), BF16),
            pltpu.SemaphoreType.DMA((2 * per_group,)),
        ],
        compiler_params=pltpu.CompilerParams(
            dimension_semantics=("arbitrary",), vmem_limit_bytes=24 * 2**20
        ),
        cost_estimate=pl.CostEstimate(
            flops=2 * 2 * bins * width * channels * devices * ROW_TILE,
            bytes_accessed=2 * bins * width * channels * 2,
            transcendentals=0,
        ),
        name="stack_products",
    )(*[col_blocks[away] for away in [0, *partners(devices)]], *row_blocks)


def pick_kernel(count, chips, *refs):
    row_refs, chan_refs = refs[:chips], refs[chips:-2 - count]
    joined_ref, out_refs, held = refs[-2 - count], refs[-1 - count:-1], refs[-1]
    tm, mine = lax.axis_index("tm"), lax.axis_index("chan")
    halves = row_refs[0].shape[0]
    for i, ref in enumerate(row_refs):
        joined_ref[i] = ref[...]
    for away, ref in enumerate((row_refs[0], *chan_refs)):
        held[jnp.bitwise_xor(mine, away)] = ref[...]
    for away, out_ref in enumerate(out_refs):
        wanted = jnp.bitwise_xor(tm, away)
        out_ref[...] = held[wanted // halves, wanted % halves]


def picked(row_blocks, chan_blocks, count):
    block = row_blocks[0]
    _, rows, width = block.shape
    chips = len(row_blocks)
    whole = pl.BlockSpec(memory_space=pltpu.VMEM)
    joined, *picks = pl.pallas_call(
        functools.partial(pick_kernel, count, chips),
        out_shape=[jax.ShapeDtypeStruct((chips, *block.shape), block.dtype)]
        + [jax.ShapeDtypeStruct((rows, width), block.dtype)] * count,
        in_specs=[whole] * (chips + len(chan_blocks)),
        out_specs=[whole] * (1 + count),
        scratch_shapes=[pltpu.VMEM((1 + len(chan_blocks), *block.shape), block.dtype)],
        compiler_params=pltpu.CompilerParams(vmem_limit_bytes=16 * 2**20),
        name="pick_blocks",
    )(*row_blocks, *chan_blocks)
    return joined, picks


def moved(block, axis, far):
    count = lax.axis_size(axis)
    return lax.ppermute(block, axis, [(i + far, i) for i in range(count) if 0 <= i + far < count])


def partners(count):
    return [*range(2, count, 2), *range(3, count, 2), 1]


def from_partner(block, axis, away):
    return lax.ppermute(block, axis, [(i, i ^ away) for i in range(lax.axis_size(axis))])


def shards(recording, offsets, band_bins, dead_flags):
    channels, block_len = recording.shape
    windows = block_len // (L // 2)
    bins = band_bins.shape[0]
    chan_count, tm_count = lax.axis_size("chan"), lax.axis_size("tm")
    halves = tm_count // chan_count
    rim = L // 2 + L // 4
    cut = min(pl.cdiv(rim, STEP) * STEP, block_len)
    own, back = spectra_of(recording, offsets, band_bins, dead_flags, windows, 0, cut, 2)
    more = moved(back, "tm", 1)
    rest, = spectra_of(recording, offsets, band_bins, dead_flags, windows, cut, block_len, 1)
    white = whiten(own, rest, more, bins, windows, halves)
    row_blocks = [white] + [from_partner(white, "tm", away) for away in range(2, tm_count, 2)]
    chan_blocks = [from_partner(white, "chan", away) for away in range(1, chan_count)]
    joined, col_blocks = picked(row_blocks, chan_blocks, tm_count)
    for away in partners(tm_count):
        col_blocks[away] = from_partner(col_blocks[away], "tm", away)
    return stacks_of(col_blocks, [joined, from_partner(joined, "tm", 1)], bins, windows)


def solution(mesh):
    placed = (P("chan", "tm"), P(), P(), P("chan"))
    return jax.shard_map(
        shards, mesh=mesh, in_specs=placed, out_specs=P(None, None, "tm", "chan"), check_vma=False
    )
```

```python
import functools
import math

import jax
import jax.numpy as jnp
from jax import lax
from jax.experimental import pallas as pl
from jax.experimental.pallas import tpu as pltpu
from jax.sharding import PartitionSpec as P

L = 15000
FLOOR = 0.7
F32 = jnp.float32
BF16 = jnp.bfloat16
LANE = 128
DEPTH = 256
STEP = 1024
ROW_TILE = 16


def cos_sin(turns, length):
    quarter = jnp.floor(turns * (4.0 / length) + 0.5)
    angle = (turns * 4.0 - quarter * length) * (math.pi / (2.0 * length))
    square = angle * angle
    sine = angle * (
        1.0 + square * (-1.0 / 6 + square * (1.0 / 120 + square * (-1.0 / 5040 + square * (1.0 / 362880))))
    )
    cosine = 1.0 + square * (
        -0.5 + square * (1.0 / 24 + square * (-1.0 / 720 + square * (1.0 / 40320)))
    )
    quadrant = quarter - 4.0 * jnp.floor(quarter * 0.25)
    odd = (quadrant == 1.0) | (quadrant == 3.0)
    cos_sign = jnp.where((quadrant == 1.0) | (quadrant == 2.0), -1.0, 1.0)
    sin_sign = jnp.where(quadrant >= 2.0, -1.0, 1.0)
    return cos_sign * jnp.where(odd, sine, cosine), sin_sign * jnp.where(odd, cosine, sine)


def spectra_kernel(
    bins, windows, block_len, low_end, high_end, sides,
    offsets_hbm, bins_hbm, dead_hbm, x_hbm, tail_ref, own_ref, *refs,
):
    back_ref = refs[0] if sides == 2 else None
    offsets, band_bins, dead, x_ref, acc, seg, part_seg, cos_now, sin_now, cos_turn, sin_turn, place, table = refs[-15:-2]
    small_sems, x_sems = refs[-2:]
    channels = x_ref.shape[1]
    length, hop = L, L // 2
    rows = bins * windows * 2
    half_tile = ROW_TILE // 2
    per_group = half_tile // windows
    groups = rows // ROW_TILE
    states = groups * half_tile
    bulk = (high_end - low_end) // ROW_TILE * ROW_TILE
    padded = x_ref.shape[0]
    steps = padded // STEP
    columns = [slice(n, min(n + DEPTH, channels)) for n in range(0, channels, DEPTH)]

    def x_copy(i):
        size = min(STEP, bulk - i * STEP)
        return pltpu.make_async_copy(
            x_hbm.at[pl.ds(low_end + i * STEP, size)], x_ref.at[pl.ds(i * STEP, size)], x_sems.at[i]
        )

    small = [
        pltpu.make_async_copy(offsets_hbm, offsets, small_sems.at[0]),
        pltpu.make_async_copy(bins_hbm, band_bins, small_sems.at[1]),
        pltpu.make_async_copy(dead_hbm, dead, small_sems.at[2]),
    ]
    for copy in small:
        copy.start()
    x_copy(0).start()
    for copy in small:
        copy.wait()
    for i in range(1, pl.cdiv(bulk, STEP)):
        x_copy(i).start()

    tm = lax.axis_index("tm")
    ahead = [offsets[tm * windows + w] + w * hop for w in range(windows)]
    before = jnp.maximum(tm - 1, 0) * windows
    behind = [offsets[before + w] + w * hop + length - block_len for w in range(windows)]
    ends = []
    for w in range(windows if sides == 2 else 0):
        ends += [jnp.minimum(ahead[w], behind[w]), jnp.maximum(ahead[w], behind[w])]
    segments = len(ends) + 1
    trash = segments

    def make_table(index):
        moved = (index * DEPTH).astype(F32)
        to_lanes = pl.ds(pl.multiple_of(index * DEPTH, DEPTH), DEPTH)
        for side in range(sides):
            limit = moved if side else -moved
            for g in range(groups):
                at = slice(side * states + g * half_tile, side * states + (g + 1) * half_tile)
                to = side * rows + g * ROW_TILE
                c, s = cos_now[at, :], sin_now[at, :]
                inside = place[at, :] >= limit
                wave = jnp.concatenate([jnp.where(inside, c, 0.0), jnp.where(inside, s, 0.0)], axis=0)
                table[to:to + ROW_TILE, to_lanes] = wave.astype(BF16)
                ct, st = cos_turn[at, :], sin_turn[at, :]
                cos_now[at, :] = c * ct + s * st
                sin_now[at, :] = s * ct - c * st

    shape = (half_tile, DEPTH)
    row = lax.broadcasted_iota(jnp.int32, shape, 0)
    lane = (lax.broadcasted_iota(jnp.int32, shape, 1) + low_end).astype(F32)
    norm = 1.0 / math.sqrt(length)
    for side in range(sides):
        for g in range(groups):
            at = slice(side * states + g * half_tile, side * states + (g + 1) * half_tile)
            tone = jnp.zeros(shape, jnp.int32)
            start = jnp.zeros(shape, jnp.int32)
            for i in range(per_group):
                tone = jnp.where(row // windows == i, band_bins[g * per_group + i], tone)
            for w in range(windows):
                here = behind[w] - length if side else ahead[w]
                start = jnp.where(row % windows == w, here, start)
            tone, start = tone.astype(F32), start.astype(F32)
            cosine, sine = cos_sin((lane - start) * tone, length)
            cos_now[at, :] = cosine * norm
            sin_now[at, :] = -sine * norm
            cos_turn[at, :], sin_turn[at, :] = cos_sin(tone * DEPTH, length)
            place[at, :] = start + (length - 1) - lane if side else lane - start

    @pl.loop(0, padded // DEPTH)
    def _(index):
        make_table(index)

    acc[...] = jnp.zeros_like(acc)
    seg[...] = jnp.zeros_like(seg)
    if padded > bulk:
        x_ref[bulk:, :] = jnp.zeros((padded - bulk, channels), BF16)
    if high_end - low_end > bulk:
        inside = lax.broadcasted_iota(jnp.int32, (ROW_TILE, channels), 0) < high_end - low_end - bulk
        x_ref[bulk:bulk + ROW_TILE, :] = jnp.where(inside, tail_ref[...].astype(F32), 0.0).astype(BF16)

    def segment_of(position):
        index = jnp.int32(0)
        for end in ends:
            index += (end <= position).astype(jnp.int32)
        return index

    def has_end(first, size):
        found = jnp.bool_(False)
        for end in ends:
            found = jnp.logical_or(found, jnp.logical_and(end >= first, end < first + size))
        return found

    def body(base, size, edge):
        view = x_ref.at[pl.ds(base, size)]
        waves = table.at[:, pl.ds(base, size)]
        tiles = size // ROW_TILE

        def squares(t, at):
            x = view[t * ROW_TILE:(t + 1) * ROW_TILE, at].astype(F32)
            square = x * x
            return square[:half_tile] + square[half_tile:]

        for at in columns:
            if not edge:
                total = squares(0, at)
                for t in range(1, tiles):
                    total = total + squares(t, at)
            product = jnp.dot(waves[...], view[:, at], preferred_element_type=F32)
            acc[:, at] += product
            if not edge:
                part_seg[:, at] = total
        if edge:
            for t in range(tiles):
                first = base + t * ROW_TILE
                target = jnp.where(has_end(first, ROW_TILE), trash, segment_of(first))
                for at in columns:
                    seg[target, :, at] += squares(t, at)
        else:
            seg[segment_of(base)] += part_seg[...]

    @pl.loop(0, steps)
    def _(i):
        base = pl.multiple_of(i * STEP, STEP)
        pltpu.make_async_copy(
            x_hbm.at[pl.ds(low_end + base, STEP)], x_ref.at[pl.ds(base, STEP)], x_sems.at[i]
        ).wait()
        if not ends:
            body(base, STEP, False)
            return
        cut = has_end(base, STEP)

        @pl.when(jnp.logical_not(cut))
        def _():
            body(base, STEP, False)

        @pl.when(cut)
        def _():
            body(base, STEP, True)

    done = steps * STEP
    if done < padded:
        if done < bulk:
            x_copy(steps).wait()
        body(done, padded - done, False)

    for i, end in enumerate(ends):
        low = ends[i - 1] if i else jnp.int32(0)
        high = ends[i + 1] if i + 1 < len(ends) else jnp.int32(high_end)
        tile = end // ROW_TILE
        x = x_ref[pl.ds(pl.multiple_of(tile * ROW_TILE, ROW_TILE), ROW_TILE), :].astype(F32)
        spot = lax.broadcasted_iota(jnp.int32, x.shape, 0) + tile * ROW_TILE
        under = jnp.logical_and(spot >= low, spot < end)
        over = jnp.logical_and(spot >= end, spot < high)
        over = jnp.logical_and(over, high // ROW_TILE != tile)
        square = x * x
        for where, index in ((under, i), (over, i + 1)):
            kept = jnp.where(where, square, 0.0)
            seg[index] += kept[:half_tile] + kept[half_tile:]

    own_ref[:rows, :] = acc[:rows, :]
    parts = [seg[i] for i in range(segments)]
    row = lax.broadcasted_iota(jnp.int32, (half_tile, channels), 0)
    own_block = jnp.where(row == windows, (1 - dead[...]).astype(F32), 0.0)
    for w in range(windows):
        after = sum(parts[2 * w + 2:]) if ends else parts[0]
        if ends:
            after = after + jnp.where(ahead[w] <= behind[w], parts[2 * w + 1], 0.0)
        own_block = jnp.where(row == w, jnp.sum(after, axis=0, keepdims=True), own_block)
    own_ref[rows:, :] = own_block
    if sides == 1:
        return
    back_ref[:rows, :] = acc[rows:, :].astype(BF16)
    back_block = jnp.zeros((ROW_TILE, channels), F32)
    back_row = lax.broadcasted_iota(jnp.int32, (ROW_TILE, channels), 0)
    for w in range(windows):
        until = sum(parts[:2 * w + 1]) + jnp.where(ahead[w] <= behind[w], parts[2 * w + 1], 0.0)
        rest = jnp.sum(until, axis=0, keepdims=True)
        for term in range(3):
            piece_of = rest.astype(BF16).astype(F32)
            rest = rest - piece_of
            back_block = jnp.where(back_row == term * windows + w, piece_of, back_block)
    back_ref[rows:, :] = back_block.astype(BF16)


def spectra_of(recording, offsets, band_bins, dead, windows, low_end, high_end, sides):
    channels, block_len = recording.shape
    bins = band_bins.shape[0]
    rows = bins * windows * 2
    padded = pl.cdiv(high_end - low_end, DEPTH) * DEPTH
    bulk = (high_end - low_end) // ROW_TILE * ROW_TILE
    tail = min(low_end + bulk, block_len - 1) // ROW_TILE
    samples = recording.T
    hbm = pl.BlockSpec(memory_space=pltpu.HBM)
    whole = pl.BlockSpec(memory_space=pltpu.VMEM)
    state = pltpu.VMEM((rows // 2 * sides, DEPTH), F32)
    out_shape = [
        jax.ShapeDtypeStruct((rows + ROW_TILE // 2, channels), F32),
        jax.ShapeDtypeStruct((rows + ROW_TILE, channels), BF16),
    ][:sides]
    return pl.pallas_call(
        functools.partial(spectra_kernel, bins, windows, block_len, low_end, high_end, sides),
        out_shape=out_shape,
        grid=(1,),
        in_specs=[
            hbm, hbm, hbm, hbm,
            pl.BlockSpec((ROW_TILE, channels), lambda i: (tail, 0)),
        ],
        out_specs=[whole] * sides,
        scratch_shapes=[
            pltpu.SMEM(offsets.shape, jnp.int32),
            pltpu.SMEM(band_bins.shape, jnp.int32),
            pltpu.VMEM((1, channels), jnp.int32),
            pltpu.VMEM((padded, channels), BF16),
            pltpu.VMEM((sides * rows, channels), F32),
            pltpu.VMEM((2 * windows + 2, ROW_TILE // 2, channels), F32),
            pltpu.VMEM((ROW_TILE // 2, channels), F32),
            state, state, state, state, state,
            pltpu.VMEM((sides * rows, padded), BF16),
            pltpu.SemaphoreType.DMA((3,)),
            pltpu.SemaphoreType.DMA((pl.cdiv(padded, STEP),)),
        ],
        compiler_params=pltpu.CompilerParams(vmem_limit_bytes=60 * 2**20),
        cost_estimate=pl.CostEstimate(
            flops=2 * channels * (high_end - low_end) * sides * rows,
            bytes_accessed=channels * (high_end - low_end) * 2,
            transcendentals=0,
        ),
        name="band_spectra" if sides == 2 else "band_spectra_rest",
    )(offsets, band_bins, dead.reshape(1, channels), samples, samples)


def whiten_kernel(bins, windows, own_ref, rest_ref, within_ref, across_ref, white_ref):
    rows = bins * windows * 2
    even = lax.axis_index("tm") % 2 == 0
    more = jnp.where(even, within_ref[...].astype(F32), across_ref[...].astype(F32))
    raw = own_ref[:rows, :] + rest_ref[:rows, :] + more[:rows]
    extra = more[rows:]
    which = lax.broadcasted_iota(jnp.int32, (rows, 1), 0) % windows
    alive = own_ref[rows + windows:rows + windows + 1, :]
    scale = factor = None
    for w in range(windows):
        energy = own_ref[rows + w:rows + w + 1, :] + rest_ref[rows + w:rows + w + 1, :]
        for term in range(3):
            energy = energy + extra[term * windows + w:term * windows + w + 1, :]
        inverse = 1.0 / jnp.sqrt(energy / L + 1e-06)
        scale = inverse if w == 0 else jnp.where(which == w, inverse, scale)
    spectra = raw * scale
    power = spectra * spectra
    for w in range(windows):
        level = jnp.sum(jnp.where(which == w, power, 0.0), axis=0, keepdims=True) * (1.0 / bins)
        one = alive / jnp.sqrt(jnp.maximum(level, FLOOR))
        factor = one if w == 0 else jnp.where(which == w, one, factor)
    white = (spectra * factor).astype(BF16)
    width = white_ref.shape[2]
    for h in range(white_ref.shape[0]):
        white_ref[h] = white[:, h * width:(h + 1) * width]


def whiten(own, rest, within, across, bins, windows, halves):
    channels = own.shape[1]
    return pl.pallas_call(
        functools.partial(whiten_kernel, bins, windows),
        out_shape=jax.ShapeDtypeStruct((halves, bins * windows * 2, channels // halves), BF16),
        compiler_params=pltpu.CompilerParams(vmem_limit_bytes=12 * 2**20),
        name="whiten",
    )(own, rest, within, across)


def stack_kernel(windows, scale, devices, *refs):
    col_refs, row_refs = refs[:devices], refs[devices:devices + 2]
    out_hbm, lhs, held, made, sems = refs[devices + 2:]
    per_group = ROW_TILE // (2 * windows)
    step = pl.program_id(0)
    width = col_refs[0].shape[1]
    depth = devices * ROW_TILE
    _, halves, _, span = row_refs[0].shape
    channels = halves * span
    exact = math.frexp(scale)[0] == 0.5

    by_partner = dict(zip([0, *partners(devices)], col_refs))
    cols = jnp.stack([by_partner[away][...].astype(F32) for away in range(devices)])
    if exact:
        cols = cols * scale
    head, tail = cols[:, :ROW_TILE // 2], cols[:, ROW_TILE // 2:]
    straight = cols.reshape(depth, width)
    turned = jnp.concatenate([-tail, head], axis=1).reshape(depth, width)
    lhs[:width, :] = straight.T.astype(BF16)
    lhs[width:, :] = turned.T.astype(BF16)
    for away in range(devices):
        to = slice(away * ROW_TILE, (away + 1) * ROW_TILE)
        for h in range(halves):
            held[to, h * span:(h + 1) * span] = row_refs[away % 2][away // 2, h].astype(F32)

    def out_copy(slot, part, bin_index):
        to = out_hbm.at[part, bin_index]
        return pltpu.make_async_copy(made.at[slot], to, sems.at[slot])

    which = lax.broadcasted_iota(jnp.int32, (depth, 1), 0) % (ROW_TILE // 2) // windows
    for b in range(per_group):
        for part in range(2):
            slot = 2 * b + part

            @pl.when(step > 0)
            def _():
                out_copy(slot, part, (step - 1) * per_group + b).wait()

        for n in range(0, channels, DEPTH):
            at = slice(n, min(n + DEPTH, channels))
            rhs = jnp.where(which == b, held[:, at], 0.0).astype(BF16)
            for part in range(2):
                product = jnp.dot(
                    lhs[part * width:(part + 1) * width, :], rhs, preferred_element_type=F32
                )
                if not exact:
                    product = product * scale
                made[2 * b + part, :, at] = product.astype(BF16)
        for part in range(2):
            out_copy(2 * b + part, part, step * per_group + b).start()

    @pl.when(step == pl.num_programs(0) - 1)
    def _():
        for b in range(per_group):
            for part in range(2):
                out_copy(2 * b + part, part, step * per_group + b).wait()


def stacks_of(col_blocks, row_blocks, bins, windows):
    devices = len(col_blocks)
    chips, halves, _, span = row_blocks[0].shape
    width = col_blocks[0].shape[1]
    per_group = ROW_TILE // (2 * windows)
    scale = 1.0 / math.sqrt(windows * devices)
    channels = halves * span
    return pl.pallas_call(
        functools.partial(stack_kernel, windows, scale, devices),
        out_shape=jax.ShapeDtypeStruct((2, bins, width, channels), BF16),
        grid=(bins // per_group,),
        in_specs=[pl.BlockSpec((ROW_TILE, width), lambda i: (i, 0))] * devices
        + [pl.BlockSpec((chips, halves, ROW_TILE, span), lambda i: (0, 0, i, 0))] * 2,
        out_specs=pl.BlockSpec(memory_space=pltpu.HBM),
        scratch_shapes=[
            pltpu.VMEM((2 * width, devices * ROW_TILE), BF16),
            pltpu.VMEM((devices * ROW_TILE, channels), F32),
            pltpu.VMEM((2 * per_group, width, channels), BF16),
            pltpu.SemaphoreType.DMA((2 * per_group,)),
        ],
        compiler_params=pltpu.CompilerParams(
            dimension_semantics=("arbitrary",), vmem_limit_bytes=24 * 2**20
        ),
        cost_estimate=pl.CostEstimate(
            flops=2 * 2 * bins * width * channels * devices * ROW_TILE,
            bytes_accessed=2 * bins * width * channels * 2,
            transcendentals=0,
        ),
        name="stack_products",
    )(*[col_blocks[away] for away in [0, *partners(devices)]], *row_blocks)


def pick_kernel(count, chips, *refs):
    row_refs, chan_refs = refs[:chips], refs[chips:-2 - count]
    joined_ref, out_refs, held = refs[-2 - count], refs[-1 - count:-1], refs[-1]
    tm, mine = lax.axis_index("tm"), lax.axis_index("chan")
    halves = row_refs[0].shape[0]
    for i, ref in enumerate(row_refs):
        joined_ref[i] = ref[...]
    for away, ref in enumerate((row_refs[0], *chan_refs)):
        held[jnp.bitwise_xor(mine, away)] = ref[...]
    for away, out_ref in enumerate(out_refs):
        wanted = jnp.bitwise_xor(tm, away)
        out_ref[...] = held[wanted // halves, wanted % halves]


def picked(row_blocks, chan_blocks, count):
    block = row_blocks[0]
    _, rows, width = block.shape
    chips = len(row_blocks)
    whole = pl.BlockSpec(memory_space=pltpu.VMEM)
    joined, *picks = pl.pallas_call(
        functools.partial(pick_kernel, count, chips),
        out_shape=[jax.ShapeDtypeStruct((chips, *block.shape), block.dtype)]
        + [jax.ShapeDtypeStruct((rows, width), block.dtype)] * count,
        in_specs=[whole] * (chips + len(chan_blocks)),
        out_specs=[whole] * (1 + count),
        scratch_shapes=[pltpu.VMEM((1 + len(chan_blocks), *block.shape), block.dtype)],
        compiler_params=pltpu.CompilerParams(vmem_limit_bytes=16 * 2**20),
        name="pick_blocks",
    )(*row_blocks, *chan_blocks)
    return joined, picks


def earlier_share(block, axis):
    count = lax.axis_size(axis)
    within = lax.ppermute(block, axis, [(i + 1, i) for i in range(0, count - 1, 2)])
    across = lax.ppermute(block, axis, [(i + 1, i) for i in range(1, count - 1, 2)])
    return within, across


def partners(count):
    return [*range(2, count, 2), *range(3, count, 2), 1]


def chan_blocks_of(block):
    count = lax.axis_size("chan")
    blocks = {0: block}
    for away in range(1, count):
        near = away & -away
        blocks[away] = from_partner(blocks[away ^ near], "chan", near)
    return [blocks[away] for away in range(1, count)]


def from_partner(block, axis, away):
    return lax.ppermute(block, axis, [(i, i ^ away) for i in range(lax.axis_size(axis))])


def shards(recording, offsets, band_bins, dead_flags):
    channels, block_len = recording.shape
    windows = block_len // (L // 2)
    bins = band_bins.shape[0]
    chan_count, tm_count = lax.axis_size("chan"), lax.axis_size("tm")
    halves = tm_count // chan_count
    rim = L // 2 + L // 4
    cut = min(pl.cdiv(rim, STEP) * STEP, block_len)
    own, back = spectra_of(recording, offsets, band_bins, dead_flags, windows, 0, cut, 2)
    more = earlier_share(back, "tm")
    rest, = spectra_of(recording, offsets, band_bins, dead_flags, windows, cut, block_len, 1)
    white = whiten(own, rest, *more, bins, windows, halves)
    row_blocks = [white] + [from_partner(white, "tm", away) for away in range(2, tm_count, 2)]
    chan_blocks = chan_blocks_of(white)
    joined, col_blocks = picked(row_blocks, chan_blocks, tm_count)
    for away in partners(tm_count):
        col_blocks[away] = from_partner(col_blocks[away], "tm", away)
    return stacks_of(col_blocks, [joined, from_partner(joined, "tm", 1)], bins, windows)


def solution(mesh):
    placed = (P("chan", "tm"), P(), P(), P("chan"))
    return jax.shard_map(
        shards, mesh=mesh, in_specs=placed, out_specs=P(None, None, "tm", "chan"), check_vma=False
    )
```

```python
import functools
import math

import jax
import jax.numpy as jnp
from jax import lax
from jax.experimental import pallas as pl
from jax.experimental.pallas import tpu as pltpu
from jax.sharding import PartitionSpec as P

L = 15000
FLOOR = 0.7
F32 = jnp.float32
BF16 = jnp.bfloat16
LANE = 128
DEPTH = 256
STEP = 1024
ROW_TILE = 16


def cos_sin(turns, length):
    quarter = jnp.floor(turns * (4.0 / length) + 0.5)
    angle = (turns * 4.0 - quarter * length) * (math.pi / (2.0 * length))
    square = angle * angle
    sine = angle * (
        1.0 + square * (-1.0 / 6 + square * (1.0 / 120 + square * (-1.0 / 5040 + square * (1.0 / 362880))))
    )
    cosine = 1.0 + square * (
        -0.5 + square * (1.0 / 24 + square * (-1.0 / 720 + square * (1.0 / 40320)))
    )
    quadrant = quarter - 4.0 * jnp.floor(quarter * 0.25)
    odd = (quadrant == 1.0) | (quadrant == 3.0)
    cos_sign = jnp.where((quadrant == 1.0) | (quadrant == 2.0), -1.0, 1.0)
    sin_sign = jnp.where(quadrant >= 2.0, -1.0, 1.0)
    return cos_sign * jnp.where(odd, sine, cosine), sin_sign * jnp.where(odd, cosine, sine)


def spectra_kernel(
    bins, windows, block_len, low_end, high_end, sides,
    offsets_hbm, bins_hbm, dead_hbm, x_hbm, tail_ref, own_ref, *refs,
):
    back_ref = refs[0] if sides == 2 else None
    offsets, band_bins, dead, x_ref, acc, seg, part_seg, cos_now, sin_now, cos_turn, sin_turn, place, table = refs[-15:-2]
    small_sems, x_sems = refs[-2:]
    channels = x_ref.shape[1]
    length, hop = L, L // 2
    rows = bins * windows * 2
    half_tile = ROW_TILE // 2
    per_group = half_tile // windows
    groups = rows // ROW_TILE
    states = groups * half_tile
    bulk = (high_end - low_end) // ROW_TILE * ROW_TILE
    padded = x_ref.shape[0]
    steps = padded // STEP
    columns = [slice(n, min(n + DEPTH, channels)) for n in range(0, channels, DEPTH)]

    def x_copy(i):
        size = min(STEP, bulk - i * STEP)
        return pltpu.make_async_copy(
            x_hbm.at[pl.ds(low_end + i * STEP, size)], x_ref.at[pl.ds(i * STEP, size)], x_sems.at[i]
        )

    small = [
        pltpu.make_async_copy(offsets_hbm, offsets, small_sems.at[0]),
        pltpu.make_async_copy(bins_hbm, band_bins, small_sems.at[1]),
        pltpu.make_async_copy(dead_hbm, dead, small_sems.at[2]),
    ]
    for copy in small:
        copy.start()
    x_copy(0).start()
    for copy in small:
        copy.wait()
    for i in range(1, pl.cdiv(bulk, STEP)):
        x_copy(i).start()

    tm = lax.axis_index("tm")
    ahead = [offsets[tm * windows + w] + w * hop for w in range(windows)]
    before = jnp.maximum(tm - 1, 0) * windows
    behind = [offsets[before + w] + w * hop + length - block_len for w in range(windows)]
    ends = []
    for w in range(windows if sides == 2 else 0):
        ends += [jnp.minimum(ahead[w], behind[w]), jnp.maximum(ahead[w], behind[w])]
    segments = len(ends) + 1
    trash = segments

    def make_table(index):
        moved = (index * DEPTH).astype(F32)
        to_lanes = pl.ds(pl.multiple_of(index * DEPTH, DEPTH), DEPTH)
        for side in range(sides):
            limit = moved if side else -moved
            for g in range(groups):
                at = slice(side * states + g * half_tile, side * states + (g + 1) * half_tile)
                to = side * rows + g * ROW_TILE
                c, s = cos_now[at, :], sin_now[at, :]
                inside = place[at, :] >= limit
                wave = jnp.concatenate([jnp.where(inside, c, 0.0), jnp.where(inside, s, 0.0)], axis=0)
                table[to:to + ROW_TILE, to_lanes] = wave.astype(BF16)
                ct, st = cos_turn[at, :], sin_turn[at, :]
                cos_now[at, :] = c * ct + s * st
                sin_now[at, :] = s * ct - c * st

    shape = (half_tile, DEPTH)
    row = lax.broadcasted_iota(jnp.int32, shape, 0)
    lane = (lax.broadcasted_iota(jnp.int32, shape, 1) + low_end).astype(F32)
    norm = 1.0 / math.sqrt(length)
    for side in range(sides):
        for g in range(groups):
            at = slice(side * states + g * half_tile, side * states + (g + 1) * half_tile)
            tone = jnp.zeros(shape, jnp.int32)
            start = jnp.zeros(shape, jnp.int32)
            for i in range(per_group):
                tone = jnp.where(row // windows == i, band_bins[g * per_group + i], tone)
            for w in range(windows):
                here = behind[w] - length if side else ahead[w]
                start = jnp.where(row % windows == w, here, start)
            tone, start = tone.astype(F32), start.astype(F32)
            cosine, sine = cos_sin((lane - start) * tone, length)
            cos_now[at, :] = cosine * norm
            sin_now[at, :] = -sine * norm
            cos_turn[at, :], sin_turn[at, :] = cos_sin(tone * DEPTH, length)
            place[at, :] = start + (length - 1) - lane if side else lane - start
    acc[...] = jnp.zeros_like(acc)
    seg[...] = jnp.zeros_like(seg)
    if padded > bulk:
        x_ref[bulk:, :] = jnp.zeros((padded - bulk, channels), BF16)
    if high_end - low_end > bulk:
        inside = lax.broadcasted_iota(jnp.int32, (ROW_TILE, channels), 0) < high_end - low_end - bulk
        x_ref[bulk:bulk + ROW_TILE, :] = jnp.where(inside, tail_ref[...].astype(F32), 0.0).astype(BF16)

    def segment_of(position):
        index = jnp.int32(0)
        for end in ends:
            index += (end <= position).astype(jnp.int32)
        return index

    def has_end(first, size):
        found = jnp.bool_(False)
        for end in ends:
            found = jnp.logical_or(found, jnp.logical_and(end >= first, end < first + size))
        return found

    def body(base, size, edge):
        view = x_ref.at[pl.ds(base, size)]
        waves = table.at[:, pl.ds(base, size)]
        tiles = size // ROW_TILE

        def squares(t, at):
            x = view[t * ROW_TILE:(t + 1) * ROW_TILE, at].astype(F32)
            square = x * x
            return square[:half_tile] + square[half_tile:]

        for at in columns:
            if not edge:
                total = squares(0, at)
                for t in range(1, tiles):
                    total = total + squares(t, at)
            product = jnp.dot(waves[...], view[:, at], preferred_element_type=F32)
            acc[:, at] += product
            if not edge:
                part_seg[:, at] = total
        if edge:
            for t in range(tiles):
                first = base + t * ROW_TILE
                target = jnp.where(has_end(first, ROW_TILE), trash, segment_of(first))
                for at in columns:
                    seg[target, :, at] += squares(t, at)
        else:
            seg[segment_of(base)] += part_seg[...]

    @pl.loop(0, steps)
    def _(i):
        base = pl.multiple_of(i * STEP, STEP)
        for j in range(STEP // DEPTH):
            make_table(i * (STEP // DEPTH) + j)
        pltpu.make_async_copy(
            x_hbm.at[pl.ds(low_end + base, STEP)], x_ref.at[pl.ds(base, STEP)], x_sems.at[i]
        ).wait()
        if not ends:
            body(base, STEP, False)
            return
        cut = has_end(base, STEP)

        @pl.when(jnp.logical_not(cut))
        def _():
            body(base, STEP, False)

        @pl.when(cut)
        def _():
            body(base, STEP, True)

    done = steps * STEP
    if done < padded:
        for j in range(done // DEPTH, padded // DEPTH):
            make_table(jnp.int32(j))
        if done < bulk:
            x_copy(steps).wait()
        body(done, padded - done, False)

    for i, end in enumerate(ends):
        low = ends[i - 1] if i else jnp.int32(0)
        high = ends[i + 1] if i + 1 < len(ends) else jnp.int32(high_end)
        tile = end // ROW_TILE
        x = x_ref[pl.ds(pl.multiple_of(tile * ROW_TILE, ROW_TILE), ROW_TILE), :].astype(F32)
        spot = lax.broadcasted_iota(jnp.int32, x.shape, 0) + tile * ROW_TILE
        under = jnp.logical_and(spot >= low, spot < end)
        over = jnp.logical_and(spot >= end, spot < high)
        over = jnp.logical_and(over, high // ROW_TILE != tile)
        square = x * x
        for where, index in ((under, i), (over, i + 1)):
            kept = jnp.where(where, square, 0.0)
            seg[index] += kept[:half_tile] + kept[half_tile:]

    own_ref[:rows, :] = acc[:rows, :]
    parts = [seg[i] for i in range(segments)]
    row = lax.broadcasted_iota(jnp.int32, (half_tile, channels), 0)
    own_block = jnp.where(row == windows, (1 - dead[...]).astype(F32), 0.0)
    for w in range(windows):
        after = sum(parts[2 * w + 2:]) if ends else parts[0]
        if ends:
            after = after + jnp.where(ahead[w] <= behind[w], parts[2 * w + 1], 0.0)
        own_block = jnp.where(row == w, jnp.sum(after, axis=0, keepdims=True), own_block)
    own_ref[rows:, :] = own_block
    if sides == 1:
        return
    back_ref[:rows, :] = acc[rows:, :].astype(BF16)
    back_block = jnp.zeros((ROW_TILE, channels), F32)
    back_row = lax.broadcasted_iota(jnp.int32, (ROW_TILE, channels), 0)
    for w in range(windows):
        until = sum(parts[:2 * w + 1]) + jnp.where(ahead[w] <= behind[w], parts[2 * w + 1], 0.0)
        rest = jnp.sum(until, axis=0, keepdims=True)
        for term in range(3):
            piece_of = rest.astype(BF16).astype(F32)
            rest = rest - piece_of
            back_block = jnp.where(back_row == term * windows + w, piece_of, back_block)
    back_ref[rows:, :] = back_block.astype(BF16)


def spectra_of(recording, offsets, band_bins, dead, windows, low_end, high_end, sides):
    channels, block_len = recording.shape
    bins = band_bins.shape[0]
    rows = bins * windows * 2
    padded = pl.cdiv(high_end - low_end, DEPTH) * DEPTH
    bulk = (high_end - low_end) // ROW_TILE * ROW_TILE
    tail = min(low_end + bulk, block_len - 1) // ROW_TILE
    samples = recording.T
    hbm = pl.BlockSpec(memory_space=pltpu.HBM)
    whole = pl.BlockSpec(memory_space=pltpu.VMEM)
    state = pltpu.VMEM((rows // 2 * sides, DEPTH), F32)
    out_shape = [
        jax.ShapeDtypeStruct((rows + ROW_TILE // 2, channels), F32),
        jax.ShapeDtypeStruct((rows + ROW_TILE, channels), BF16),
    ][:sides]
    return pl.pallas_call(
        functools.partial(spectra_kernel, bins, windows, block_len, low_end, high_end, sides),
        out_shape=out_shape,
        grid=(1,),
        in_specs=[
            hbm, hbm, hbm, hbm,
            pl.BlockSpec((ROW_TILE, channels), lambda i: (tail, 0)),
        ],
        out_specs=[whole] * sides,
        scratch_shapes=[
            pltpu.SMEM(offsets.shape, jnp.int32),
            pltpu.SMEM(band_bins.shape, jnp.int32),
            pltpu.VMEM((1, channels), jnp.int32),
            pltpu.VMEM((padded, channels), BF16),
            pltpu.VMEM((sides * rows, channels), F32),
            pltpu.VMEM((2 * windows + 2, ROW_TILE // 2, channels), F32),
            pltpu.VMEM((ROW_TILE // 2, channels), F32),
            state, state, state, state, state,
            pltpu.VMEM((sides * rows, padded), BF16),
            pltpu.SemaphoreType.DMA((3,)),
            pltpu.SemaphoreType.DMA((pl.cdiv(padded, STEP),)),
        ],
        compiler_params=pltpu.CompilerParams(vmem_limit_bytes=60 * 2**20),
        cost_estimate=pl.CostEstimate(
            flops=2 * channels * (high_end - low_end) * sides * rows,
            bytes_accessed=channels * (high_end - low_end) * 2,
            transcendentals=0,
        ),
        name="band_spectra" if sides == 2 else "band_spectra_rest",
    )(offsets, band_bins, dead.reshape(1, channels), samples, samples)


def whiten_kernel(bins, windows, own_ref, rest_ref, more_ref, white_ref):
    rows = bins * windows * 2
    more = more_ref[...].astype(F32)
    raw = own_ref[:rows, :] + rest_ref[:rows, :] + more[:rows]
    extra = more[rows:]
    which = lax.broadcasted_iota(jnp.int32, (rows, 1), 0) % windows
    alive = own_ref[rows + windows:rows + windows + 1, :]
    scale = factor = None
    for w in range(windows):
        energy = own_ref[rows + w:rows + w + 1, :] + rest_ref[rows + w:rows + w + 1, :]
        for term in range(3):
            energy = energy + extra[term * windows + w:term * windows + w + 1, :]
        inverse = 1.0 / jnp.sqrt(energy / L + 1e-06)
        scale = inverse if w == 0 else jnp.where(which == w, inverse, scale)
    spectra = raw * scale
    power = spectra * spectra
    for w in range(windows):
        level = jnp.sum(jnp.where(which == w, power, 0.0), axis=0, keepdims=True) * (1.0 / bins)
        one = alive / jnp.sqrt(jnp.maximum(level, FLOOR))
        factor = one if w == 0 else jnp.where(which == w, one, factor)
    white = (spectra * factor).astype(BF16)
    width = white_ref.shape[2]
    for h in range(white_ref.shape[0]):
        white_ref[h] = white[:, h * width:(h + 1) * width]


def whiten(own, rest, more, bins, windows, halves):
    channels = own.shape[1]
    return pl.pallas_call(
        functools.partial(whiten_kernel, bins, windows),
        out_shape=jax.ShapeDtypeStruct((halves, bins * windows * 2, channels // halves), BF16),
        compiler_params=pltpu.CompilerParams(vmem_limit_bytes=12 * 2**20),
        name="whiten",
    )(own, rest, more)


def stack_kernel(windows, scale, devices, *refs):
    col_refs, row_refs = refs[:devices], refs[devices:devices + 2]
    out_hbm, lhs, held, made, sems = refs[devices + 2:]
    per_group = ROW_TILE // (2 * windows)
    step = pl.program_id(0)
    width = col_refs[0].shape[1]
    depth = devices * ROW_TILE
    _, halves, _, span = row_refs[0].shape
    channels = halves * span
    exact = math.frexp(scale)[0] == 0.5

    by_partner = dict(zip([0, *partners(devices)], col_refs))
    cols = jnp.stack([by_partner[away][...].astype(F32) for away in range(devices)])
    if exact:
        cols = cols * scale
    head, tail = cols[:, :ROW_TILE // 2], cols[:, ROW_TILE // 2:]
    straight = cols.reshape(depth, width)
    turned = jnp.concatenate([-tail, head], axis=1).reshape(depth, width)
    lhs[:width, :] = straight.T.astype(BF16)
    lhs[width:, :] = turned.T.astype(BF16)
    for away in range(devices):
        to = slice(away * ROW_TILE, (away + 1) * ROW_TILE)
        for h in range(halves):
            held[to, h * span:(h + 1) * span] = row_refs[away % 2][away // 2, h].astype(F32)

    def out_copy(slot, part, bin_index):
        to = out_hbm.at[part, bin_index]
        return pltpu.make_async_copy(made.at[slot], to, sems.at[slot])

    which = lax.broadcasted_iota(jnp.int32, (depth, 1), 0) % (ROW_TILE // 2) // windows
    for b in range(per_group):
        for part in range(2):
            slot = 2 * b + part

            @pl.when(step > 0)
            def _():
                out_copy(slot, part, (step - 1) * per_group + b).wait()

        for n in range(0, channels, DEPTH):
            at = slice(n, min(n + DEPTH, channels))
            rhs = jnp.where(which == b, held[:, at], 0.0).astype(BF16)
            for part in range(2):
                product = jnp.dot(
                    lhs[part * width:(part + 1) * width, :], rhs, preferred_element_type=F32
                )
                if not exact:
                    product = product * scale
                made[2 * b + part, :, at] = product.astype(BF16)
        for part in range(2):
            out_copy(2 * b + part, part, step * per_group + b).start()

    @pl.when(step == pl.num_programs(0) - 1)
    def _():
        for b in range(per_group):
            for part in range(2):
                out_copy(2 * b + part, part, step * per_group + b).wait()


def stacks_of(col_blocks, row_blocks, bins, windows):
    devices = len(col_blocks)
    chips, halves, _, span = row_blocks[0].shape
    width = col_blocks[0].shape[1]
    per_group = ROW_TILE // (2 * windows)
    scale = 1.0 / math.sqrt(windows * devices)
    channels = halves * span
    return pl.pallas_call(
        functools.partial(stack_kernel, windows, scale, devices),
        out_shape=jax.ShapeDtypeStruct((2, bins, width, channels), BF16),
        grid=(bins // per_group,),
        in_specs=[pl.BlockSpec((ROW_TILE, width), lambda i: (i, 0))] * devices
        + [pl.BlockSpec((chips, halves, ROW_TILE, span), lambda i: (0, 0, i, 0))] * 2,
        out_specs=pl.BlockSpec(memory_space=pltpu.HBM),
        scratch_shapes=[
            pltpu.VMEM((2 * width, devices * ROW_TILE), BF16),
            pltpu.VMEM((devices * ROW_TILE, channels), F32),
            pltpu.VMEM((2 * per_group, width, channels), BF16),
            pltpu.SemaphoreType.DMA((2 * per_group,)),
        ],
        compiler_params=pltpu.CompilerParams(
            dimension_semantics=("arbitrary",), vmem_limit_bytes=24 * 2**20
        ),
        cost_estimate=pl.CostEstimate(
            flops=2 * 2 * bins * width * channels * devices * ROW_TILE,
            bytes_accessed=2 * bins * width * channels * 2,
            transcendentals=0,
        ),
        name="stack_products",
    )(*[col_blocks[away] for away in [0, *partners(devices)]], *row_blocks)


def pick_kernel(count, chips, *refs):
    row_refs, chan_refs = refs[:chips], refs[chips:-2 - count]
    joined_ref, out_refs, held = refs[-2 - count], refs[-1 - count:-1], refs[-1]
    tm, mine = lax.axis_index("tm"), lax.axis_index("chan")
    halves = row_refs[0].shape[0]
    for i, ref in enumerate(row_refs):
        joined_ref[i] = ref[...]
    for away, ref in enumerate((row_refs[0], *chan_refs)):
        held[jnp.bitwise_xor(mine, away)] = ref[...]
    for away, out_ref in enumerate(out_refs):
        wanted = jnp.bitwise_xor(tm, away)
        out_ref[...] = held[wanted // halves, wanted % halves]


def picked(row_blocks, chan_blocks, count):
    block = row_blocks[0]
    _, rows, width = block.shape
    chips = len(row_blocks)
    whole = pl.BlockSpec(memory_space=pltpu.VMEM)
    joined, *picks = pl.pallas_call(
        functools.partial(pick_kernel, count, chips),
        out_shape=[jax.ShapeDtypeStruct((chips, *block.shape), block.dtype)]
        + [jax.ShapeDtypeStruct((rows, width), block.dtype)] * count,
        in_specs=[whole] * (chips + len(chan_blocks)),
        out_specs=[whole] * (1 + count),
        scratch_shapes=[pltpu.VMEM((1 + len(chan_blocks), *block.shape), block.dtype)],
        compiler_params=pltpu.CompilerParams(vmem_limit_bytes=16 * 2**20),
        name="pick_blocks",
    )(*row_blocks, *chan_blocks)
    return joined, picks


def moved(block, axis, far):
    count = lax.axis_size(axis)
    return lax.ppermute(block, axis, [(i + far, i) for i in range(count) if 0 <= i + far < count])


def partners(count):
    return [*range(2, count, 2), *range(3, count, 2), 1]


def chan_blocks_of(block):
    count = lax.axis_size("chan")
    blocks = {0: block}
    for away in range(1, count):
        near = away & -away
        blocks[away] = from_partner(blocks[away ^ near], "chan", near)
    return [blocks[away] for away in range(1, count)]


def from_partner(block, axis, away):
    return lax.ppermute(block, axis, [(i, i ^ away) for i in range(lax.axis_size(axis))])


def shards(recording, offsets, band_bins, dead_flags):
    channels, block_len = recording.shape
    windows = block_len // (L // 2)
    bins = band_bins.shape[0]
    chan_count, tm_count = lax.axis_size("chan"), lax.axis_size("tm")
    halves = tm_count // chan_count
    rim = L // 2 + L // 4
    cut = min(pl.cdiv(rim, STEP) * STEP, block_len)
    own, back = spectra_of(recording, offsets, band_bins, dead_flags, windows, 0, cut, 2)
    more = moved(back, "tm", 1)
    rest, = spectra_of(recording, offsets, band_bins, dead_flags, windows, cut, block_len, 1)
    white = whiten(own, rest, more, bins, windows, halves)
    row_blocks = [white] + [from_partner(white, "tm", away) for away in range(2, tm_count, 2)]
    chan_blocks = chan_blocks_of(white)
    joined, col_blocks = picked(row_blocks, chan_blocks, tm_count)
    for away in partners(tm_count):
        col_blocks[away] = from_partner(col_blocks[away], "tm", away)
    return stacks_of(col_blocks, [joined, from_partner(joined, "tm", 1)], bins, windows)


def solution(mesh):
    placed = (P("chan", "tm"), P(), P(), P("chan"))
    return jax.shard_map(
        shards, mesh=mesh, in_specs=placed, out_specs=P(None, None, "tm", "chan"), check_vma=False
    )
```

```python
import functools
import math

import jax
import jax.numpy as jnp
from jax import lax
from jax.experimental import pallas as pl
from jax.experimental.pallas import tpu as pltpu
from jax.sharding import PartitionSpec as P

L = 15000
FLOOR = 0.7
F32 = jnp.float32
BF16 = jnp.bfloat16
LANE = 128
DEPTH = 256
STEP = 1024
ROW_TILE = 16


def cos_sin(turns, length):
    quarter = jnp.floor(turns * (4.0 / length) + 0.5)
    angle = (turns * 4.0 - quarter * length) * (math.pi / (2.0 * length))
    square = angle * angle
    sine = angle * (
        1.0 + square * (-1.0 / 6 + square * (1.0 / 120 + square * (-1.0 / 5040 + square * (1.0 / 362880))))
    )
    cosine = 1.0 + square * (
        -0.5 + square * (1.0 / 24 + square * (-1.0 / 720 + square * (1.0 / 40320)))
    )
    quadrant = quarter - 4.0 * jnp.floor(quarter * 0.25)
    odd = (quadrant == 1.0) | (quadrant == 3.0)
    cos_sign = jnp.where((quadrant == 1.0) | (quadrant == 2.0), -1.0, 1.0)
    sin_sign = jnp.where(quadrant >= 2.0, -1.0, 1.0)
    return cos_sign * jnp.where(odd, sine, cosine), sin_sign * jnp.where(odd, cosine, sine)


def load_samples(x_hbm, x_ref, x_sems, low_end, size):
    return [
        pltpu.make_async_copy(
            x_hbm.at[pl.ds(low_end + i, min(STEP, size - i))], x_ref.at[pl.ds(i, min(STEP, size - i))],
            x_sems.at[i // STEP],
        )
        for i in range(0, size, STEP)
    ]


def make_table(table, state, place, index, windows_rows):
    rows = table.shape[0]
    to_lanes = pl.ds(pl.multiple_of(index * DEPTH, DEPTH), DEPTH)
    moved = (index * DEPTH).astype(F32)
    for r in range(0, rows, ROW_TILE):
        values = []
        for at in (slice(r, r + 8), slice(r + 8, r + 16)):
            u, v = state[0, at, :], state[1, at, :]
            ct, st = state[2, at, :], state[3, at, :]
            if place is not None:
                limit = -moved if at.start < windows_rows else moved
                values.append(jnp.where(place[at, :] >= limit, u, 0.0))
            else:
                values.append(u)
            state[0, at, :] = u * ct - v * st
            state[1, at, :] = v * ct + u * st
        table[r:r + ROW_TILE, to_lanes] = jnp.concatenate(values, axis=0).astype(BF16)


def add_products(table, x_ref, acc, base, size, row_range, energy_at):
    view = x_ref.at[pl.ds(base, size)]
    waves = table.at[:, pl.ds(base, size)]
    low, high = row_range
    channels = x_ref.shape[1]
    for n in range(0, channels, DEPTH):
        at = slice(n, min(n + DEPTH, channels))
        if energy_at is not None:
            total = squares(view, 0, at)
            for t in range(1, size // ROW_TILE):
                total = total + squares(view, t, at)
        product = jnp.dot(waves[low:high, :], view[:, at], preferred_element_type=F32)
        acc[low:high, at] += product
        if energy_at is not None:
            energy_at[:, at] = total


def squares(view, t, at):
    x = view[t * ROW_TILE:(t + 1) * ROW_TILE, at].astype(F32)
    square = x * x
    return square[:ROW_TILE // 2] + square[ROW_TILE // 2:]


def mix_windows(out_ref, acc, first, windows, per_window, per_group):
    for w in range(windows):
        own_at = first + (windows - 1 - w) * per_window
        for q in range(0, per_window, per_group):
            to = q * windows + w * per_group
            out_ref[to:to + per_group, :] = acc[own_at + q:own_at + q + per_group, :]


def spectra_kernel(
    bins, windows, block_len, high_end,
    offsets_hbm, bins_hbm, dead_hbm, x_hbm, own_ref, back_ref, state_ref,
    offsets, band_bins, dead, x_ref, acc, seg, part_seg, mixed, state, place, table, small_sems, x_sems,
):
    channels = x_ref.shape[1]
    length, hop = L, L // 2
    per_window = 2 * bins
    rows = windows * per_window
    half_tile = ROW_TILE // 2
    per_group = half_tile // windows
    steps = high_end // STEP

    small = [
        pltpu.make_async_copy(offsets_hbm, offsets, small_sems.at[0]),
        pltpu.make_async_copy(bins_hbm, band_bins, small_sems.at[1]),
        pltpu.make_async_copy(dead_hbm, dead, small_sems.at[2]),
    ]
    for copy in small:
        copy.start()
    loads = load_samples(x_hbm, x_ref, x_sems, 0, high_end)
    loads[0].start()
    for copy in small:
        copy.wait()
    for copy in loads[1:]:
        copy.start()

    tm = lax.axis_index("tm")
    ahead = [offsets[tm * windows + w] + w * hop for w in range(windows)]
    before = jnp.maximum(tm - 1, 0) * windows
    behind = [offsets[before + w] + w * hop + length - block_len for w in range(windows)]
    ends = []
    for w in range(windows):
        ends += [jnp.minimum(ahead[w], behind[w]), jnp.maximum(ahead[w], behind[w])]
    segments = len(ends) + 1
    trash = segments

    shape = (half_tile, DEPTH)
    lane = lax.broadcasted_iota(jnp.int32, shape, 1).astype(F32)
    norm = 1.0 / math.sqrt(length)
    for r in range(0, 2 * rows, half_tile):
        at = slice(r, r + half_tile)
        row = lax.broadcasted_iota(jnp.int32, shape, 0) + r
        block, inner = row // per_window, row % per_window
        part = inner // per_group % 2
        bin_index = inner // (2 * per_group) * per_group + inner % per_group
        tone = jnp.zeros(shape, jnp.int32)
        for b in range(bins):
            if r // per_window != (r + half_tile - 1) // per_window or (
                r % per_window // (2 * per_group) * per_group <= b
                < (r % per_window + half_tile - 1) // (2 * per_group) * per_group + per_group
            ):
                tone = jnp.where(bin_index == b, band_bins[b], tone)
        start = jnp.zeros(shape, jnp.int32)
        for w in range(windows):
            start = jnp.where(block == windows - 1 - w, ahead[w], start)
            start = jnp.where(block == 2 * windows - 1 - w, behind[w] - length, start)
        tone, start = tone.astype(F32), start.astype(F32)
        cosine, sine = cos_sin((lane - start) * tone, length)
        state[0, at, :] = jnp.where(part == 1, -sine, cosine) * norm
        state[1, at, :] = jnp.where(part == 1, cosine, sine) * norm
        state[2, at, :], state[3, at, :] = cos_sin(tone * DEPTH, length)
        place[at, :] = lane - start if r < rows else start + (length - 1) - lane
    acc[...] = jnp.zeros_like(acc)
    seg[...] = jnp.zeros_like(seg)

    def segment_of(position):
        index = jnp.int32(0)
        for end in ends:
            index += (end <= position).astype(jnp.int32)
        return index

    def has_end(first, size):
        found = jnp.bool_(False)
        for end in ends:
            found = jnp.logical_or(found, jnp.logical_and(end >= first, end < first + size))
        return found

    def body(base, row_range, edge):
        add_products(table, x_ref, acc, base, STEP, row_range, None if edge else part_seg)
        if not edge:
            seg[segment_of(base)] += part_seg[...]
            return
        view = x_ref.at[pl.ds(base, STEP)]
        for t in range(STEP // ROW_TILE):
            first = base + t * ROW_TILE
            target = jnp.where(has_end(first, ROW_TILE), trash, segment_of(first))
            for n in range(0, channels, DEPTH):
                at = slice(n, min(n + DEPTH, channels))
                seg[target, :, at] += squares(view, t, at)

    def reach(i):
        low, high = i * STEP, (i + 1) * STEP
        own = [w for w in range(windows) if w * hop < high]
        back = [w for w in range(windows) if w * hop + hop // 2 + length - block_len > low]
        first = (windows - 1 - max(own)) * per_window // ROW_TILE * ROW_TILE
        last = (2 * windows - min(back, default=windows)) * per_window
        edges = any(
            w * hop + shift < high and w * hop + hop // 2 + shift > low
            for w in range(windows) for shift in (0, length - block_len)
        )
        return (first, min(pl.cdiv(last, ROW_TILE) * ROW_TILE, 2 * rows)), edges

    kinds = [reach(i) for i in range(steps)]
    i = 0
    while i < steps:
        until = i
        while until < steps and kinds[until] == kinds[i]:
            until += 1
        row_range, edges = kinds[i]

        @pl.loop(i, until)
        def _(step):
            base = pl.multiple_of(step * STEP, STEP)
            for j in range(STEP // DEPTH):
                make_table(table, state, place, step * (STEP // DEPTH) + j, rows)
            at = pl.ds(base, STEP)
            pltpu.make_async_copy(x_hbm.at[at], x_ref.at[at], x_sems.at[step]).wait()
            if not edges:
                body(base, row_range, False)
                return
            cut = has_end(base, STEP)

            @pl.when(jnp.logical_not(cut))
            def _():
                body(base, row_range, False)

            @pl.when(cut)
            def _():
                body(base, row_range, True)

        i = until

    for i, end in enumerate(ends):
        low = ends[i - 1] if i else jnp.int32(0)
        high = ends[i + 1] if i + 1 < len(ends) else jnp.int32(high_end)
        tile = end // ROW_TILE
        x = x_ref[pl.ds(pl.multiple_of(tile * ROW_TILE, ROW_TILE), ROW_TILE), :].astype(F32)
        spot = lax.broadcasted_iota(jnp.int32, x.shape, 0) + tile * ROW_TILE
        under = jnp.logical_and(spot >= low, spot < end)
        over = jnp.logical_and(spot >= end, spot < high)
        over = jnp.logical_and(over, high // ROW_TILE != tile)
        square = x * x
        for where, index in ((under, i), (over, i + 1)):
            kept = jnp.where(where, square, 0.0)
            seg[index] += kept[:half_tile] + kept[half_tile:]

    state_ref[...] = state[:, :rows, :]
    mix_windows(own_ref, acc, 0, windows, per_window, per_group)
    mix_windows(mixed, acc, rows, windows, per_window, per_group)
    back_ref[:rows, :] = mixed[...].astype(BF16)
    parts = [seg[i] for i in range(segments)]
    row = lax.broadcasted_iota(jnp.int32, (half_tile, channels), 0)
    own_block = jnp.where(row == windows, (1 - dead[...]).astype(F32), 0.0)
    back_block = jnp.zeros((ROW_TILE, channels), F32)
    back_row = lax.broadcasted_iota(jnp.int32, (ROW_TILE, channels), 0)
    for w in range(windows):
        turn = jnp.where(ahead[w] <= behind[w], parts[2 * w + 1], 0.0)
        own_energy = jnp.sum(sum(parts[2 * w + 2:]) + turn, axis=0, keepdims=True)
        own_block = jnp.where(row == w, own_energy, own_block)
        rest = jnp.sum(sum(parts[:2 * w + 1]) + turn, axis=0, keepdims=True)
        for term in range(3):
            piece_of = rest.astype(BF16).astype(F32)
            rest = rest - piece_of
            back_block = jnp.where(back_row == term * windows + w, piece_of, back_block)
    own_ref[rows:, :] = own_block
    back_ref[rows:, :] = back_block.astype(BF16)


def rest_kernel(
    bins, windows, block_len, low_end, state_in, x_hbm, tail_ref, own_ref,
    x_ref, acc, part_seg, total_seg, state, table, x_sems,
):
    channels = x_ref.shape[1]
    per_window = 2 * bins
    rows = windows * per_window
    half_tile = ROW_TILE // 2
    count = block_len - low_end
    bulk = count // ROW_TILE * ROW_TILE
    padded = x_ref.shape[0]
    loads = load_samples(x_hbm, x_ref, x_sems, low_end, bulk)
    for copy in loads:
        copy.start()
    state[...] = state_in[...]
    acc[...] = jnp.zeros_like(acc)
    total_seg[...] = jnp.zeros_like(total_seg)
    if padded > bulk:
        x_ref[bulk:, :] = jnp.zeros((padded - bulk, channels), BF16)
    if count > bulk:
        inside = lax.broadcasted_iota(jnp.int32, (ROW_TILE, channels), 0) < count - bulk
        x_ref[bulk:bulk + ROW_TILE, :] = jnp.where(inside, tail_ref[...].astype(F32), 0.0).astype(BF16)
    for i in range(0, padded, STEP):
        size = min(STEP, padded - i)
        for j in range(size // DEPTH):
            make_table(table, state, None, jnp.int32(i // DEPTH + j), rows)
        if i // STEP < len(loads):
            loads[i // STEP].wait()
        add_products(table, x_ref, acc, i, size, (0, rows), part_seg)
        total_seg[...] += part_seg[...]
    mix_windows(own_ref, acc, 0, windows, per_window, half_tile // windows)
    energy = jnp.sum(total_seg[...], axis=0, keepdims=True)
    row = lax.broadcasted_iota(jnp.int32, (half_tile, channels), 0)
    own_ref[rows:, :] = jnp.where(row < windows, energy, 0.0)


def spectra_of(recording, offsets, band_bins, dead, windows, high_end):
    channels, block_len = recording.shape
    bins = band_bins.shape[0]
    rows = bins * windows * 2
    samples = recording.T
    hbm = pl.BlockSpec(memory_space=pltpu.HBM)
    whole = pl.BlockSpec(memory_space=pltpu.VMEM)
    return pl.pallas_call(
        functools.partial(spectra_kernel, bins, windows, block_len, high_end),
        out_shape=[
            jax.ShapeDtypeStruct((rows + ROW_TILE // 2, channels), F32),
            jax.ShapeDtypeStruct((rows + ROW_TILE, channels), BF16),
            jax.ShapeDtypeStruct((4, rows, DEPTH), F32),
        ],
        in_specs=[hbm, hbm, hbm, hbm],
        out_specs=[whole] * 3,
        scratch_shapes=[
            pltpu.SMEM(offsets.shape, jnp.int32),
            pltpu.SMEM(band_bins.shape, jnp.int32),
            pltpu.VMEM((1, channels), jnp.int32),
            pltpu.VMEM((high_end, channels), BF16),
            pltpu.VMEM((2 * rows, channels), F32),
            pltpu.VMEM((2 * windows + 2, ROW_TILE // 2, channels), F32),
            pltpu.VMEM((ROW_TILE // 2, channels), F32),
            pltpu.VMEM((rows, channels), F32),
            pltpu.VMEM((4, 2 * rows, DEPTH), F32),
            pltpu.VMEM((2 * rows, DEPTH), F32),
            pltpu.VMEM((2 * rows, high_end), BF16),
            pltpu.SemaphoreType.DMA((3,)),
            pltpu.SemaphoreType.DMA((high_end // STEP,)),
        ],
        compiler_params=pltpu.CompilerParams(vmem_limit_bytes=60 * 2**20),
        cost_estimate=pl.CostEstimate(
            flops=2 * channels * high_end * 2 * rows, bytes_accessed=channels * high_end * 2, transcendentals=0
        ),
        name="band_spectra",
    )(offsets, band_bins, dead.reshape(1, channels), samples)


def rest_of(recording, state, bins, windows, low_end):
    channels, block_len = recording.shape
    rows = bins * windows * 2
    count = block_len - low_end
    padded = pl.cdiv(count, DEPTH) * DEPTH
    bulk = count // ROW_TILE * ROW_TILE
    tail = min(low_end + bulk, block_len - 1) // ROW_TILE
    samples = recording.T
    whole = pl.BlockSpec(memory_space=pltpu.VMEM)
    return pl.pallas_call(
        functools.partial(rest_kernel, bins, windows, block_len, low_end),
        out_shape=jax.ShapeDtypeStruct((rows + ROW_TILE // 2, channels), F32),
        grid=(1,),
        in_specs=[
            whole,
            pl.BlockSpec(memory_space=pltpu.HBM),
            pl.BlockSpec((ROW_TILE, channels), lambda i: (tail, 0)),
        ],
        out_specs=whole,
        scratch_shapes=[
            pltpu.VMEM((padded, channels), BF16),
            pltpu.VMEM((rows, channels), F32),
            pltpu.VMEM((ROW_TILE // 2, channels), F32),
            pltpu.VMEM((ROW_TILE // 2, channels), F32),
            pltpu.VMEM((4, rows, DEPTH), F32),
            pltpu.VMEM((rows, padded), BF16),
            pltpu.SemaphoreType.DMA((pl.cdiv(padded, STEP),)),
        ],
        compiler_params=pltpu.CompilerParams(vmem_limit_bytes=24 * 2**20),
        cost_estimate=pl.CostEstimate(
            flops=2 * channels * count * rows, bytes_accessed=channels * count * 2, transcendentals=0
        ),
        name="band_spectra_rest",
    )(state, samples, samples)


def whiten_kernel(bins, windows, own_ref, rest_ref, more_ref, white_ref):
    rows = bins * windows * 2
    more = more_ref[...].astype(F32)
    raw = own_ref[:rows, :] + rest_ref[:rows, :] + more[:rows]
    extra = more[rows:]
    per_group = ROW_TILE // (2 * windows)
    which = lax.broadcasted_iota(jnp.int32, (rows, 1), 0) // per_group % windows
    alive = own_ref[rows + windows:rows + windows + 1, :]
    scale = factor = None
    for w in range(windows):
        energy = own_ref[rows + w:rows + w + 1, :] + rest_ref[rows + w:rows + w + 1, :]
        for term in range(3):
            energy = energy + extra[term * windows + w:term * windows + w + 1, :]
        inverse = 1.0 / jnp.sqrt(energy / L + 1e-06)
        scale = inverse if w == 0 else jnp.where(which == w, inverse, scale)
    spectra = raw * scale
    power = spectra * spectra
    for w in range(windows):
        level = jnp.sum(jnp.where(which == w, power, 0.0), axis=0, keepdims=True) * (1.0 / bins)
        one = alive / jnp.sqrt(jnp.maximum(level, FLOOR))
        factor = one if w == 0 else jnp.where(which == w, one, factor)
    white = (spectra * factor).astype(BF16)
    width = white_ref.shape[2]
    for h in range(white_ref.shape[0]):
        white_ref[h] = white[:, h * width:(h + 1) * width]


def whiten(own, rest, more, bins, windows, halves):
    channels = own.shape[1]
    return pl.pallas_call(
        functools.partial(whiten_kernel, bins, windows),
        out_shape=jax.ShapeDtypeStruct((halves, bins * windows * 2, channels // halves), BF16),
        compiler_params=pltpu.CompilerParams(vmem_limit_bytes=12 * 2**20),
        name="whiten",
    )(own, rest, more)


def stack_kernel(windows, scale, devices, *refs):
    col_refs, row_refs = refs[:devices], refs[devices:devices + 2]
    out_hbm, lhs, held, made, sems = refs[devices + 2:]
    per_group = ROW_TILE // (2 * windows)
    step = pl.program_id(0)
    width = col_refs[0].shape[1]
    depth = devices * ROW_TILE
    _, halves, _, span = row_refs[0].shape
    channels = halves * span
    exact = math.frexp(scale)[0] == 0.5

    by_partner = dict(zip([0, *partners(devices)], col_refs))
    cols = jnp.stack([by_partner[away][...].astype(F32) for away in range(devices)])
    if exact:
        cols = cols * scale
    head, tail = cols[:, :ROW_TILE // 2], cols[:, ROW_TILE // 2:]
    straight = cols.reshape(depth, width)
    turned = jnp.concatenate([-tail, head], axis=1).reshape(depth, width)
    lhs[:width, :] = straight.T.astype(BF16)
    lhs[width:, :] = turned.T.astype(BF16)
    for away in range(devices):
        to = slice(away * ROW_TILE, (away + 1) * ROW_TILE)
        for h in range(halves):
            held[to, h * span:(h + 1) * span] = row_refs[away % 2][away // 2, h].astype(F32)

    def out_copy(slot, part, bin_index):
        to = out_hbm.at[part, bin_index]
        return pltpu.make_async_copy(made.at[slot], to, sems.at[slot])

    which = lax.broadcasted_iota(jnp.int32, (depth, 1), 0) % per_group
    for b in range(per_group):
        for part in range(2):
            slot = 2 * b + part

            @pl.when(step > 0)
            def _():
                out_copy(slot, part, (step - 1) * per_group + b).wait()

        for n in range(0, channels, DEPTH):
            at = slice(n, min(n + DEPTH, channels))
            rhs = jnp.where(which == b, held[:, at], 0.0).astype(BF16)
            for part in range(2):
                product = jnp.dot(
                    lhs[part * width:(part + 1) * width, :], rhs, preferred_element_type=F32
                )
                if not exact:
                    product = product * scale
                made[2 * b + part, :, at] = product.astype(BF16)
        for part in range(2):
            out_copy(2 * b + part, part, step * per_group + b).start()

    @pl.when(step == pl.num_programs(0) - 1)
    def _():
        for b in range(per_group):
            for part in range(2):
                out_copy(2 * b + part, part, step * per_group + b).wait()


def stacks_of(col_blocks, row_blocks, bins, windows):
    devices = len(col_blocks)
    chips, halves, _, span = row_blocks[0].shape
    width = col_blocks[0].shape[1]
    per_group = ROW_TILE // (2 * windows)
    scale = 1.0 / math.sqrt(windows * devices)
    channels = halves * span
    return pl.pallas_call(
        functools.partial(stack_kernel, windows, scale, devices),
        out_shape=jax.ShapeDtypeStruct((2, bins, width, channels), BF16),
        grid=(bins // per_group,),
        in_specs=[pl.BlockSpec((ROW_TILE, width), lambda i: (i, 0))] * devices
        + [pl.BlockSpec((chips, halves, ROW_TILE, span), lambda i: (0, 0, i, 0))] * 2,
        out_specs=pl.BlockSpec(memory_space=pltpu.HBM),
        scratch_shapes=[
            pltpu.VMEM((2 * width, devices * ROW_TILE), BF16),
            pltpu.VMEM((devices * ROW_TILE, channels), F32),
            pltpu.VMEM((2 * per_group, width, channels), BF16),
            pltpu.SemaphoreType.DMA((2 * per_group,)),
        ],
        compiler_params=pltpu.CompilerParams(
            dimension_semantics=("arbitrary",), vmem_limit_bytes=24 * 2**20
        ),
        cost_estimate=pl.CostEstimate(
            flops=2 * 2 * bins * width * channels * devices * ROW_TILE,
            bytes_accessed=2 * bins * width * channels * 2,
            transcendentals=0,
        ),
        name="stack_products",
    )(*[col_blocks[away] for away in [0, *partners(devices)]], *row_blocks)


def pick_kernel(count, chips, *refs):
    row_refs, chan_refs = refs[:chips], refs[chips:-2 - count]
    joined_ref, out_refs, held = refs[-2 - count], refs[-1 - count:-1], refs[-1]
    tm, mine = lax.axis_index("tm"), lax.axis_index("chan")
    halves = row_refs[0].shape[0]
    for i, ref in enumerate(row_refs):
        joined_ref[i] = ref[...]
    for away, ref in enumerate((row_refs[0], *chan_refs)):
        held[jnp.bitwise_xor(mine, away)] = ref[...]
    for away, out_ref in enumerate(out_refs):
        wanted = jnp.bitwise_xor(tm, away)
        out_ref[...] = held[wanted // halves, wanted % halves]


def picked(row_blocks, chan_blocks, count):
    block = row_blocks[0]
    _, rows, width = block.shape
    chips = len(row_blocks)
    whole = pl.BlockSpec(memory_space=pltpu.VMEM)
    joined, *picks = pl.pallas_call(
        functools.partial(pick_kernel, count, chips),
        out_shape=[jax.ShapeDtypeStruct((chips, *block.shape), block.dtype)]
        + [jax.ShapeDtypeStruct((rows, width), block.dtype)] * count,
        in_specs=[whole] * (chips + len(chan_blocks)),
        out_specs=[whole] * (1 + count),
        scratch_shapes=[pltpu.VMEM((1 + len(chan_blocks), *block.shape), block.dtype)],
        compiler_params=pltpu.CompilerParams(vmem_limit_bytes=16 * 2**20),
        name="pick_blocks",
    )(*row_blocks, *chan_blocks)
    return joined, picks


def moved(block, axis, far):
    count = lax.axis_size(axis)
    return lax.ppermute(block, axis, [(i + far, i) for i in range(count) if 0 <= i + far < count])


def partners(count):
    return [*range(2, count, 2), *range(3, count, 2), 1]


def chan_blocks_of(block):
    count = lax.axis_size("chan")
    blocks = {0: block}
    for away in range(1, count):
        near = away & -away
        blocks[away] = from_partner(blocks[away ^ near], "chan", near)
    return [blocks[away] for away in range(1, count)]


def from_partner(block, axis, away):
    return lax.ppermute(block, axis, [(i, i ^ away) for i in range(lax.axis_size(axis))])


def shards(recording, offsets, band_bins, dead_flags):
    channels, block_len = recording.shape
    windows = block_len // (L // 2)
    bins = band_bins.shape[0]
    chan_count, tm_count = lax.axis_size("chan"), lax.axis_size("tm")
    halves = tm_count // chan_count
    rim = L // 2 + L // 4
    cut = min(pl.cdiv(rim, STEP) * STEP, block_len)
    rim = L // 2 + L // 4
    cut = pl.cdiv(rim, STEP) * STEP
    own, back, state = spectra_of(recording, offsets, band_bins, dead_flags, windows, cut)
    more = moved(back, "tm", 1)
    rest = rest_of(recording, state, bins, windows, cut)
    white = whiten(own, rest, more, bins, windows, halves)
    row_blocks = [white] + [from_partner(white, "tm", away) for away in range(2, tm_count, 2)]
    chan_blocks = chan_blocks_of(white)
    joined, col_blocks = picked(row_blocks, chan_blocks, tm_count)
    for away in partners(tm_count):
        col_blocks[away] = from_partner(col_blocks[away], "tm", away)
    return stacks_of(col_blocks, [joined, from_partner(joined, "tm", 1)], bins, windows)


def solution(mesh):
    placed = (P("chan", "tm"), P(), P(), P("chan"))
    return jax.shard_map(
        shards, mesh=mesh, in_specs=placed, out_specs=P(None, None, "tm", "chan"), check_vma=False
    )
```

```python
import functools
import math

import jax
import jax.numpy as jnp
from jax import lax
from jax.experimental import pallas as pl
from jax.experimental.pallas import tpu as pltpu
from jax.sharding import PartitionSpec as P

L = 15000
FLOOR = 0.7
F32 = jnp.float32
BF16 = jnp.bfloat16
LANE = 128
DEPTH = 256
STEP = 1024
ROW_TILE = 16


def cos_sin(turns, length):
    quarter = jnp.floor(turns * (4.0 / length) + 0.5)
    angle = (turns * 4.0 - quarter * length) * (math.pi / (2.0 * length))
    square = angle * angle
    sine = angle * (
        1.0 + square * (-1.0 / 6 + square * (1.0 / 120 + square * (-1.0 / 5040 + square * (1.0 / 362880))))
    )
    cosine = 1.0 + square * (
        -0.5 + square * (1.0 / 24 + square * (-1.0 / 720 + square * (1.0 / 40320)))
    )
    quadrant = quarter - 4.0 * jnp.floor(quarter * 0.25)
    odd = (quadrant == 1.0) | (quadrant == 3.0)
    cos_sign = jnp.where((quadrant == 1.0) | (quadrant == 2.0), -1.0, 1.0)
    sin_sign = jnp.where(quadrant >= 2.0, -1.0, 1.0)
    return cos_sign * jnp.where(odd, sine, cosine), sin_sign * jnp.where(odd, cosine, sine)


def load_samples(x_hbm, x_ref, x_sems, low_end, size):
    return [
        pltpu.make_async_copy(
            x_hbm.at[pl.ds(low_end + i, min(STEP, size - i))], x_ref.at[pl.ds(i, min(STEP, size - i))],
            x_sems.at[i // STEP],
        )
        for i in range(0, size, STEP)
    ]


def make_tables(table, state, place, first, count, windows_rows):
    rows = table.shape[0]
    for r in range(0, rows, ROW_TILE):
        halves = (slice(r, r + 8), slice(r + 8, r + 16))
        now = [(state[0, at, :], state[1, at, :]) for at in halves]
        turn = [(state[2, at, :], state[3, at, :]) for at in halves]
        spot = None if place is None else [place[at, :] for at in halves]
        for j in range(count):
            moved = ((first + j) * DEPTH).astype(F32)
            values = [u for u, _ in now]
            if place is not None:
                values = [
                    jnp.where(where >= (-moved if at.start < windows_rows else moved), u, 0.0)
                    for at, where, u in zip(halves, spot, values)
                ]
            to_lanes = pl.ds(pl.multiple_of((first + j) * DEPTH, DEPTH), DEPTH)
            table[r:r + ROW_TILE, to_lanes] = jnp.concatenate(values, axis=0).astype(BF16)
            now = [(u * ct - v * st, v * ct + u * st) for (u, v), (ct, st) in zip(now, turn)]
        for at, (u, v) in zip(halves, now):
            state[0, at, :], state[1, at, :] = u, v


def add_products(table, x_ref, acc, base, size, row_range, energy_at):
    view = x_ref.at[pl.ds(base, size)]
    waves = table.at[:, pl.ds(base, size)]
    low, high = row_range
    channels = x_ref.shape[1]
    for n in range(0, channels, DEPTH):
        at = slice(n, min(n + DEPTH, channels))
        if energy_at is not None:
            total = squares(view, 0, 2, at)
            for t in range(2, size // ROW_TILE, 2):
                total = total + squares(view, t, 2, at)
        product = jnp.dot(waves[low:high, :], view[:, at], preferred_element_type=F32)
        acc[low:high, at] += product
        if energy_at is not None:
            energy_at[:, at] = total


def squares(view, first, count, at):
    total = None
    for t in range(first, first + count):
        x = view[t * ROW_TILE:(t + 1) * ROW_TILE, at]
        total = x * x if total is None else total + x * x
    total = total.astype(F32)
    return total[:ROW_TILE // 2] + total[ROW_TILE // 2:]


def mix_windows(out_ref, acc, first, windows, per_window, per_group):
    for w in range(windows):
        own_at = first + (windows - 1 - w) * per_window
        for q in range(0, per_window, per_group):
            to = q * windows + w * per_group
            out_ref[to:to + per_group, :] = acc[own_at + q:own_at + q + per_group, :]


def spectra_kernel(
    bins, windows, block_len, high_end,
    offsets_hbm, bins_hbm, dead_hbm, x_hbm, own_ref, back_ref, state_ref,
    offsets, band_bins, dead, x_ref, acc, seg, part_seg, mixed, state, place, table, small_sems, x_sems,
):
    channels = x_ref.shape[1]
    length, hop = L, L // 2
    per_window = 2 * bins
    rows = windows * per_window
    half_tile = ROW_TILE // 2
    per_group = half_tile // windows
    steps = high_end // STEP

    small = [
        pltpu.make_async_copy(offsets_hbm, offsets, small_sems.at[0]),
        pltpu.make_async_copy(bins_hbm, band_bins, small_sems.at[1]),
        pltpu.make_async_copy(dead_hbm, dead, small_sems.at[2]),
    ]
    for copy in small:
        copy.start()
    loads = load_samples(x_hbm, x_ref, x_sems, 0, high_end)
    loads[0].start()
    for copy in small:
        copy.wait()
    for copy in loads[1:]:
        copy.start()

    tm = lax.axis_index("tm")
    ahead = [offsets[tm * windows + w] + w * hop for w in range(windows)]
    before = jnp.maximum(tm - 1, 0) * windows
    behind = [offsets[before + w] + w * hop + length - block_len for w in range(windows)]
    ends = []
    for w in range(windows):
        ends += [jnp.minimum(ahead[w], behind[w]), jnp.maximum(ahead[w], behind[w])]
    segments = len(ends) + 1
    trash = segments

    shape = (half_tile, DEPTH)
    lane = lax.broadcasted_iota(jnp.int32, shape, 1).astype(F32)
    norm = 1.0 / math.sqrt(length)
    for r in range(0, 2 * rows, half_tile):
        at = slice(r, r + half_tile)
        row = lax.broadcasted_iota(jnp.int32, shape, 0) + r
        block, inner = row // per_window, row % per_window
        part = inner // per_group % 2
        bin_index = inner // (2 * per_group) * per_group + inner % per_group
        tone = jnp.zeros(shape, jnp.int32)
        for b in range(bins):
            if r // per_window != (r + half_tile - 1) // per_window or (
                r % per_window // (2 * per_group) * per_group <= b
                < (r % per_window + half_tile - 1) // (2 * per_group) * per_group + per_group
            ):
                tone = jnp.where(bin_index == b, band_bins[b], tone)
        start = jnp.zeros(shape, jnp.int32)
        for w in range(windows):
            start = jnp.where(block == windows - 1 - w, ahead[w], start)
            start = jnp.where(block == 2 * windows - 1 - w, behind[w] - length, start)
        tone, start = tone.astype(F32), start.astype(F32)
        cosine, sine = cos_sin((lane - start) * tone, length)
        state[0, at, :] = jnp.where(part == 1, -sine, cosine) * norm
        state[1, at, :] = jnp.where(part == 1, cosine, sine) * norm
        state[2, at, :], state[3, at, :] = cos_sin(tone * DEPTH, length)
        place[at, :] = lane - start if r < rows else start + (length - 1) - lane
    acc[...] = jnp.zeros_like(acc)
    seg[...] = jnp.zeros_like(seg)

    def segment_of(position):
        index = jnp.int32(0)
        for end in ends:
            index += (end <= position).astype(jnp.int32)
        return index

    def has_end(first, size):
        found = jnp.bool_(False)
        for end in ends:
            found = jnp.logical_or(found, jnp.logical_and(end >= first, end < first + size))
        return found

    def body(base, row_range, edge):
        add_products(table, x_ref, acc, base, STEP, row_range, None if edge else part_seg)
        if not edge:
            seg[segment_of(base)] += part_seg[...]
            return
        view = x_ref.at[pl.ds(base, STEP)]
        for t in range(STEP // ROW_TILE):
            first = base + t * ROW_TILE
            target = jnp.where(has_end(first, ROW_TILE), trash, segment_of(first))
            for n in range(0, channels, DEPTH):
                at = slice(n, min(n + DEPTH, channels))
                seg[target, :, at] += squares(view, t, 1, at)

    def reach(i):
        low, high = i * STEP, (i + 1) * STEP
        own = [w for w in range(windows) if w * hop < high]
        back = [w for w in range(windows) if w * hop + hop // 2 + length - block_len > low]
        first = (windows - 1 - max(own)) * per_window // ROW_TILE * ROW_TILE
        last = (2 * windows - min(back, default=windows)) * per_window
        edges = any(
            w * hop + shift < high and w * hop + hop // 2 + shift > low
            for w in range(windows) for shift in (0, length - block_len)
        )
        return (first, min(pl.cdiv(last, ROW_TILE) * ROW_TILE, 2 * rows)), edges

    kinds = [reach(i) for i in range(steps)]
    i = 0
    while i < steps:
        until = i
        while until < steps and kinds[until] == kinds[i]:
            until += 1
        row_range, edges = kinds[i]

        @pl.loop(i, until)
        def _(step):
            base = pl.multiple_of(step * STEP, STEP)
            make_tables(table, state, place, step * (STEP // DEPTH), STEP // DEPTH, rows)
            at = pl.ds(base, STEP)
            pltpu.make_async_copy(x_hbm.at[at], x_ref.at[at], x_sems.at[step]).wait()
            if not edges:
                body(base, row_range, False)
                return
            cut = has_end(base, STEP)

            @pl.when(jnp.logical_not(cut))
            def _():
                body(base, row_range, False)

            @pl.when(cut)
            def _():
                body(base, row_range, True)

        i = until

    for i, end in enumerate(ends):
        low = ends[i - 1] if i else jnp.int32(0)
        high = ends[i + 1] if i + 1 < len(ends) else jnp.int32(high_end)
        tile = end // ROW_TILE
        x = x_ref[pl.ds(pl.multiple_of(tile * ROW_TILE, ROW_TILE), ROW_TILE), :].astype(F32)
        spot = lax.broadcasted_iota(jnp.int32, x.shape, 0) + tile * ROW_TILE
        under = jnp.logical_and(spot >= low, spot < end)
        over = jnp.logical_and(spot >= end, spot < high)
        over = jnp.logical_and(over, high // ROW_TILE != tile)
        square = x * x
        for where, index in ((under, i), (over, i + 1)):
            kept = jnp.where(where, square, 0.0)
            seg[index] += kept[:half_tile] + kept[half_tile:]

    state_ref[...] = state[:, :rows, :]
    mix_windows(own_ref, acc, 0, windows, per_window, per_group)
    mix_windows(mixed, acc, rows, windows, per_window, per_group)
    back_ref[:rows, :] = mixed[...].astype(BF16)
    parts = [seg[i] for i in range(segments)]
    row = lax.broadcasted_iota(jnp.int32, (half_tile, channels), 0)
    own_block = jnp.where(row == windows, (1 - dead[...]).astype(F32), 0.0)
    back_block = jnp.zeros((ROW_TILE, channels), F32)
    back_row = lax.broadcasted_iota(jnp.int32, (ROW_TILE, channels), 0)
    for w in range(windows):
        turn = jnp.where(ahead[w] <= behind[w], parts[2 * w + 1], 0.0)
        own_energy = jnp.sum(sum(parts[2 * w + 2:]) + turn, axis=0, keepdims=True)
        own_block = jnp.where(row == w, own_energy, own_block)
        rest = jnp.sum(sum(parts[:2 * w + 1]) + turn, axis=0, keepdims=True)
        for term in range(3):
            piece_of = rest.astype(BF16).astype(F32)
            rest = rest - piece_of
            back_block = jnp.where(back_row == term * windows + w, piece_of, back_block)
    own_ref[rows:, :] = own_block
    back_ref[rows:, :] = back_block.astype(BF16)


def rest_kernel(
    bins, windows, block_len, low_end, state_in, x_hbm, tail_ref, own_ref,
    x_ref, acc, part_seg, total_seg, state, table, x_sems,
):
    channels = x_ref.shape[1]
    per_window = 2 * bins
    rows = windows * per_window
    half_tile = ROW_TILE // 2
    count = block_len - low_end
    bulk = count // ROW_TILE * ROW_TILE
    padded = x_ref.shape[0]
    loads = load_samples(x_hbm, x_ref, x_sems, low_end, bulk)
    for copy in loads:
        copy.start()
    state[...] = state_in[...]
    acc[...] = jnp.zeros_like(acc)
    total_seg[...] = jnp.zeros_like(total_seg)
    if padded > bulk:
        x_ref[bulk:, :] = jnp.zeros((padded - bulk, channels), BF16)
    if count > bulk:
        inside = lax.broadcasted_iota(jnp.int32, (ROW_TILE, channels), 0) < count - bulk
        x_ref[bulk:bulk + ROW_TILE, :] = jnp.where(inside, tail_ref[...].astype(F32), 0.0).astype(BF16)
    for i in range(0, padded, STEP):
        size = min(STEP, padded - i)
        make_tables(table, state, None, jnp.int32(i // DEPTH), size // DEPTH, rows)
        if i // STEP < len(loads):
            loads[i // STEP].wait()
        add_products(table, x_ref, acc, i, size, (0, rows), part_seg)
        total_seg[...] += part_seg[...]
    mix_windows(own_ref, acc, 0, windows, per_window, half_tile // windows)
    energy = jnp.sum(total_seg[...], axis=0, keepdims=True)
    row = lax.broadcasted_iota(jnp.int32, (half_tile, channels), 0)
    own_ref[rows:, :] = jnp.where(row < windows, energy, 0.0)


def spectra_of(recording, offsets, band_bins, dead, windows, high_end):
    channels, block_len = recording.shape
    bins = band_bins.shape[0]
    rows = bins * windows * 2
    samples = recording.T
    hbm = pl.BlockSpec(memory_space=pltpu.HBM)
    whole = pl.BlockSpec(memory_space=pltpu.VMEM)
    return pl.pallas_call(
        functools.partial(spectra_kernel, bins, windows, block_len, high_end),
        out_shape=[
            jax.ShapeDtypeStruct((rows + ROW_TILE // 2, channels), F32),
            jax.ShapeDtypeStruct((rows + ROW_TILE, channels), BF16),
            jax.ShapeDtypeStruct((4, rows, DEPTH), F32),
        ],
        in_specs=[hbm, hbm, hbm, hbm],
        out_specs=[whole] * 3,
        scratch_shapes=[
            pltpu.SMEM(offsets.shape, jnp.int32),
            pltpu.SMEM(band_bins.shape, jnp.int32),
            pltpu.VMEM((1, channels), jnp.int32),
            pltpu.VMEM((high_end, channels), BF16),
            pltpu.VMEM((2 * rows, channels), F32),
            pltpu.VMEM((2 * windows + 2, ROW_TILE // 2, channels), F32),
            pltpu.VMEM((ROW_TILE // 2, channels), F32),
            pltpu.VMEM((rows, channels), F32),
            pltpu.VMEM((4, 2 * rows, DEPTH), F32),
            pltpu.VMEM((2 * rows, DEPTH), F32),
            pltpu.VMEM((2 * rows, high_end), BF16),
            pltpu.SemaphoreType.DMA((3,)),
            pltpu.SemaphoreType.DMA((high_end // STEP,)),
        ],
        compiler_params=pltpu.CompilerParams(vmem_limit_bytes=60 * 2**20),
        cost_estimate=pl.CostEstimate(
            flops=2 * channels * high_end * 2 * rows, bytes_accessed=channels * high_end * 2, transcendentals=0
        ),
        name="band_spectra",
    )(offsets, band_bins, dead.reshape(1, channels), samples)


def rest_of(recording, state, bins, windows, low_end):
    channels, block_len = recording.shape
    rows = bins * windows * 2
    count = block_len - low_end
    padded = pl.cdiv(count, DEPTH) * DEPTH
    bulk = count // ROW_TILE * ROW_TILE
    tail = min(low_end + bulk, block_len - 1) // ROW_TILE
    samples = recording.T
    whole = pl.BlockSpec(memory_space=pltpu.VMEM)
    return pl.pallas_call(
        functools.partial(rest_kernel, bins, windows, block_len, low_end),
        out_shape=jax.ShapeDtypeStruct((rows + ROW_TILE // 2, channels), F32),
        grid=(1,),
        in_specs=[
            whole,
            pl.BlockSpec(memory_space=pltpu.HBM),
            pl.BlockSpec((ROW_TILE, channels), lambda i: (tail, 0)),
        ],
        out_specs=whole,
        scratch_shapes=[
            pltpu.VMEM((padded, channels), BF16),
            pltpu.VMEM((rows, channels), F32),
            pltpu.VMEM((ROW_TILE // 2, channels), F32),
            pltpu.VMEM((ROW_TILE // 2, channels), F32),
            pltpu.VMEM((4, rows, DEPTH), F32),
            pltpu.VMEM((rows, padded), BF16),
            pltpu.SemaphoreType.DMA((pl.cdiv(padded, STEP),)),
        ],
        compiler_params=pltpu.CompilerParams(vmem_limit_bytes=24 * 2**20),
        cost_estimate=pl.CostEstimate(
            flops=2 * channels * count * rows, bytes_accessed=channels * count * 2, transcendentals=0
        ),
        name="band_spectra_rest",
    )(state, samples, samples)


def whiten_kernel(bins, windows, own_ref, rest_ref, more_ref, white_ref):
    rows = bins * windows * 2
    more = more_ref[...].astype(F32)
    raw = own_ref[:rows, :] + rest_ref[:rows, :] + more[:rows]
    extra = more[rows:]
    per_group = ROW_TILE // (2 * windows)
    which = lax.broadcasted_iota(jnp.int32, (rows, 1), 0) // per_group % windows
    alive = own_ref[rows + windows:rows + windows + 1, :]
    scale = factor = None
    for w in range(windows):
        energy = own_ref[rows + w:rows + w + 1, :] + rest_ref[rows + w:rows + w + 1, :]
        for term in range(3):
            energy = energy + extra[term * windows + w:term * windows + w + 1, :]
        inverse = 1.0 / jnp.sqrt(energy / L + 1e-06)
        scale = inverse if w == 0 else jnp.where(which == w, inverse, scale)
    spectra = raw * scale
    power = spectra * spectra
    for w in range(windows):
        level = jnp.sum(jnp.where(which == w, power, 0.0), axis=0, keepdims=True) * (1.0 / bins)
        one = alive / jnp.sqrt(jnp.maximum(level, FLOOR))
        factor = one if w == 0 else jnp.where(which == w, one, factor)
    white = (spectra * factor).astype(BF16)
    width = white_ref.shape[2]
    for h in range(white_ref.shape[0]):
        white_ref[h] = white[:, h * width:(h + 1) * width]


def whiten(own, rest, more, bins, windows, halves):
    channels = own.shape[1]
    return pl.pallas_call(
        functools.partial(whiten_kernel, bins, windows),
        out_shape=jax.ShapeDtypeStruct((halves, bins * windows * 2, channels // halves), BF16),
        compiler_params=pltpu.CompilerParams(vmem_limit_bytes=12 * 2**20),
        name="whiten",
    )(own, rest, more)


def stack_kernel(windows, scale, devices, *refs):
    col_refs, row_refs = refs[:devices], refs[devices:devices + 2]
    out_hbm, lhs, held, made, sems = refs[devices + 2:]
    per_group = ROW_TILE // (2 * windows)
    step = pl.program_id(0)
    width = col_refs[0].shape[1]
    depth = devices * ROW_TILE
    _, halves, _, span = row_refs[0].shape
    channels = halves * span
    exact = math.frexp(scale)[0] == 0.5

    by_partner = dict(zip([0, *partners(devices)], col_refs))
    cols = jnp.stack([by_partner[away][...].astype(F32) for away in range(devices)])
    if exact:
        cols = cols * scale
    head, tail = cols[:, :ROW_TILE // 2], cols[:, ROW_TILE // 2:]
    straight = cols.reshape(depth, width)
    turned = jnp.concatenate([-tail, head], axis=1).reshape(depth, width)
    lhs[:width, :] = straight.T.astype(BF16)
    lhs[width:, :] = turned.T.astype(BF16)
    for away in range(devices):
        to = slice(away * ROW_TILE, (away + 1) * ROW_TILE)
        for h in range(halves):
            held[to, h * span:(h + 1) * span] = row_refs[away % 2][away // 2, h].astype(F32)

    def out_copy(slot, part, bin_index):
        to = out_hbm.at[part, bin_index]
        return pltpu.make_async_copy(made.at[slot], to, sems.at[slot])

    which = lax.broadcasted_iota(jnp.int32, (depth, 1), 0) % per_group
    for b in range(per_group):
        for part in range(2):
            slot = 2 * b + part

            @pl.when(step > 0)
            def _():
                out_copy(slot, part, (step - 1) * per_group + b).wait()

        for n in range(0, channels, DEPTH):
            at = slice(n, min(n + DEPTH, channels))
            rhs = jnp.where(which == b, held[:, at], 0.0).astype(BF16)
            for part in range(2):
                product = jnp.dot(
                    lhs[part * width:(part + 1) * width, :], rhs, preferred_element_type=F32
                )
                if not exact:
                    product = product * scale
                made[2 * b + part, :, at] = product.astype(BF16)
        for part in range(2):
            out_copy(2 * b + part, part, step * per_group + b).start()

    @pl.when(step == pl.num_programs(0) - 1)
    def _():
        for b in range(per_group):
            for part in range(2):
                out_copy(2 * b + part, part, step * per_group + b).wait()


def stacks_of(col_blocks, row_blocks, bins, windows):
    devices = len(col_blocks)
    chips, halves, _, span = row_blocks[0].shape
    width = col_blocks[0].shape[1]
    per_group = ROW_TILE // (2 * windows)
    scale = 1.0 / math.sqrt(windows * devices)
    channels = halves * span
    return pl.pallas_call(
        functools.partial(stack_kernel, windows, scale, devices),
        out_shape=jax.ShapeDtypeStruct((2, bins, width, channels), BF16),
        grid=(bins // per_group,),
        in_specs=[pl.BlockSpec((ROW_TILE, width), lambda i: (i, 0))] * devices
        + [pl.BlockSpec((chips, halves, ROW_TILE, span), lambda i: (0, 0, i, 0))] * 2,
        out_specs=pl.BlockSpec(memory_space=pltpu.HBM),
        scratch_shapes=[
            pltpu.VMEM((2 * width, devices * ROW_TILE), BF16),
            pltpu.VMEM((devices * ROW_TILE, channels), F32),
            pltpu.VMEM((2 * per_group, width, channels), BF16),
            pltpu.SemaphoreType.DMA((2 * per_group,)),
        ],
        compiler_params=pltpu.CompilerParams(
            dimension_semantics=("arbitrary",), vmem_limit_bytes=24 * 2**20
        ),
        cost_estimate=pl.CostEstimate(
            flops=2 * 2 * bins * width * channels * devices * ROW_TILE,
            bytes_accessed=2 * bins * width * channels * 2,
            transcendentals=0,
        ),
        name="stack_products",
    )(*[col_blocks[away] for away in [0, *partners(devices)]], *row_blocks)


def pick_kernel(count, chips, *refs):
    row_refs, chan_refs = refs[:chips], refs[chips:-2 - count]
    joined_ref, out_refs, held = refs[-2 - count], refs[-1 - count:-1], refs[-1]
    tm, mine = lax.axis_index("tm"), lax.axis_index("chan")
    halves = row_refs[0].shape[0]
    for i, ref in enumerate(row_refs):
        joined_ref[i] = ref[...]
    for away, ref in enumerate((row_refs[0], *chan_refs)):
        held[jnp.bitwise_xor(mine, away)] = ref[...]
    for away, out_ref in enumerate(out_refs):
        wanted = jnp.bitwise_xor(tm, away)
        out_ref[...] = held[wanted // halves, wanted % halves]


def picked(row_blocks, chan_blocks, count):
    block = row_blocks[0]
    _, rows, width = block.shape
    chips = len(row_blocks)
    whole = pl.BlockSpec(memory_space=pltpu.VMEM)
    joined, *picks = pl.pallas_call(
        functools.partial(pick_kernel, count, chips),
        out_shape=[jax.ShapeDtypeStruct((chips, *block.shape), block.dtype)]
        + [jax.ShapeDtypeStruct((rows, width), block.dtype)] * count,
        in_specs=[whole] * (chips + len(chan_blocks)),
        out_specs=[whole] * (1 + count),
        scratch_shapes=[pltpu.VMEM((1 + len(chan_blocks), *block.shape), block.dtype)],
        compiler_params=pltpu.CompilerParams(vmem_limit_bytes=16 * 2**20),
        name="pick_blocks",
    )(*row_blocks, *chan_blocks)
    return joined, picks


def moved(block, axis, far):
    count = lax.axis_size(axis)
    return lax.ppermute(block, axis, [(i + far, i) for i in range(count) if 0 <= i + far < count])


def partners(count):
    return [*range(2, count, 2), *range(3, count, 2), 1]


def chan_blocks_of(block):
    count = lax.axis_size("chan")
    blocks = {0: block}
    for away in range(1, count):
        near = away & -away
        blocks[away] = from_partner(blocks[away ^ near], "chan", near)
    return [blocks[away] for away in range(1, count)]


def from_partner(block, axis, away):
    return lax.ppermute(block, axis, [(i, i ^ away) for i in range(lax.axis_size(axis))])


def shards(recording, offsets, band_bins, dead_flags):
    channels, block_len = recording.shape
    windows = block_len // (L // 2)
    bins = band_bins.shape[0]
    chan_count, tm_count = lax.axis_size("chan"), lax.axis_size("tm")
    halves = tm_count // chan_count
    rim = L // 2 + L // 4
    cut = min(pl.cdiv(rim, STEP) * STEP, block_len)
    rim = L // 2 + L // 4
    cut = pl.cdiv(rim, STEP) * STEP
    own, back, state = spectra_of(recording, offsets, band_bins, dead_flags, windows, cut)
    more = moved(back, "tm", 1)
    rest = rest_of(recording, state, bins, windows, cut)
    white = whiten(own, rest, more, bins, windows, halves)
    row_blocks = [white] + [from_partner(white, "tm", away) for away in range(2, tm_count, 2)]
    chan_blocks = chan_blocks_of(white)
    joined, col_blocks = picked(row_blocks, chan_blocks, tm_count)
    for away in partners(tm_count):
        col_blocks[away] = from_partner(col_blocks[away], "tm", away)
    return stacks_of(col_blocks, [joined, from_partner(joined, "tm", 1)], bins, windows)


def solution(mesh):
    placed = (P("chan", "tm"), P(), P(), P("chan"))
    return jax.shard_map(
        shards, mesh=mesh, in_specs=placed, out_specs=P(None, None, "tm", "chan"), check_vma=False
    )
```

```python
import functools
import math

import jax
import jax.numpy as jnp
from jax import lax
from jax.experimental import pallas as pl
from jax.experimental.pallas import tpu as pltpu
from jax.sharding import PartitionSpec as P

L = 15000
FLOOR = 0.7
F32 = jnp.float32
BF16 = jnp.bfloat16
LANE = 128
DEPTH = 256
STEP = 1024
ROW_TILE = 16


def cos_sin(turns, length):
    quarter = jnp.floor(turns * (4.0 / length) + 0.5)
    angle = (turns * 4.0 - quarter * length) * (math.pi / (2.0 * length))
    square = angle * angle
    sine = angle * (
        1.0 + square * (-1.0 / 6 + square * (1.0 / 120 + square * (-1.0 / 5040 + square * (1.0 / 362880))))
    )
    cosine = 1.0 + square * (
        -0.5 + square * (1.0 / 24 + square * (-1.0 / 720 + square * (1.0 / 40320)))
    )
    quadrant = quarter - 4.0 * jnp.floor(quarter * 0.25)
    odd = (quadrant == 1.0) | (quadrant == 3.0)
    cos_sign = jnp.where((quadrant == 1.0) | (quadrant == 2.0), -1.0, 1.0)
    sin_sign = jnp.where(quadrant >= 2.0, -1.0, 1.0)
    return cos_sign * jnp.where(odd, sine, cosine), sin_sign * jnp.where(odd, cosine, sine)


def load_samples(x_hbm, x_ref, x_sems, low_end, size):
    return [
        pltpu.make_async_copy(
            x_hbm.at[pl.ds(low_end + i, min(STEP, size - i))], x_ref.at[pl.ds(i, min(STEP, size - i))],
            x_sems.at[i // STEP],
        )
        for i in range(0, size, STEP)
    ]


def make_tables(table, state, place, first, count, windows_rows):
    rows = table.shape[0]
    for r in range(0, rows, ROW_TILE):
        halves = (slice(r, r + 8), slice(r + 8, r + 16))
        now = [(state[0, at, :], state[1, at, :]) for at in halves]
        turn = [(state[2, at, :], state[3, at, :]) for at in halves]
        spot = None if place is None else [place[at, :] for at in halves]
        for j in range(count):
            moved = ((first + j) * DEPTH).astype(F32)
            values = [u for u, _ in now]
            if place is not None:
                values = [
                    jnp.where(where >= (-moved if at.start < windows_rows else moved), u, 0.0)
                    for at, where, u in zip(halves, spot, values)
                ]
            to_lanes = pl.ds(pl.multiple_of((first + j) * DEPTH, DEPTH), DEPTH)
            table[r:r + ROW_TILE, to_lanes] = jnp.concatenate(values, axis=0).astype(BF16)
            now = [(u * ct - v * st, v * ct + u * st) for (u, v), (ct, st) in zip(now, turn)]
        for at, (u, v) in zip(halves, now):
            state[0, at, :], state[1, at, :] = u, v


def add_products(table, x_ref, acc, base, size, row_range, energy_at):
    view = x_ref.at[pl.ds(base, size)]
    waves = table.at[:, pl.ds(base, size)]
    low, high = row_range
    channels = x_ref.shape[1]
    for n in range(0, channels, DEPTH):
        at = slice(n, min(n + DEPTH, channels))
        if energy_at is not None:
            total = squares(view, 0, 2, at)
            for t in range(2, size // ROW_TILE, 2):
                total = total + squares(view, t, 2, at)
        product = jnp.dot(waves[low:high, :], view[:, at], preferred_element_type=F32)
        acc[low:high, at] += product
        if energy_at is not None:
            energy_at[:, at] = total


def squares(view, first, count, at):
    total = None
    for t in range(first, first + count):
        x = view[t * ROW_TILE:(t + 1) * ROW_TILE, at]
        total = x * x if total is None else total + x * x
    total = total.astype(F32)
    return total[:ROW_TILE // 2] + total[ROW_TILE // 2:]


def mix_windows(out_ref, acc, first, windows, per_window, per_group):
    for w in range(windows):
        own_at = first + (windows - 1 - w) * per_window
        for q in range(0, per_window, per_group):
            to = q * windows + w * per_group
            out_ref[to:to + per_group, :] = acc[own_at + q:own_at + q + per_group, :]


def spectra_kernel(
    bins, windows, block_len, high_end,
    offsets_hbm, bins_hbm, dead_hbm, x_hbm, own_ref, back_ref, state_ref,
    offsets, band_bins, dead, x_ref, acc, seg, part_seg, mixed, state, place, table, small_sems, x_sems,
):
    channels = x_ref.shape[1]
    length, hop = L, L // 2
    per_window = 2 * bins
    rows = windows * per_window
    half_tile = ROW_TILE // 2
    per_group = half_tile // windows
    steps = high_end // STEP

    small = [
        pltpu.make_async_copy(offsets_hbm, offsets, small_sems.at[0]),
        pltpu.make_async_copy(bins_hbm, band_bins, small_sems.at[1]),
        pltpu.make_async_copy(dead_hbm, dead, small_sems.at[2]),
    ]
    for copy in small:
        copy.start()
    loads = load_samples(x_hbm, x_ref, x_sems, 0, high_end)
    loads[0].start()
    for copy in small:
        copy.wait()
    for copy in loads[1:]:
        copy.start()

    tm = lax.axis_index("tm")
    ahead = [offsets[tm * windows + w] + w * hop for w in range(windows)]
    before = jnp.maximum(tm - 1, 0) * windows
    behind = [offsets[before + w] + w * hop + length - block_len for w in range(windows)]
    ends = []
    for w in range(windows):
        ends += [jnp.minimum(ahead[w], behind[w]), jnp.maximum(ahead[w], behind[w])]
    segments = len(ends) + 1
    trash = segments

    shape = (half_tile, DEPTH)
    lane = lax.broadcasted_iota(jnp.int32, shape, 1).astype(F32)
    norm = 1.0 / math.sqrt(length)
    for r in range(0, 2 * rows, half_tile):
        at = slice(r, r + half_tile)
        row = lax.broadcasted_iota(jnp.int32, shape, 0) + r
        block, inner = row // per_window, row % per_window
        part = inner // per_group % 2
        bin_index = inner // (2 * per_group) * per_group + inner % per_group
        tone = jnp.zeros(shape, jnp.int32)
        for b in range(bins):
            if r // per_window != (r + half_tile - 1) // per_window or (
                r % per_window // (2 * per_group) * per_group <= b
                < (r % per_window + half_tile - 1) // (2 * per_group) * per_group + per_group
            ):
                tone = jnp.where(bin_index == b, band_bins[b], tone)
        start = jnp.zeros(shape, jnp.int32)
        for w in range(windows):
            start = jnp.where(block == windows - 1 - w, ahead[w], start)
            start = jnp.where(block == 2 * windows - 1 - w, behind[w] - length, start)
        tone, start = tone.astype(F32), start.astype(F32)
        cosine, sine = cos_sin((lane - start) * tone, length)
        state[0, at, :] = jnp.where(part == 1, -sine, cosine) * norm
        state[1, at, :] = jnp.where(part == 1, cosine, sine) * norm
        state[2, at, :], state[3, at, :] = cos_sin(tone * DEPTH, length)
        place[at, :] = lane - start if r < rows else start + (length - 1) - lane
    acc[...] = jnp.zeros_like(acc)
    seg[...] = jnp.zeros_like(seg)

    def segment_of(position):
        index = jnp.int32(0)
        for end in ends:
            index += (end <= position).astype(jnp.int32)
        return index

    def has_end(first, size):
        found = jnp.bool_(False)
        for end in ends:
            found = jnp.logical_or(found, jnp.logical_and(end >= first, end < first + size))
        return found

    def body(base, row_range, edge):
        add_products(table, x_ref, acc, base, STEP, row_range, None if edge else part_seg)
        if not edge:
            seg[segment_of(base)] += part_seg[...]
            return
        view = x_ref.at[pl.ds(base, STEP)]
        for t in range(STEP // ROW_TILE):
            first = base + t * ROW_TILE
            target = jnp.where(has_end(first, ROW_TILE), trash, segment_of(first))
            for n in range(0, channels, DEPTH):
                at = slice(n, min(n + DEPTH, channels))
                seg[target, :, at] += squares(view, t, 1, at)

    def reach(i):
        low, high = i * STEP, (i + 1) * STEP
        own = [w for w in range(windows) if w * hop < high]
        back = [w for w in range(windows) if w * hop + hop // 2 + length - block_len > low]
        first = (windows - 1 - max(own)) * per_window // ROW_TILE * ROW_TILE
        last = (2 * windows - min(back, default=windows)) * per_window
        edges = any(
            w * hop + shift < high and w * hop + hop // 2 + shift > low
            for w in range(windows) for shift in (0, length - block_len)
        )
        return (first, min(pl.cdiv(last, ROW_TILE) * ROW_TILE, 2 * rows)), edges

    kinds = [reach(i) for i in range(steps)]
    i = 0
    while i < steps:
        until = i
        while until < steps and kinds[until] == kinds[i]:
            until += 1
        row_range, edges = kinds[i]

        @pl.loop(i, until)
        def _(step):
            base = pl.multiple_of(step * STEP, STEP)
            make_tables(table, state, place, step * (STEP // DEPTH), STEP // DEPTH, rows)
            at = pl.ds(base, STEP)
            pltpu.make_async_copy(x_hbm.at[at], x_ref.at[at], x_sems.at[step]).wait()
            if not edges:
                body(base, row_range, False)
                return
            cut = has_end(base, STEP)

            @pl.when(jnp.logical_not(cut))
            def _():
                body(base, row_range, False)

            @pl.when(cut)
            def _():
                body(base, row_range, True)

        i = until

    for i, end in enumerate(ends):
        low = ends[i - 1] if i else jnp.int32(0)
        high = ends[i + 1] if i + 1 < len(ends) else jnp.int32(high_end)
        tile = end // ROW_TILE
        x = x_ref[pl.ds(pl.multiple_of(tile * ROW_TILE, ROW_TILE), ROW_TILE), :].astype(F32)
        spot = lax.broadcasted_iota(jnp.int32, x.shape, 0) + tile * ROW_TILE
        under = jnp.logical_and(spot >= low, spot < end)
        over = jnp.logical_and(spot >= end, spot < high)
        over = jnp.logical_and(over, high // ROW_TILE != tile)
        square = x * x
        for where, index in ((under, i), (over, i + 1)):
            kept = jnp.where(where, square, 0.0)
            seg[index] += kept[:half_tile] + kept[half_tile:]

    state_ref[...] = state[:, :rows, :]
    mix_windows(own_ref, acc, 0, windows, per_window, per_group)
    mix_windows(mixed, acc, rows, windows, per_window, per_group)
    back_ref[:rows, :] = mixed[...].astype(BF16)
    parts = [seg[i] for i in range(segments)]
    row = lax.broadcasted_iota(jnp.int32, (half_tile, channels), 0)
    own_block = jnp.where(row == windows, (1 - dead[...]).astype(F32), 0.0)
    back_block = jnp.zeros((ROW_TILE, channels), F32)
    back_row = lax.broadcasted_iota(jnp.int32, (ROW_TILE, channels), 0)
    for w in range(windows):
        turn = jnp.where(ahead[w] <= behind[w], parts[2 * w + 1], 0.0)
        own_energy = jnp.sum(sum(parts[2 * w + 2:]) + turn, axis=0, keepdims=True)
        own_block = jnp.where(row == w, own_energy, own_block)
        rest = jnp.sum(sum(parts[:2 * w + 1]) + turn, axis=0, keepdims=True)
        for term in range(3):
            piece_of = rest.astype(BF16).astype(F32)
            rest = rest - piece_of
            back_block = jnp.where(back_row == term * windows + w, piece_of, back_block)
    own_ref[rows:, :] = own_block
    back_ref[rows:, :] = back_block.astype(BF16)


def rest_kernel(
    bins, windows, block_len, low_end, state_in, x_hbm, tail_ref, own_ref,
    x_ref, acc, part_seg, total_seg, state, table, x_sems,
):
    channels = x_ref.shape[1]
    per_window = 2 * bins
    rows = windows * per_window
    half_tile = ROW_TILE // 2
    count = block_len - low_end
    bulk = count // ROW_TILE * ROW_TILE
    padded = x_ref.shape[0]
    loads = load_samples(x_hbm, x_ref, x_sems, low_end, bulk)
    for copy in loads:
        copy.start()
    state[...] = state_in[...]
    acc[...] = jnp.zeros_like(acc)
    total_seg[...] = jnp.zeros_like(total_seg)
    if padded > bulk:
        x_ref[bulk:, :] = jnp.zeros((padded - bulk, channels), BF16)
    if count > bulk:
        inside = lax.broadcasted_iota(jnp.int32, (ROW_TILE, channels), 0) < count - bulk
        x_ref[bulk:bulk + ROW_TILE, :] = jnp.where(inside, tail_ref[...].astype(F32), 0.0).astype(BF16)
    for i in range(0, padded, STEP):
        size = min(STEP, padded - i)
        make_tables(table, state, None, jnp.int32(i // DEPTH), size // DEPTH, rows)
        if i // STEP < len(loads):
            loads[i // STEP].wait()
        add_products(table, x_ref, acc, i, size, (0, rows), part_seg)
        total_seg[...] += part_seg[...]
    mix_windows(own_ref, acc, 0, windows, per_window, half_tile // windows)
    energy = jnp.sum(total_seg[...], axis=0, keepdims=True)
    row = lax.broadcasted_iota(jnp.int32, (half_tile, channels), 0)
    own_ref[rows:, :] = jnp.where(row < windows, energy, 0.0)


def spectra_of(recording, offsets, band_bins, dead, windows, high_end):
    channels, block_len = recording.shape
    bins = band_bins.shape[0]
    rows = bins * windows * 2
    samples = recording.T
    hbm = pl.BlockSpec(memory_space=pltpu.HBM)
    whole = pl.BlockSpec(memory_space=pltpu.VMEM)
    return pl.pallas_call(
        functools.partial(spectra_kernel, bins, windows, block_len, high_end),
        out_shape=[
            jax.ShapeDtypeStruct((rows + ROW_TILE // 2, channels), F32),
            jax.ShapeDtypeStruct((rows + ROW_TILE, channels), BF16),
            jax.ShapeDtypeStruct((4, rows, DEPTH), F32),
        ],
        in_specs=[hbm, hbm, hbm, hbm],
        out_specs=[whole] * 3,
        scratch_shapes=[
            pltpu.SMEM(offsets.shape, jnp.int32),
            pltpu.SMEM(band_bins.shape, jnp.int32),
            pltpu.VMEM((1, channels), jnp.int32),
            pltpu.VMEM((high_end, channels), BF16),
            pltpu.VMEM((2 * rows, channels), F32),
            pltpu.VMEM((2 * windows + 2, ROW_TILE // 2, channels), F32),
            pltpu.VMEM((ROW_TILE // 2, channels), F32),
            pltpu.VMEM((rows, channels), F32),
            pltpu.VMEM((4, 2 * rows, DEPTH), F32),
            pltpu.VMEM((2 * rows, DEPTH), F32),
            pltpu.VMEM((2 * rows, high_end), BF16),
            pltpu.SemaphoreType.DMA((3,)),
            pltpu.SemaphoreType.DMA((high_end // STEP,)),
        ],
        compiler_params=pltpu.CompilerParams(vmem_limit_bytes=60 * 2**20),
        cost_estimate=pl.CostEstimate(
            flops=2 * channels * high_end * 2 * rows, bytes_accessed=channels * high_end * 2, transcendentals=0
        ),
        name="band_spectra",
    )(offsets, band_bins, dead.reshape(1, channels), samples)


def rest_of(recording, state, bins, windows, low_end):
    channels, block_len = recording.shape
    rows = bins * windows * 2
    count = block_len - low_end
    padded = pl.cdiv(count, DEPTH) * DEPTH
    bulk = count // ROW_TILE * ROW_TILE
    tail = min(low_end + bulk, block_len - 1) // ROW_TILE
    samples = recording.T
    whole = pl.BlockSpec(memory_space=pltpu.VMEM)
    return pl.pallas_call(
        functools.partial(rest_kernel, bins, windows, block_len, low_end),
        out_shape=jax.ShapeDtypeStruct((rows + ROW_TILE // 2, channels), F32),
        grid=(1,),
        in_specs=[
            whole,
            pl.BlockSpec(memory_space=pltpu.HBM),
            pl.BlockSpec((ROW_TILE, channels), lambda i: (tail, 0)),
        ],
        out_specs=whole,
        scratch_shapes=[
            pltpu.VMEM((padded, channels), BF16),
            pltpu.VMEM((rows, channels), F32),
            pltpu.VMEM((ROW_TILE // 2, channels), F32),
            pltpu.VMEM((ROW_TILE // 2, channels), F32),
            pltpu.VMEM((4, rows, DEPTH), F32),
            pltpu.VMEM((rows, padded), BF16),
            pltpu.SemaphoreType.DMA((pl.cdiv(padded, STEP),)),
        ],
        compiler_params=pltpu.CompilerParams(vmem_limit_bytes=24 * 2**20),
        cost_estimate=pl.CostEstimate(
            flops=2 * channels * count * rows, bytes_accessed=channels * count * 2, transcendentals=0
        ),
        name="band_spectra_rest",
    )(state, samples, samples)


def whiten_kernel(bins, windows, own_ref, rest_ref, more_ref, white_ref):
    rows = bins * windows * 2
    more = more_ref[...].astype(F32)
    raw = own_ref[:rows, :] + rest_ref[:rows, :] + more[:rows]
    extra = more[rows:]
    per_group = ROW_TILE // (2 * windows)
    which = lax.broadcasted_iota(jnp.int32, (rows, 1), 0) // per_group % windows
    alive = own_ref[rows + windows:rows + windows + 1, :]
    scale = factor = None
    for w in range(windows):
        energy = own_ref[rows + w:rows + w + 1, :] + rest_ref[rows + w:rows + w + 1, :]
        for term in range(3):
            energy = energy + extra[term * windows + w:term * windows + w + 1, :]
        inverse = 1.0 / jnp.sqrt(energy / L + 1e-06)
        scale = inverse if w == 0 else jnp.where(which == w, inverse, scale)
    spectra = raw * scale
    power = spectra * spectra
    for w in range(windows):
        level = jnp.sum(jnp.where(which == w, power, 0.0), axis=0, keepdims=True) * (1.0 / bins)
        one = alive / jnp.sqrt(jnp.maximum(level, FLOOR))
        factor = one if w == 0 else jnp.where(which == w, one, factor)
    white = (spectra * factor).astype(BF16)
    width = white_ref.shape[2]
    for h in range(white_ref.shape[0]):
        white_ref[h] = white[:, h * width:(h + 1) * width]


def whiten(own, rest, more, bins, windows, halves):
    channels = own.shape[1]
    return pl.pallas_call(
        functools.partial(whiten_kernel, bins, windows),
        out_shape=jax.ShapeDtypeStruct((halves, bins * windows * 2, channels // halves), BF16),
        compiler_params=pltpu.CompilerParams(vmem_limit_bytes=12 * 2**20),
        name="whiten",
    )(own, rest, more)


def stack_kernel(windows, scale, devices, *refs):
    col_refs, row_refs = refs[:devices], refs[devices:devices + 2]
    out_hbm, lhs, held, made, sems = refs[devices + 2:]
    per_group = ROW_TILE // (2 * windows)
    step = pl.program_id(0)
    width = col_refs[0].shape[1]
    depth = devices * ROW_TILE
    _, halves, _, span = row_refs[0].shape
    channels = halves * span
    exact = math.frexp(scale)[0] == 0.5

    by_partner = dict(zip([0, *partners(devices)], col_refs))
    cols = jnp.stack([by_partner[away][...].astype(F32) for away in range(devices)])
    if exact:
        cols = cols * scale
    head, tail = cols[:, :ROW_TILE // 2], cols[:, ROW_TILE // 2:]
    straight = cols.reshape(depth, width)
    turned = jnp.concatenate([-tail, head], axis=1).reshape(depth, width)
    bin_of = lax.broadcasted_iota(jnp.int32, (1, depth), 1) % per_group
    for part, block in enumerate((straight, turned)):
        turned_over = block.T
        for b in range(per_group):
            kept = jnp.where(bin_of == b, turned_over, 0.0).astype(BF16)
            lhs[b, part * width:(part + 1) * width, :] = kept
    for away in range(devices):
        to = slice(away * ROW_TILE, (away + 1) * ROW_TILE)
        for h in range(halves):
            held[to, h * span:(h + 1) * span] = row_refs[away % 2][away // 2, h]

    def out_copy(slot, part, bin_index):
        to = out_hbm.at[part, bin_index]
        return pltpu.make_async_copy(made.at[slot], to, sems.at[slot])

    for b in range(per_group):
        for part in range(2):
            slot = 2 * b + part

            @pl.when(step > 0)
            def _():
                out_copy(slot, part, (step - 1) * per_group + b).wait()

        for n in range(0, channels, DEPTH):
            at = slice(n, min(n + DEPTH, channels))
            product = jnp.dot(lhs[b], held[:, at], preferred_element_type=F32)
            if not exact:
                product = product * scale
            for part in range(2):
                made[2 * b + part, :, at] = product[part * width:(part + 1) * width].astype(BF16)
        for part in range(2):
            out_copy(2 * b + part, part, step * per_group + b).start()

    @pl.when(step == pl.num_programs(0) - 1)
    def _():
        for b in range(per_group):
            for part in range(2):
                out_copy(2 * b + part, part, step * per_group + b).wait()


def stacks_of(col_blocks, row_blocks, bins, windows):
    devices = len(col_blocks)
    chips, halves, _, span = row_blocks[0].shape
    width = col_blocks[0].shape[1]
    per_group = ROW_TILE // (2 * windows)
    scale = 1.0 / math.sqrt(windows * devices)
    channels = halves * span
    return pl.pallas_call(
        functools.partial(stack_kernel, windows, scale, devices),
        out_shape=jax.ShapeDtypeStruct((2, bins, width, channels), BF16),
        grid=(bins // per_group,),
        in_specs=[pl.BlockSpec((ROW_TILE, width), lambda i: (i, 0))] * devices
        + [pl.BlockSpec((chips, halves, ROW_TILE, span), lambda i: (0, 0, i, 0))] * 2,
        out_specs=pl.BlockSpec(memory_space=pltpu.HBM),
        scratch_shapes=[
            pltpu.VMEM((per_group, 2 * width, devices * ROW_TILE), BF16),
            pltpu.VMEM((devices * ROW_TILE, channels), BF16),
            pltpu.VMEM((2 * per_group, width, channels), BF16),
            pltpu.SemaphoreType.DMA((2 * per_group,)),
        ],
        compiler_params=pltpu.CompilerParams(
            dimension_semantics=("arbitrary",), vmem_limit_bytes=24 * 2**20
        ),
        cost_estimate=pl.CostEstimate(
            flops=2 * 2 * bins * width * channels * devices * ROW_TILE,
            bytes_accessed=2 * bins * width * channels * 2,
            transcendentals=0,
        ),
        name="stack_products",
    )(*[col_blocks[away] for away in [0, *partners(devices)]], *row_blocks)


def pick_kernel(count, chips, *refs):
    row_refs, chan_refs = refs[:chips], refs[chips:-2 - count]
    joined_ref, out_refs, held = refs[-2 - count], refs[-1 - count:-1], refs[-1]
    tm, mine = lax.axis_index("tm"), lax.axis_index("chan")
    halves = row_refs[0].shape[0]
    for i, ref in enumerate(row_refs):
        joined_ref[i] = ref[...]
    for away, ref in enumerate((row_refs[0], *chan_refs)):
        held[jnp.bitwise_xor(mine, away)] = ref[...]
    for away, out_ref in enumerate(out_refs):
        wanted = jnp.bitwise_xor(tm, away)
        out_ref[...] = held[wanted // halves, wanted % halves]


def picked(row_blocks, chan_blocks, count):
    block = row_blocks[0]
    _, rows, width = block.shape
    chips = len(row_blocks)
    whole = pl.BlockSpec(memory_space=pltpu.VMEM)
    joined, *picks = pl.pallas_call(
        functools.partial(pick_kernel, count, chips),
        out_shape=[jax.ShapeDtypeStruct((chips, *block.shape), block.dtype)]
        + [jax.ShapeDtypeStruct((rows, width), block.dtype)] * count,
        in_specs=[whole] * (chips + len(chan_blocks)),
        out_specs=[whole] * (1 + count),
        scratch_shapes=[pltpu.VMEM((1 + len(chan_blocks), *block.shape), block.dtype)],
        compiler_params=pltpu.CompilerParams(vmem_limit_bytes=16 * 2**20),
        name="pick_blocks",
    )(*row_blocks, *chan_blocks)
    return joined, picks


def moved(block, axis, far):
    count = lax.axis_size(axis)
    return lax.ppermute(block, axis, [(i + far, i) for i in range(count) if 0 <= i + far < count])


def partners(count):
    return sorted(range(1, count), key=lambda away: (-bin(away >> 1).count("1"), away % 2, away))


def chan_blocks_of(block):
    count = lax.axis_size("chan")
    blocks = {0: block}
    for away in range(1, count):
        near = away & -away
        blocks[away] = from_partner(blocks[away ^ near], "chan", near)
    return [blocks[away] for away in range(1, count)]


def from_partner(block, axis, away):
    return lax.ppermute(block, axis, [(i, i ^ away) for i in range(lax.axis_size(axis))])


def shards(recording, offsets, band_bins, dead_flags):
    channels, block_len = recording.shape
    windows = block_len // (L // 2)
    bins = band_bins.shape[0]
    chan_count, tm_count = lax.axis_size("chan"), lax.axis_size("tm")
    halves = tm_count // chan_count
    rim = L // 2 + L // 4
    cut = min(pl.cdiv(rim, STEP) * STEP, block_len)
    rim = L // 2 + L // 4
    cut = pl.cdiv(rim, STEP) * STEP
    own, back, state = spectra_of(recording, offsets, band_bins, dead_flags, windows, cut)
    more = moved(back, "tm", 1)
    rest = rest_of(recording, state, bins, windows, cut)
    white = whiten(own, rest, more, bins, windows, halves)
    row_blocks = [white] + [from_partner(white, "tm", away) for away in range(2, tm_count, 2)]
    chan_blocks = chan_blocks_of(white)
    joined, col_blocks = picked(row_blocks, chan_blocks, tm_count)
    for away in partners(tm_count):
        col_blocks[away] = from_partner(col_blocks[away], "tm", away)
    return stacks_of(col_blocks, [joined, from_partner(joined, "tm", 1)], bins, windows)


def solution(mesh):
    placed = (P("chan", "tm"), P(), P(), P("chan"))
    return jax.shard_map(
        shards, mesh=mesh, in_specs=placed, out_specs=P(None, None, "tm", "chan"), check_vma=False
    )
```

```python
import functools
import math

import jax
import jax.numpy as jnp
from jax import lax
from jax.experimental import pallas as pl
from jax.experimental.pallas import tpu as pltpu
from jax.sharding import PartitionSpec as P

L = 15000
FLOOR = 0.7
F32 = jnp.float32
BF16 = jnp.bfloat16
LANE = 128
DEPTH = 256
STEP = 1024
ROW_TILE = 16


def cos_sin(turns, length):
    quarter = jnp.floor(turns * (4.0 / length) + 0.5)
    angle = (turns * 4.0 - quarter * length) * (math.pi / (2.0 * length))
    square = angle * angle
    sine = angle * (
        1.0 + square * (-1.0 / 6 + square * (1.0 / 120 + square * (-1.0 / 5040 + square * (1.0 / 362880))))
    )
    cosine = 1.0 + square * (
        -0.5 + square * (1.0 / 24 + square * (-1.0 / 720 + square * (1.0 / 40320)))
    )
    quadrant = quarter - 4.0 * jnp.floor(quarter * 0.25)
    odd = (quadrant == 1.0) | (quadrant == 3.0)
    cos_sign = jnp.where((quadrant == 1.0) | (quadrant == 2.0), -1.0, 1.0)
    sin_sign = jnp.where(quadrant >= 2.0, -1.0, 1.0)
    return cos_sign * jnp.where(odd, sine, cosine), sin_sign * jnp.where(odd, cosine, sine)


def load_samples(x_hbm, x_ref, x_sems, low_end, size):
    return [
        pltpu.make_async_copy(
            x_hbm.at[pl.ds(low_end + i, min(STEP, size - i))], x_ref.at[pl.ds(i, min(STEP, size - i))],
            x_sems.at[i // STEP],
        )
        for i in range(0, size, STEP)
    ]


def make_tables(table, state, place, first, count, windows_rows):
    rows = table.shape[0]
    for r in range(0, rows, ROW_TILE):
        halves = (slice(r, r + 8), slice(r + 8, r + 16))
        now = [(state[0, at, :], state[1, at, :]) for at in halves]
        turn = [(state[2, at, :], state[3, at, :]) for at in halves]
        spot = None if place is None else [place[at, :] for at in halves]
        for j in range(count):
            moved = ((first + j) * DEPTH).astype(F32)
            values = [u for u, _ in now]
            if place is not None:
                values = [
                    jnp.where(where >= (-moved if at.start < windows_rows else moved), u, 0.0)
                    for at, where, u in zip(halves, spot, values)
                ]
            to_lanes = pl.ds(pl.multiple_of((first + j) * DEPTH, DEPTH), DEPTH)
            table[r:r + ROW_TILE, to_lanes] = jnp.concatenate(values, axis=0).astype(BF16)
            now = [(u * ct - v * st, v * ct + u * st) for (u, v), (ct, st) in zip(now, turn)]
        for at, (u, v) in zip(halves, now):
            state[0, at, :], state[1, at, :] = u, v


def add_products(table, x_ref, acc, base, size, row_range, energy_at):
    view = x_ref.at[pl.ds(base, size)]
    waves = table.at[:, pl.ds(base, size)]
    low, high = row_range
    channels = x_ref.shape[1]
    for n in range(0, channels, DEPTH):
        at = slice(n, min(n + DEPTH, channels))
        if energy_at is not None:
            total = squares(view, 0, 2, at)
            for t in range(2, size // ROW_TILE, 2):
                total = total + squares(view, t, 2, at)
        product = jnp.dot(waves[low:high, :], view[:, at], preferred_element_type=F32)
        acc[low:high, at] += product
        if energy_at is not None:
            energy_at[:, at] = total


def squares(view, first, count, at):
    total = None
    for t in range(first, first + count):
        x = view[t * ROW_TILE:(t + 1) * ROW_TILE, at]
        total = x * x if total is None else total + x * x
    total = total.astype(F32)
    return total[:ROW_TILE // 2] + total[ROW_TILE // 2:]


def mix_windows(out_ref, acc, first, windows, per_window, per_group):
    for w in range(windows):
        own_at = first + (windows - 1 - w) * per_window
        for q in range(0, per_window, per_group):
            to = q * windows + w * per_group
            out_ref[to:to + per_group, :] = acc[own_at + q:own_at + q + per_group, :]


def spectra_kernel(
    bins, windows, block_len, high_end,
    offsets_hbm, bins_hbm, dead_hbm, x_hbm, own_ref, back_ref, state_ref,
    offsets, band_bins, dead, x_ref, acc, seg, part_seg, mixed, state, place, table, small_sems, x_sems,
):
    channels = x_ref.shape[1]
    length, hop = L, L // 2
    per_window = 2 * bins
    rows = windows * per_window
    half_tile = ROW_TILE // 2
    per_group = half_tile // windows
    steps = high_end // STEP

    small = [
        pltpu.make_async_copy(offsets_hbm, offsets, small_sems.at[0]),
        pltpu.make_async_copy(bins_hbm, band_bins, small_sems.at[1]),
        pltpu.make_async_copy(dead_hbm, dead, small_sems.at[2]),
    ]
    for copy in small:
        copy.start()
    loads = load_samples(x_hbm, x_ref, x_sems, 0, high_end)
    loads[0].start()
    for copy in small:
        copy.wait()
    for copy in loads[1:]:
        copy.start()

    tm = lax.axis_index("tm")
    ahead = [offsets[tm * windows + w] + w * hop for w in range(windows)]
    before = jnp.maximum(tm - 1, 0) * windows
    behind = [offsets[before + w] + w * hop + length - block_len for w in range(windows)]
    ends = []
    for w in range(windows):
        ends += [jnp.minimum(ahead[w], behind[w]), jnp.maximum(ahead[w], behind[w])]
    segments = len(ends) + 1
    trash = segments

    shape = (half_tile, DEPTH)
    lane = lax.broadcasted_iota(jnp.int32, shape, 1).astype(F32)
    norm = 1.0 / math.sqrt(length)
    for r in range(0, 2 * rows, half_tile):
        at = slice(r, r + half_tile)
        row = lax.broadcasted_iota(jnp.int32, shape, 0) + r
        block, inner = row // per_window, row % per_window
        part = inner // per_group % 2
        bin_index = inner // (2 * per_group) * per_group + inner % per_group
        tone = jnp.zeros(shape, jnp.int32)
        for b in range(bins):
            if r // per_window != (r + half_tile - 1) // per_window or (
                r % per_window // (2 * per_group) * per_group <= b
                < (r % per_window + half_tile - 1) // (2 * per_group) * per_group + per_group
            ):
                tone = jnp.where(bin_index == b, band_bins[b], tone)
        start = jnp.zeros(shape, jnp.int32)
        for w in range(windows):
            start = jnp.where(block == windows - 1 - w, ahead[w], start)
            start = jnp.where(block == 2 * windows - 1 - w, behind[w] - length, start)
        tone, start = tone.astype(F32), start.astype(F32)
        cosine, sine = cos_sin((lane - start) * tone, length)
        state[0, at, :] = jnp.where(part == 1, -sine, cosine) * norm
        state[1, at, :] = jnp.where(part == 1, cosine, sine) * norm
        state[2, at, :], state[3, at, :] = cos_sin(tone * DEPTH, length)
        place[at, :] = lane - start if r < rows else start + (length - 1) - lane
    acc[...] = jnp.zeros_like(acc)
    seg[...] = jnp.zeros_like(seg)

    def segment_of(position):
        index = jnp.int32(0)
        for end in ends:
            index += (end <= position).astype(jnp.int32)
        return index

    def has_end(first, size):
        found = jnp.bool_(False)
        for end in ends:
            found = jnp.logical_or(found, jnp.logical_and(end >= first, end < first + size))
        return found

    def body(base, row_range, edge):
        add_products(table, x_ref, acc, base, STEP, row_range, None if edge else part_seg)
        if not edge:
            seg[segment_of(base)] += part_seg[...]
            return
        view = x_ref.at[pl.ds(base, STEP)]
        for t in range(STEP // ROW_TILE):
            first = base + t * ROW_TILE
            target = jnp.where(has_end(first, ROW_TILE), trash, segment_of(first))
            for n in range(0, channels, DEPTH):
                at = slice(n, min(n + DEPTH, channels))
                seg[target, :, at] += squares(view, t, 1, at)

    def reach(i):
        low, high = i * STEP, (i + 1) * STEP
        own = [w for w in range(windows) if w * hop < high]
        back = [w for w in range(windows) if w * hop + hop // 2 + length - block_len > low]
        first = (windows - 1 - max(own)) * per_window // ROW_TILE * ROW_TILE
        last = (2 * windows - min(back, default=windows)) * per_window
        edges = any(
            w * hop + shift < high and w * hop + hop // 2 + shift > low
            for w in range(windows) for shift in (0, length - block_len)
        )
        return (first, min(pl.cdiv(last, ROW_TILE) * ROW_TILE, 2 * rows)), edges

    kinds = [reach(i) for i in range(steps)]
    i = 0
    while i < steps:
        until = i
        while until < steps and kinds[until] == kinds[i]:
            until += 1
        row_range, edges = kinds[i]

        @pl.loop(i, until)
        def _(step):
            base = pl.multiple_of(step * STEP, STEP)
            make_tables(table, state, place, step * (STEP // DEPTH), STEP // DEPTH, rows)
            at = pl.ds(base, STEP)
            pltpu.make_async_copy(x_hbm.at[at], x_ref.at[at], x_sems.at[step]).wait()
            if not edges:
                body(base, row_range, False)
                return
            cut = has_end(base, STEP)

            @pl.when(jnp.logical_not(cut))
            def _():
                body(base, row_range, False)

            @pl.when(cut)
            def _():
                body(base, row_range, True)

        i = until

    for i, end in enumerate(ends):
        low = ends[i - 1] if i else jnp.int32(0)
        high = ends[i + 1] if i + 1 < len(ends) else jnp.int32(high_end)
        tile = end // ROW_TILE
        x = x_ref[pl.ds(pl.multiple_of(tile * ROW_TILE, ROW_TILE), ROW_TILE), :].astype(F32)
        spot = lax.broadcasted_iota(jnp.int32, x.shape, 0) + tile * ROW_TILE
        under = jnp.logical_and(spot >= low, spot < end)
        over = jnp.logical_and(spot >= end, spot < high)
        over = jnp.logical_and(over, high // ROW_TILE != tile)
        square = x * x
        for where, index in ((under, i), (over, i + 1)):
            kept = jnp.where(where, square, 0.0)
            seg[index] += kept[:half_tile] + kept[half_tile:]

    state_ref[...] = state[:, :rows, :]
    mix_windows(own_ref, acc, 0, windows, per_window, per_group)
    mix_windows(mixed, acc, rows, windows, per_window, per_group)
    back_ref[:rows, :] = mixed[...].astype(BF16)
    parts = [seg[i] for i in range(segments)]
    row = lax.broadcasted_iota(jnp.int32, (half_tile, channels), 0)
    own_block = jnp.where(row == windows, (1 - dead[...]).astype(F32), 0.0)
    back_block = jnp.zeros((ROW_TILE, channels), F32)
    back_row = lax.broadcasted_iota(jnp.int32, (ROW_TILE, channels), 0)
    for w in range(windows):
        turn = jnp.where(ahead[w] <= behind[w], parts[2 * w + 1], 0.0)
        own_energy = jnp.sum(sum(parts[2 * w + 2:]) + turn, axis=0, keepdims=True)
        own_block = jnp.where(row == w, own_energy, own_block)
        rest = jnp.sum(sum(parts[:2 * w + 1]) + turn, axis=0, keepdims=True)
        for term in range(3):
            piece_of = rest.astype(BF16).astype(F32)
            rest = rest - piece_of
            back_block = jnp.where(back_row == term * windows + w, piece_of, back_block)
    own_ref[rows:, :] = own_block
    back_ref[rows:, :] = back_block.astype(BF16)


def rest_kernel(
    bins, windows, block_len, low_end, state_in, x_hbm, tail_ref, own_ref,
    x_ref, acc, part_seg, total_seg, state, table, x_sems,
):
    channels = x_ref.shape[1]
    per_window = 2 * bins
    rows = windows * per_window
    half_tile = ROW_TILE // 2
    count = block_len - low_end
    bulk = count // ROW_TILE * ROW_TILE
    padded = x_ref.shape[0]
    loads = load_samples(x_hbm, x_ref, x_sems, low_end, bulk)
    for copy in loads:
        copy.start()
    state[...] = state_in[...]
    acc[...] = jnp.zeros_like(acc)
    total_seg[...] = jnp.zeros_like(total_seg)
    if padded > bulk:
        x_ref[bulk:, :] = jnp.zeros((padded - bulk, channels), BF16)
    if count > bulk:
        inside = lax.broadcasted_iota(jnp.int32, (ROW_TILE, channels), 0) < count - bulk
        x_ref[bulk:bulk + ROW_TILE, :] = jnp.where(inside, tail_ref[...].astype(F32), 0.0).astype(BF16)
    for i in range(0, padded, STEP):
        size = min(STEP, padded - i)
        make_tables(table, state, None, jnp.int32(i // DEPTH), size // DEPTH, rows)
        if i // STEP < len(loads):
            loads[i // STEP].wait()
        add_products(table, x_ref, acc, i, size, (0, rows), part_seg)
        total_seg[...] += part_seg[...]
    mix_windows(own_ref, acc, 0, windows, per_window, half_tile // windows)
    energy = jnp.sum(total_seg[...], axis=0, keepdims=True)
    row = lax.broadcasted_iota(jnp.int32, (half_tile, channels), 0)
    own_ref[rows:, :] = jnp.where(row < windows, energy, 0.0)


def spectra_of(recording, offsets, band_bins, dead, windows, high_end):
    channels, block_len = recording.shape
    bins = band_bins.shape[0]
    rows = bins * windows * 2
    samples = recording.T
    hbm = pl.BlockSpec(memory_space=pltpu.HBM)
    whole = pl.BlockSpec(memory_space=pltpu.VMEM)
    return pl.pallas_call(
        functools.partial(spectra_kernel, bins, windows, block_len, high_end),
        out_shape=[
            jax.ShapeDtypeStruct((rows + ROW_TILE // 2, channels), F32),
            jax.ShapeDtypeStruct((rows + ROW_TILE, channels), BF16),
            jax.ShapeDtypeStruct((4, rows, DEPTH), F32),
        ],
        in_specs=[hbm, hbm, hbm, hbm],
        out_specs=[whole] * 3,
        scratch_shapes=[
            pltpu.SMEM(offsets.shape, jnp.int32),
            pltpu.SMEM(band_bins.shape, jnp.int32),
            pltpu.VMEM((1, channels), jnp.int32),
            pltpu.VMEM((high_end, channels), BF16),
            pltpu.VMEM((2 * rows, channels), F32),
            pltpu.VMEM((2 * windows + 2, ROW_TILE // 2, channels), F32),
            pltpu.VMEM((ROW_TILE // 2, channels), F32),
            pltpu.VMEM((rows, channels), F32),
            pltpu.VMEM((4, 2 * rows, DEPTH), F32),
            pltpu.VMEM((2 * rows, DEPTH), F32),
            pltpu.VMEM((2 * rows, high_end), BF16),
            pltpu.SemaphoreType.DMA((3,)),
            pltpu.SemaphoreType.DMA((high_end // STEP,)),
        ],
        compiler_params=pltpu.CompilerParams(vmem_limit_bytes=60 * 2**20),
        cost_estimate=pl.CostEstimate(
            flops=2 * channels * high_end * 2 * rows, bytes_accessed=channels * high_end * 2, transcendentals=0
        ),
        name="band_spectra",
    )(offsets, band_bins, dead.reshape(1, channels), samples)


def rest_of(recording, state, bins, windows, low_end):
    channels, block_len = recording.shape
    rows = bins * windows * 2
    count = block_len - low_end
    padded = pl.cdiv(count, DEPTH) * DEPTH
    bulk = count // ROW_TILE * ROW_TILE
    tail = min(low_end + bulk, block_len - 1) // ROW_TILE
    samples = recording.T
    whole = pl.BlockSpec(memory_space=pltpu.VMEM)
    return pl.pallas_call(
        functools.partial(rest_kernel, bins, windows, block_len, low_end),
        out_shape=jax.ShapeDtypeStruct((rows + ROW_TILE // 2, channels), F32),
        grid=(1,),
        in_specs=[
            whole,
            pl.BlockSpec(memory_space=pltpu.HBM),
            pl.BlockSpec((ROW_TILE, channels), lambda i: (tail, 0)),
        ],
        out_specs=whole,
        scratch_shapes=[
            pltpu.VMEM((padded, channels), BF16),
            pltpu.VMEM((rows, channels), F32),
            pltpu.VMEM((ROW_TILE // 2, channels), F32),
            pltpu.VMEM((ROW_TILE // 2, channels), F32),
            pltpu.VMEM((4, rows, DEPTH), F32),
            pltpu.VMEM((rows, padded), BF16),
            pltpu.SemaphoreType.DMA((pl.cdiv(padded, STEP),)),
        ],
        compiler_params=pltpu.CompilerParams(vmem_limit_bytes=24 * 2**20),
        cost_estimate=pl.CostEstimate(
            flops=2 * channels * count * rows, bytes_accessed=channels * count * 2, transcendentals=0
        ),
        name="band_spectra_rest",
    )(state, samples, samples)


def whiten_kernel(bins, windows, own_ref, rest_ref, more_ref, white_ref):
    rows = bins * windows * 2
    more = more_ref[...].astype(F32)
    raw = own_ref[:rows, :] + rest_ref[:rows, :] + more[:rows]
    extra = more[rows:]
    per_group = ROW_TILE // (2 * windows)
    which = lax.broadcasted_iota(jnp.int32, (rows, 1), 0) // per_group % windows
    alive = own_ref[rows + windows:rows + windows + 1, :]
    scale = factor = None
    for w in range(windows):
        energy = own_ref[rows + w:rows + w + 1, :] + rest_ref[rows + w:rows + w + 1, :]
        for term in range(3):
            energy = energy + extra[term * windows + w:term * windows + w + 1, :]
        inverse = 1.0 / jnp.sqrt(energy / L + 1e-06)
        scale = inverse if w == 0 else jnp.where(which == w, inverse, scale)
    spectra = raw * scale
    power = spectra * spectra
    for w in range(windows):
        level = jnp.sum(jnp.where(which == w, power, 0.0), axis=0, keepdims=True) * (1.0 / bins)
        one = alive / jnp.sqrt(jnp.maximum(level, FLOOR))
        factor = one if w == 0 else jnp.where(which == w, one, factor)
    white = (spectra * factor).astype(BF16)
    width = white_ref.shape[2]
    for h in range(white_ref.shape[0]):
        white_ref[h] = white[:, h * width:(h + 1) * width]


def whiten(own, rest, more, bins, windows, halves):
    channels = own.shape[1]
    return pl.pallas_call(
        functools.partial(whiten_kernel, bins, windows),
        out_shape=jax.ShapeDtypeStruct((halves, bins * windows * 2, channels // halves), BF16),
        compiler_params=pltpu.CompilerParams(vmem_limit_bytes=12 * 2**20),
        name="whiten",
    )(own, rest, more)


def stack_kernel(windows, scale, devices, *refs):
    col_refs, row_refs = refs[:devices], refs[devices:2 * devices]
    out_hbm, lhs, held, made, sems = refs[2 * devices:]
    per_group = ROW_TILE // (2 * windows)
    step = pl.program_id(0)
    width = col_refs[0].shape[1]
    depth = devices * ROW_TILE
    halves, _, span = row_refs[0].shape
    channels = halves * span
    exact = math.frexp(scale)[0] == 0.5

    by_partner = dict(zip([0, *partners(devices)], col_refs))
    cols = jnp.stack([by_partner[away][...].astype(F32) for away in range(devices)])
    if exact:
        cols = cols * scale
    head, tail = cols[:, :ROW_TILE // 2], cols[:, ROW_TILE // 2:]
    straight = cols.reshape(depth, width)
    turned = jnp.concatenate([-tail, head], axis=1).reshape(depth, width)
    lhs[:width, :] = straight.T.astype(BF16)
    lhs[width:, :] = turned.T.astype(BF16)
    for away in range(devices):
        to = slice(away * ROW_TILE, (away + 1) * ROW_TILE)
        for h in range(halves):
            held[to, h * span:(h + 1) * span] = row_refs[away][h].astype(F32)

    def out_copy(slot, part, bin_index):
        to = out_hbm.at[part, bin_index]
        return pltpu.make_async_copy(made.at[slot], to, sems.at[slot])

    which = lax.broadcasted_iota(jnp.int32, (depth, 1), 0) % per_group
    for b in range(per_group):
        for part in range(2):
            slot = 2 * b + part

            @pl.when(step > 0)
            def _():
                out_copy(slot, part, (step - 1) * per_group + b).wait()

        for n in range(0, channels, DEPTH):
            at = slice(n, min(n + DEPTH, channels))
            rhs = jnp.where(which == b, held[:, at], 0.0).astype(BF16)
            for part in range(2):
                product = jnp.dot(
                    lhs[part * width:(part + 1) * width, :], rhs, preferred_element_type=F32
                )
                if not exact:
                    product = product * scale
                made[2 * b + part, :, at] = product.astype(BF16)
        for part in range(2):
            out_copy(2 * b + part, part, step * per_group + b).start()

    @pl.when(step == pl.num_programs(0) - 1)
    def _():
        for b in range(per_group):
            for part in range(2):
                out_copy(2 * b + part, part, step * per_group + b).wait()


def stacks_of(col_blocks, row_blocks, bins, windows):
    devices = len(col_blocks)
    halves, _, span = row_blocks[0].shape
    width = col_blocks[0].shape[1]
    per_group = ROW_TILE // (2 * windows)
    scale = 1.0 / math.sqrt(windows * devices)
    channels = halves * span
    return pl.pallas_call(
        functools.partial(stack_kernel, windows, scale, devices),
        out_shape=jax.ShapeDtypeStruct((2, bins, width, channels), BF16),
        grid=(bins // per_group,),
        in_specs=[pl.BlockSpec((ROW_TILE, width), lambda i: (i, 0))] * devices
        + [pl.BlockSpec((halves, ROW_TILE, span), lambda i: (0, i, 0))] * devices,
        out_specs=pl.BlockSpec(memory_space=pltpu.HBM),
        scratch_shapes=[
            pltpu.VMEM((2 * width, devices * ROW_TILE), BF16),
            pltpu.VMEM((devices * ROW_TILE, channels), F32),
            pltpu.VMEM((2 * per_group, width, channels), BF16),
            pltpu.SemaphoreType.DMA((2 * per_group,)),
        ],
        compiler_params=pltpu.CompilerParams(
            dimension_semantics=("arbitrary",), vmem_limit_bytes=24 * 2**20
        ),
        cost_estimate=pl.CostEstimate(
            flops=2 * 2 * bins * width * channels * devices * ROW_TILE,
            bytes_accessed=2 * bins * width * channels * 2,
            transcendentals=0,
        ),
        name="stack_products",
    )(*[col_blocks[away] for away in [0, *partners(devices)]], *row_blocks)


def pick_kernel(count, waits, *refs):
    white_ref, chan_refs, out_refs, held = refs[0], refs[1 + waits:-1 - count], refs[-1 - count:-1], refs[-1]
    tm, mine = lax.axis_index("tm"), lax.axis_index("chan")
    halves = white_ref.shape[0]
    for away, ref in enumerate((white_ref, *chan_refs)):
        held[jnp.bitwise_xor(mine, away)] = ref[...]
    for away, out_ref in enumerate(out_refs):
        wanted = jnp.bitwise_xor(tm, away)
        out_ref[...] = held[wanted // halves, wanted % halves]


def picked(row_blocks, chan_blocks, count):
    block = row_blocks[0]
    _, rows, width = block.shape
    whole = pl.BlockSpec(memory_space=pltpu.VMEM)
    waits = len(row_blocks) - 1
    return pl.pallas_call(
        functools.partial(pick_kernel, count, waits),
        out_shape=[jax.ShapeDtypeStruct((rows, width), block.dtype)] * count,
        in_specs=[whole] + [pl.BlockSpec(memory_space=pl.ANY)] * waits + [whole] * len(chan_blocks),
        out_specs=[whole] * count,
        scratch_shapes=[pltpu.VMEM((1 + len(chan_blocks), *block.shape), block.dtype)],
        compiler_params=pltpu.CompilerParams(vmem_limit_bytes=16 * 2**20),
        name="pick_blocks",
    )(*row_blocks, *chan_blocks)


def moved(block, axis, far):
    count = lax.axis_size(axis)
    return lax.ppermute(block, axis, [(i + far, i) for i in range(count) if 0 <= i + far < count])


def partners(count):
    return [*range(2, count, 2), *range(3, count, 2), 1]


def chan_blocks_of(block):
    count = lax.axis_size("chan")
    blocks = {0: block}
    for away in range(1, count):
        near = away & -away
        blocks[away] = from_partner(blocks[away ^ near], "chan", near)
    return [blocks[away] for away in range(1, count)]


def from_partner(block, axis, away):
    return lax.ppermute(block, axis, [(i, i ^ away) for i in range(lax.axis_size(axis))])


def shards(recording, offsets, band_bins, dead_flags):
    channels, block_len = recording.shape
    windows = block_len // (L // 2)
    bins = band_bins.shape[0]
    chan_count, tm_count = lax.axis_size("chan"), lax.axis_size("tm")
    halves = tm_count // chan_count
    rim = L // 2 + L // 4
    cut = min(pl.cdiv(rim, STEP) * STEP, block_len)
    rim = L // 2 + L // 4
    cut = pl.cdiv(rim, STEP) * STEP
    own, back, state = spectra_of(recording, offsets, band_bins, dead_flags, windows, cut)
    more = moved(back, "tm", 1)
    rest = rest_of(recording, state, bins, windows, cut)
    white = whiten(own, rest, more, bins, windows, halves)
    row_blocks = [white] + [from_partner(white, "tm", away) for away in range(2, tm_count, 2)]
    chan_blocks = chan_blocks_of(white)
    col_blocks = list(picked(row_blocks, chan_blocks, tm_count))
    for away in partners(tm_count):
        col_blocks[away] = from_partner(col_blocks[away], "tm", away)
    all_rows = []
    for block in row_blocks:
        all_rows += [block, from_partner(block, "tm", 1)]
    return stacks_of(col_blocks, all_rows, bins, windows)


def solution(mesh):
    placed = (P("chan", "tm"), P(), P(), P("chan"))
    return jax.shard_map(
        shards, mesh=mesh, in_specs=placed, out_specs=P(None, None, "tm", "chan"), check_vma=False
    )
```

```python
import functools
import math

import jax
import jax.numpy as jnp
from jax import lax
from jax.experimental import pallas as pl
from jax.experimental.pallas import tpu as pltpu
from jax.sharding import PartitionSpec as P

L = 15000
FLOOR = 0.7
F32 = jnp.float32
BF16 = jnp.bfloat16
LANE = 128
DEPTH = 256
STEP = 1024
ROW_TILE = 16


def cos_sin(turns, length):
    quarter = jnp.floor(turns * (4.0 / length) + 0.5)
    angle = (turns * 4.0 - quarter * length) * (math.pi / (2.0 * length))
    square = angle * angle
    sine = angle * (
        1.0 + square * (-1.0 / 6 + square * (1.0 / 120 + square * (-1.0 / 5040 + square * (1.0 / 362880))))
    )
    cosine = 1.0 + square * (
        -0.5 + square * (1.0 / 24 + square * (-1.0 / 720 + square * (1.0 / 40320)))
    )
    quadrant = quarter - 4.0 * jnp.floor(quarter * 0.25)
    odd = (quadrant == 1.0) | (quadrant == 3.0)
    cos_sign = jnp.where((quadrant == 1.0) | (quadrant == 2.0), -1.0, 1.0)
    sin_sign = jnp.where(quadrant >= 2.0, -1.0, 1.0)
    return cos_sign * jnp.where(odd, sine, cosine), sin_sign * jnp.where(odd, cosine, sine)


def load_samples(x_hbm, x_ref, x_sems, low_end, size):
    return [
        pltpu.make_async_copy(
            x_hbm.at[pl.ds(low_end + i, min(STEP, size - i))], x_ref.at[pl.ds(i, min(STEP, size - i))],
            x_sems.at[i // STEP],
        )
        for i in range(0, size, STEP)
    ]


def make_tables(table, state, place, first, count, windows_rows):
    rows = table.shape[0]
    for r in range(0, rows, ROW_TILE):
        halves = (slice(r, r + 8), slice(r + 8, r + 16))
        now = [(state[0, at, :], state[1, at, :]) for at in halves]
        turn = [(state[2, at, :], state[3, at, :]) for at in halves]
        spot = None if place is None else [place[at, :] for at in halves]
        for j in range(count):
            moved = ((first + j) * DEPTH).astype(F32)
            values = [u for u, _ in now]
            if place is not None:
                values = [
                    jnp.where(where >= (-moved if at.start < windows_rows else moved), u, 0.0)
                    for at, where, u in zip(halves, spot, values)
                ]
            to_lanes = pl.ds(pl.multiple_of((first + j) * DEPTH, DEPTH), DEPTH)
            table[r:r + ROW_TILE, to_lanes] = jnp.concatenate(values, axis=0).astype(BF16)
            now = [(u * ct - v * st, v * ct + u * st) for (u, v), (ct, st) in zip(now, turn)]
        for at, (u, v) in zip(halves, now):
            state[0, at, :], state[1, at, :] = u, v


def add_products(table, x_ref, acc, base, size, row_range, energy_at):
    view = x_ref.at[pl.ds(base, size)]
    waves = table.at[:, pl.ds(base, size)]
    low, high = row_range
    channels = x_ref.shape[1]
    for n in range(0, channels, DEPTH):
        at = slice(n, min(n + DEPTH, channels))
        if energy_at is not None:
            total = squares(view, 0, 2, at)
            for t in range(2, size // ROW_TILE, 2):
                total = total + squares(view, t, 2, at)
        product = jnp.dot(waves[low:high, :], view[:, at], preferred_element_type=F32)
        acc[low:high, at] += product
        if energy_at is not None:
            energy_at[:, at] = total


def squares(view, first, count, at):
    total = None
    for t in range(first, first + count):
        x = view[t * ROW_TILE:(t + 1) * ROW_TILE, at]
        total = x * x if total is None else total + x * x
    total = total.astype(F32)
    return total[:ROW_TILE // 2] + total[ROW_TILE // 2:]


def mix_windows(out_ref, acc, first, windows, per_window, per_group):
    for w in range(windows):
        own_at = first + (windows - 1 - w) * per_window
        for q in range(0, per_window, per_group):
            to = q * windows + w * per_group
            out_ref[to:to + per_group, :] = acc[own_at + q:own_at + q + per_group, :]


def spectra_kernel(
    bins, windows, block_len, high_end,
    offsets_hbm, bins_hbm, dead_hbm, x_hbm, own_ref, back_ref, state_ref,
    offsets, band_bins, dead, x_ref, acc, seg, part_seg, mixed, state, place, table, small_sems, x_sems,
):
    channels = x_ref.shape[1]
    length, hop = L, L // 2
    per_window = 2 * bins
    rows = windows * per_window
    half_tile = ROW_TILE // 2
    per_group = half_tile // windows
    steps = high_end // STEP

    small = [
        pltpu.make_async_copy(offsets_hbm, offsets, small_sems.at[0]),
        pltpu.make_async_copy(bins_hbm, band_bins, small_sems.at[1]),
        pltpu.make_async_copy(dead_hbm, dead, small_sems.at[2]),
    ]
    for copy in small:
        copy.start()
    loads = load_samples(x_hbm, x_ref, x_sems, 0, high_end)
    loads[0].start()
    for copy in small:
        copy.wait()
    for copy in loads[1:]:
        copy.start()

    tm = lax.axis_index("tm")
    ahead = [offsets[tm * windows + w] + w * hop for w in range(windows)]
    before = jnp.maximum(tm - 1, 0) * windows
    behind = [offsets[before + w] + w * hop + length - block_len for w in range(windows)]
    ends = []
    for w in range(windows):
        ends += [jnp.minimum(ahead[w], behind[w]), jnp.maximum(ahead[w], behind[w])]
    segments = len(ends) + 1
    trash = segments

    shape = (half_tile, DEPTH)
    lane = lax.broadcasted_iota(jnp.int32, shape, 1).astype(F32)
    norm = 1.0 / math.sqrt(length)
    for r in range(0, 2 * rows, half_tile):
        at = slice(r, r + half_tile)
        row = lax.broadcasted_iota(jnp.int32, shape, 0) + r
        block, inner = row // per_window, row % per_window
        part = inner // per_group % 2
        bin_index = inner // (2 * per_group) * per_group + inner % per_group
        tone = jnp.zeros(shape, jnp.int32)
        for b in range(bins):
            if r // per_window != (r + half_tile - 1) // per_window or (
                r % per_window // (2 * per_group) * per_group <= b
                < (r % per_window + half_tile - 1) // (2 * per_group) * per_group + per_group
            ):
                tone = jnp.where(bin_index == b, band_bins[b], tone)
        start = jnp.zeros(shape, jnp.int32)
        for w in range(windows):
            start = jnp.where(block == windows - 1 - w, ahead[w], start)
            start = jnp.where(block == 2 * windows - 1 - w, behind[w] - length, start)
        tone, start = tone.astype(F32), start.astype(F32)
        cosine, sine = cos_sin((lane - start) * tone, length)
        state[0, at, :] = jnp.where(part == 1, -sine, cosine) * norm
        state[1, at, :] = jnp.where(part == 1, cosine, sine) * norm
        state[2, at, :], state[3, at, :] = cos_sin(tone * DEPTH, length)
        place[at, :] = lane - start if r < rows else start + (length - 1) - lane
    acc[...] = jnp.zeros_like(acc)
    seg[...] = jnp.zeros_like(seg)

    def segment_of(position):
        index = jnp.int32(0)
        for end in ends:
            index += (end <= position).astype(jnp.int32)
        return index

    def has_end(first, size):
        found = jnp.bool_(False)
        for end in ends:
            found = jnp.logical_or(found, jnp.logical_and(end >= first, end < first + size))
        return found

    def body(base, row_range, edge):
        add_products(table, x_ref, acc, base, STEP, row_range, None if edge else part_seg)
        if not edge:
            seg[segment_of(base)] += part_seg[...]
            return
        view = x_ref.at[pl.ds(base, STEP)]
        for t in range(STEP // ROW_TILE):
            first = base + t * ROW_TILE
            target = jnp.where(has_end(first, ROW_TILE), trash, segment_of(first))
            for n in range(0, channels, DEPTH):
                at = slice(n, min(n + DEPTH, channels))
                seg[target, :, at] += squares(view, t, 1, at)

    def reach(i):
        low, high = i * STEP, (i + 1) * STEP
        own = [w for w in range(windows) if w * hop < high]
        back = [w for w in range(windows) if w * hop + hop // 2 + length - block_len > low]
        first = (windows - 1 - max(own)) * per_window // ROW_TILE * ROW_TILE
        last = (2 * windows - min(back, default=windows)) * per_window
        edges = any(
            w * hop + shift < high and w * hop + hop // 2 + shift > low
            for w in range(windows) for shift in (0, length - block_len)
        )
        return (first, min(pl.cdiv(last, ROW_TILE) * ROW_TILE, 2 * rows)), edges

    kinds = [reach(i) for i in range(steps)]
    i = 0
    while i < steps:
        until = i
        while until < steps and kinds[until] == kinds[i]:
            until += 1
        row_range, edges = kinds[i]

        @pl.loop(i, until)
        def _(step):
            base = pl.multiple_of(step * STEP, STEP)
            make_tables(table, state, place, step * (STEP // DEPTH), STEP // DEPTH, rows)
            at = pl.ds(base, STEP)
            pltpu.make_async_copy(x_hbm.at[at], x_ref.at[at], x_sems.at[step]).wait()
            if not edges:
                body(base, row_range, False)
                return
            cut = has_end(base, STEP)

            @pl.when(jnp.logical_not(cut))
            def _():
                body(base, row_range, False)

            @pl.when(cut)
            def _():
                body(base, row_range, True)

        i = until

    for i, end in enumerate(ends):
        low = ends[i - 1] if i else jnp.int32(0)
        high = ends[i + 1] if i + 1 < len(ends) else jnp.int32(high_end)
        tile = end // ROW_TILE
        x = x_ref[pl.ds(pl.multiple_of(tile * ROW_TILE, ROW_TILE), ROW_TILE), :].astype(F32)
        spot = lax.broadcasted_iota(jnp.int32, x.shape, 0) + tile * ROW_TILE
        under = jnp.logical_and(spot >= low, spot < end)
        over = jnp.logical_and(spot >= end, spot < high)
        over = jnp.logical_and(over, high // ROW_TILE != tile)
        square = x * x
        for where, index in ((under, i), (over, i + 1)):
            kept = jnp.where(where, square, 0.0)
            seg[index] += kept[:half_tile] + kept[half_tile:]

    state_ref[...] = state[:, :rows, :]
    mix_windows(own_ref, acc, 0, windows, per_window, per_group)
    mix_windows(mixed, acc, rows, windows, per_window, per_group)
    back_ref[:rows, :] = mixed[...].astype(BF16)
    parts = [seg[i] for i in range(segments)]
    row = lax.broadcasted_iota(jnp.int32, (half_tile, channels), 0)
    own_block = jnp.where(row == windows, (1 - dead[...]).astype(F32), 0.0)
    back_block = jnp.zeros((ROW_TILE, channels), F32)
    back_row = lax.broadcasted_iota(jnp.int32, (ROW_TILE, channels), 0)
    for w in range(windows):
        turn = jnp.where(ahead[w] <= behind[w], parts[2 * w + 1], 0.0)
        own_energy = jnp.sum(sum(parts[2 * w + 2:]) + turn, axis=0, keepdims=True)
        own_block = jnp.where(row == w, own_energy, own_block)
        rest = jnp.sum(sum(parts[:2 * w + 1]) + turn, axis=0, keepdims=True)
        for term in range(3):
            piece_of = rest.astype(BF16).astype(F32)
            rest = rest - piece_of
            back_block = jnp.where(back_row == term * windows + w, piece_of, back_block)
    own_ref[rows:, :] = own_block
    back_ref[rows:, :] = back_block.astype(BF16)


def rest_kernel(
    bins, windows, block_len, low_end, state_in, x_hbm, tail_ref, own_ref,
    x_ref, acc, part_seg, total_seg, state, table, x_sems,
):
    channels = x_ref.shape[1]
    per_window = 2 * bins
    rows = windows * per_window
    half_tile = ROW_TILE // 2
    count = block_len - low_end
    bulk = count // ROW_TILE * ROW_TILE
    padded = x_ref.shape[0]
    loads = load_samples(x_hbm, x_ref, x_sems, low_end, bulk)
    for copy in loads:
        copy.start()
    state[...] = state_in[...]
    acc[...] = jnp.zeros_like(acc)
    total_seg[...] = jnp.zeros_like(total_seg)
    if padded > bulk:
        x_ref[bulk:, :] = jnp.zeros((padded - bulk, channels), BF16)
    if count > bulk:
        inside = lax.broadcasted_iota(jnp.int32, (ROW_TILE, channels), 0) < count - bulk
        x_ref[bulk:bulk + ROW_TILE, :] = jnp.where(inside, tail_ref[...].astype(F32), 0.0).astype(BF16)
    for i in range(0, padded, STEP):
        size = min(STEP, padded - i)
        make_tables(table, state, None, jnp.int32(i // DEPTH), size // DEPTH, rows)
        if i // STEP < len(loads):
            loads[i // STEP].wait()
        add_products(table, x_ref, acc, i, size, (0, rows), part_seg)
        total_seg[...] += part_seg[...]
    mix_windows(own_ref, acc, 0, windows, per_window, half_tile // windows)
    energy = jnp.sum(total_seg[...], axis=0, keepdims=True)
    row = lax.broadcasted_iota(jnp.int32, (half_tile, channels), 0)
    own_ref[rows:, :] = jnp.where(row < windows, energy, 0.0)


def spectra_of(recording, offsets, band_bins, dead, windows, high_end):
    channels, block_len = recording.shape
    bins = band_bins.shape[0]
    rows = bins * windows * 2
    samples = recording.T
    hbm = pl.BlockSpec(memory_space=pltpu.HBM)
    whole = pl.BlockSpec(memory_space=pltpu.VMEM)
    return pl.pallas_call(
        functools.partial(spectra_kernel, bins, windows, block_len, high_end),
        out_shape=[
            jax.ShapeDtypeStruct((rows + ROW_TILE // 2, channels), F32),
            jax.ShapeDtypeStruct((rows + ROW_TILE, channels), BF16),
            jax.ShapeDtypeStruct((4, rows, DEPTH), F32),
        ],
        in_specs=[hbm, hbm, hbm, hbm],
        out_specs=[whole] * 3,
        scratch_shapes=[
            pltpu.SMEM(offsets.shape, jnp.int32),
            pltpu.SMEM(band_bins.shape, jnp.int32),
            pltpu.VMEM((1, channels), jnp.int32),
            pltpu.VMEM((high_end, channels), BF16),
            pltpu.VMEM((2 * rows, channels), F32),
            pltpu.VMEM((2 * windows + 2, ROW_TILE // 2, channels), F32),
            pltpu.VMEM((ROW_TILE // 2, channels), F32),
            pltpu.VMEM((rows, channels), F32),
            pltpu.VMEM((4, 2 * rows, DEPTH), F32),
            pltpu.VMEM((2 * rows, DEPTH), F32),
            pltpu.VMEM((2 * rows, high_end), BF16),
            pltpu.SemaphoreType.DMA((3,)),
            pltpu.SemaphoreType.DMA((high_end // STEP,)),
        ],
        compiler_params=pltpu.CompilerParams(vmem_limit_bytes=60 * 2**20),
        cost_estimate=pl.CostEstimate(
            flops=2 * channels * high_end * 2 * rows, bytes_accessed=channels * high_end * 2, transcendentals=0
        ),
        name="band_spectra",
    )(offsets, band_bins, dead.reshape(1, channels), samples)


def rest_of(recording, state, bins, windows, low_end):
    channels, block_len = recording.shape
    rows = bins * windows * 2
    count = block_len - low_end
    padded = pl.cdiv(count, DEPTH) * DEPTH
    bulk = count // ROW_TILE * ROW_TILE
    tail = min(low_end + bulk, block_len - 1) // ROW_TILE
    samples = recording.T
    whole = pl.BlockSpec(memory_space=pltpu.VMEM)
    return pl.pallas_call(
        functools.partial(rest_kernel, bins, windows, block_len, low_end),
        out_shape=jax.ShapeDtypeStruct((rows + ROW_TILE // 2, channels), F32),
        grid=(1,),
        in_specs=[
            whole,
            pl.BlockSpec(memory_space=pltpu.HBM),
            pl.BlockSpec((ROW_TILE, channels), lambda i: (tail, 0)),
        ],
        out_specs=whole,
        scratch_shapes=[
            pltpu.VMEM((padded, channels), BF16),
            pltpu.VMEM((rows, channels), F32),
            pltpu.VMEM((ROW_TILE // 2, channels), F32),
            pltpu.VMEM((ROW_TILE // 2, channels), F32),
            pltpu.VMEM((4, rows, DEPTH), F32),
            pltpu.VMEM((rows, padded), BF16),
            pltpu.SemaphoreType.DMA((pl.cdiv(padded, STEP),)),
        ],
        compiler_params=pltpu.CompilerParams(vmem_limit_bytes=24 * 2**20),
        cost_estimate=pl.CostEstimate(
            flops=2 * channels * count * rows, bytes_accessed=channels * count * 2, transcendentals=0
        ),
        name="band_spectra_rest",
    )(state, samples, samples)


def whiten_kernel(bins, windows, own_ref, rest_ref, more_ref, white_ref):
    rows = bins * windows * 2
    more = more_ref[...].astype(F32)
    raw = own_ref[:rows, :] + rest_ref[:rows, :] + more[:rows]
    extra = more[rows:]
    per_group = ROW_TILE // (2 * windows)
    which = lax.broadcasted_iota(jnp.int32, (rows, 1), 0) // per_group % windows
    alive = own_ref[rows + windows:rows + windows + 1, :]
    scale = factor = None
    for w in range(windows):
        energy = own_ref[rows + w:rows + w + 1, :] + rest_ref[rows + w:rows + w + 1, :]
        for term in range(3):
            energy = energy + extra[term * windows + w:term * windows + w + 1, :]
        inverse = 1.0 / jnp.sqrt(energy / L + 1e-06)
        scale = inverse if w == 0 else jnp.where(which == w, inverse, scale)
    spectra = raw * scale
    power = spectra * spectra
    for w in range(windows):
        level = jnp.sum(jnp.where(which == w, power, 0.0), axis=0, keepdims=True) * (1.0 / bins)
        one = alive / jnp.sqrt(jnp.maximum(level, FLOOR))
        factor = one if w == 0 else jnp.where(which == w, one, factor)
    white = (spectra * factor).astype(BF16)
    width = white_ref.shape[2]
    for h in range(white_ref.shape[0]):
        white_ref[h] = white[:, h * width:(h + 1) * width]


def whiten(own, rest, more, bins, windows, halves):
    channels = own.shape[1]
    return pl.pallas_call(
        functools.partial(whiten_kernel, bins, windows),
        out_shape=jax.ShapeDtypeStruct((halves, bins * windows * 2, channels // halves), BF16),
        compiler_params=pltpu.CompilerParams(vmem_limit_bytes=12 * 2**20),
        name="whiten",
    )(own, rest, more)


def stack_kernel(windows, scale, devices, *refs):
    col_refs, row_refs = refs[:2], refs[2:2 + devices]
    out_hbm, lhs, held, made, sems = refs[2 + devices:]
    per_group = ROW_TILE // (2 * windows)
    step = pl.program_id(0)
    width = col_refs[0].shape[2]
    depth = devices * ROW_TILE
    halves, _, span = row_refs[0].shape
    channels = halves * span
    exact = math.frexp(scale)[0] == 0.5

    cols = jnp.stack([col_refs[away % 2][away // 2].astype(F32) for away in range(devices)])
    if exact:
        cols = cols * scale
    head, tail = cols[:, :ROW_TILE // 2], cols[:, ROW_TILE // 2:]
    straight = cols.reshape(depth, width)
    turned = jnp.concatenate([-tail, head], axis=1).reshape(depth, width)
    lhs[:width, :] = straight.T.astype(BF16)
    lhs[width:, :] = turned.T.astype(BF16)
    for away in range(devices):
        to = slice(away * ROW_TILE, (away + 1) * ROW_TILE)
        for h in range(halves):
            held[to, h * span:(h + 1) * span] = row_refs[away][h].astype(F32)

    def out_copy(slot, part, bin_index):
        to = out_hbm.at[part, bin_index]
        return pltpu.make_async_copy(made.at[slot], to, sems.at[slot])

    which = lax.broadcasted_iota(jnp.int32, (depth, 1), 0) % per_group
    for b in range(per_group):
        for part in range(2):
            slot = 2 * b + part

            @pl.when(step > 0)
            def _():
                out_copy(slot, part, (step - 1) * per_group + b).wait()

        for n in range(0, channels, DEPTH):
            at = slice(n, min(n + DEPTH, channels))
            rhs = jnp.where(which == b, held[:, at], 0.0).astype(BF16)
            for part in range(2):
                product = jnp.dot(
                    lhs[part * width:(part + 1) * width, :], rhs, preferred_element_type=F32
                )
                if not exact:
                    product = product * scale
                made[2 * b + part, :, at] = product.astype(BF16)
        for part in range(2):
            out_copy(2 * b + part, part, step * per_group + b).start()

    @pl.when(step == pl.num_programs(0) - 1)
    def _():
        for b in range(per_group):
            for part in range(2):
                out_copy(2 * b + part, part, step * per_group + b).wait()


def stacks_of(col_blocks, row_blocks, bins, windows):
    devices = len(row_blocks)
    halves, _, span = row_blocks[0].shape
    chips, _, width = col_blocks[0].shape
    per_group = ROW_TILE // (2 * windows)
    scale = 1.0 / math.sqrt(windows * devices)
    channels = halves * span
    return pl.pallas_call(
        functools.partial(stack_kernel, windows, scale, devices),
        out_shape=jax.ShapeDtypeStruct((2, bins, width, channels), BF16),
        grid=(bins // per_group,),
        in_specs=[pl.BlockSpec((chips, ROW_TILE, width), lambda i: (0, i, 0))] * 2
        + [pl.BlockSpec((halves, ROW_TILE, span), lambda i: (0, i, 0))] * devices,
        out_specs=pl.BlockSpec(memory_space=pltpu.HBM),
        scratch_shapes=[
            pltpu.VMEM((2 * width, devices * ROW_TILE), BF16),
            pltpu.VMEM((devices * ROW_TILE, channels), F32),
            pltpu.VMEM((2 * per_group, width, channels), BF16),
            pltpu.SemaphoreType.DMA((2 * per_group,)),
        ],
        compiler_params=pltpu.CompilerParams(
            dimension_semantics=("arbitrary",), vmem_limit_bytes=24 * 2**20
        ),
        cost_estimate=pl.CostEstimate(
            flops=2 * 2 * bins * width * channels * devices * ROW_TILE,
            bytes_accessed=2 * bins * width * channels * 2,
            transcendentals=0,
        ),
        name="stack_products",
    )(*col_blocks, *row_blocks)


def pick_kernel(count, waits, *refs):
    white_ref, chan_refs, out_refs, held = refs[0], refs[1 + waits:-1 - count], refs[-1 - count:-1], refs[-1]
    tm, mine = lax.axis_index("tm"), lax.axis_index("chan")
    halves = white_ref.shape[0]
    for away, ref in enumerate((white_ref, *chan_refs)):
        held[jnp.bitwise_xor(mine, away)] = ref[...]
    for away, out_ref in enumerate(out_refs):
        out_ref[...] = held[jnp.bitwise_xor(tm // halves, away)]


def picked(row_blocks, chan_blocks, count):
    block = row_blocks[0]
    whole = pl.BlockSpec(memory_space=pltpu.VMEM)
    waits = len(row_blocks) - 1
    return pl.pallas_call(
        functools.partial(pick_kernel, count, waits),
        out_shape=[jax.ShapeDtypeStruct(block.shape, block.dtype)] * count,
        in_specs=[whole] + [pl.BlockSpec(memory_space=pl.ANY)] * waits + [whole] * len(chan_blocks),
        out_specs=[whole] * count,
        scratch_shapes=[pltpu.VMEM((1 + len(chan_blocks), *block.shape), block.dtype)],
        compiler_params=pltpu.CompilerParams(vmem_limit_bytes=16 * 2**20),
        name="pick_blocks",
    )(*row_blocks, *chan_blocks)


def part_kernel(count, *refs):
    blocks, (mine_ref, other_ref) = refs[:count], refs[-2:]
    halves = blocks[0].shape[0]
    core = lax.axis_index("tm") % halves
    for i, block in enumerate(blocks):
        mine_ref[i] = block[core]
        other_ref[i] = block[halves - 1 - core]


def parted(blocks, others):
    whole = pl.BlockSpec(memory_space=pltpu.VMEM)
    shape = jax.ShapeDtypeStruct((len(blocks), *blocks[0].shape[1:]), blocks[0].dtype)
    return pl.pallas_call(
        functools.partial(part_kernel, len(blocks)),
        out_shape=[shape] * 2,
        in_specs=[whole] * len(blocks) + [pl.BlockSpec(memory_space=pl.ANY)] * len(others),
        out_specs=[whole] * 2,
        compiler_params=pltpu.CompilerParams(vmem_limit_bytes=8 * 2**20),
        name="part_blocks",
    )(*blocks, *others)


def moved(block, axis, far):
    count = lax.axis_size(axis)
    return lax.ppermute(block, axis, [(i + far, i) for i in range(count) if 0 <= i + far < count])


def chan_blocks_of(block):
    count = lax.axis_size("chan")
    blocks = {0: block}
    for away in range(1, count):
        near = away & -away
        blocks[away] = from_partner(blocks[away ^ near], "chan", near)
    return [blocks[away] for away in range(1, count)]


def from_partner(block, axis, away):
    return lax.ppermute(block, axis, [(i, i ^ away) for i in range(lax.axis_size(axis))])


def shards(recording, offsets, band_bins, dead_flags):
    channels, block_len = recording.shape
    windows = block_len // (L // 2)
    bins = band_bins.shape[0]
    chan_count, tm_count = lax.axis_size("chan"), lax.axis_size("tm")
    halves = tm_count // chan_count
    rim = L // 2 + L // 4
    cut = min(pl.cdiv(rim, STEP) * STEP, block_len)
    rim = L // 2 + L // 4
    cut = pl.cdiv(rim, STEP) * STEP
    own, back, state = spectra_of(recording, offsets, band_bins, dead_flags, windows, cut)
    more = moved(back, "tm", 1)
    rest = rest_of(recording, state, bins, windows, cut)
    white = whiten(own, rest, more, bins, windows, halves)
    row_blocks = [white] + [from_partner(white, "tm", away) for away in range(2, tm_count, 2)]
    chan_blocks = chan_blocks_of(white)
    chips = len(row_blocks)
    chip_blocks = list(picked(row_blocks, chan_blocks, chips))
    for away in range(1, chips):
        chip_blocks[away] = from_partner(chip_blocks[away], "tm", 2 * away)
    rows_there = [from_partner(block, "tm", 1) for block in row_blocks]
    mine, other = parted(chip_blocks, rows_there)
    col_blocks = [mine, from_partner(other, "tm", 1)]
    all_rows = []
    for here, there in zip(row_blocks, rows_there):
        all_rows += [here, there]
    return stacks_of(col_blocks, all_rows, bins, windows)


def solution(mesh):
    placed = (P("chan", "tm"), P(), P(), P("chan"))
    return jax.shard_map(
        shards, mesh=mesh, in_specs=placed, out_specs=P(None, None, "tm", "chan"), check_vma=False
    )
```
